128 devices in a mesh: depth: 8 (over y_lo, z), strip: 16 (over x, y_hi, core).
Axes of the slice: x: 4, y: 4 (y_hi: 2, y_lo: 2; y = y_hi * 2 + y_lo), z: 4, core: 2. Of those that a mesh axis runs over, the one named last changes fastest.
Arguments:
- conductivity: float32 [128, 128, 1536], P('depth', 'strip'), may hold values from 0.3 to 3
- forward_states: float32 [5, 128, 128, 1536], P(None, 'depth', 'strip'), may hold values from -6 to 6
- sensor_cell: int32 [524288], P(('depth', 'strip')), may hold values from 0 to 196607
- sensor_window: int32 [524288], P(('depth', 'strip')), may hold values from 0 to 4
- sensor_misfit: float32 [524288], P(('depth', 'strip')), may hold values from -6 to 6
- prior_conductance: float32 [3, 32, 384, 128], P(None, 'strip', 'depth'), may hold values from 0.2 to 8, as said below
Outputs:
- coarse_grad: float32 [32, 384, 128], P('strip', 'depth')
- prior_step: float32 [32, 384, 128], P('strip', 'depth')
The draws below stay inside these ranges and needn't reach their ends.
Inputs may be any that keep to these rules, and one draw needn't show every extreme that they name: sensor_cell indexes a cell of the block of 16 x 8 x 1536 cells of the device that holds the record. `prior_conductance`: positive conductances.
All inputs are finite; a program needn't handle non-finite values.
Results may differ from the reference program's by a relative error of at most 0.00002.
Values sent between devices are 32-bit elements; how exact they have to be, the bound alone decides.
No kernel may reach another device: no remote copies, remote signals or barrier semaphores. Data moves between devices by JAX's collectives and lax.ppermute only.
A program may use at most 128 MiB of HBM per device.

```python
import math
import jax
import jax.numpy as jnp

CZ = 16
CX = 8
NY = 1536
SENS_DEV = 4096
STEPS = 5
SWEEPS = 2
CHEB = 6
NZ = 128
NX = 128
PX = 32
PY = 384
SENSORS = 524288
N_STRIP = 16


def draw_prior_conductance(key, part):
    shape = (3, PX, PY, NZ)
    across = jnp.arange(PX, dtype=jnp.float32).reshape(1, PX, 1, 1) / max(PX - 1, 1)
    along = jnp.arange(PY, dtype=jnp.float32).reshape(1, 1, PY, 1) / max(PY - 1, 1)
    base = jnp.exp(jax.random.uniform(key, shape, jnp.float32, math.log(0.2), math.log(2.0)))
    ramp = 1.0 + across + along
    return (base * ramp).astype(jnp.float32)


def plant(entries, own_key, smallest, top_value):
    longest = entries.shape.index(max(entries.shape))
    spots = []
    for shift in (0, 1):
        where = [jax.random.randint(jax.random.fold_in(own_key, axis), (), 0, length) for axis, length in enumerate(entries.shape)]
        where[longest] = (where[longest] + shift) % entries.shape[longest]
        spots.append(tuple(where))
    return entries.at[spots[0]].set(smallest).at[spots[1]].set(top_value)


def shard_levels(key, dims, pieces, smallest, top_value):
    def one(dim, blocks):
        heights = jax.random.uniform(jax.random.fold_in(jax.random.fold_in(key, 6), dim), (blocks,), jnp.float32, smallest / len(pieces), top_value / len(pieces))
        return jnp.repeat(jnp.exp(heights), dims[dim] // blocks).reshape((-1,) + (1,) * (len(dims) - dim - 1))

    factor_of = one(*pieces[0])
    for cut in pieces[1:]:
        factor_of = factor_of * one(*cut)
    return factor_of


def noise(rng, extent, width, most, split=(), kind=jnp.bfloat16):
    values = jax.random.normal(rng, extent, jnp.float32) * width
    if len(split) > 0:
        values = shard_levels(rng, extent, split, -0.22, 0.18) * values
    return jnp.clip(values, min=-most, max=most).astype(kind)


def setup_inputs(seed: int = 0) -> dict:
    arg_keys = jax.random.split(jax.random.key(seed), 7)
    return {
        "conductivity": jnp.clip(jnp.exp(math.log(3.0) - 2.3025851 * jax.random.uniform(arg_keys[0], (NZ, NX, NY), jnp.float32) ** shard_levels(arg_keys[0], (NZ, NX, NY), ((0, 8), (1, 16)), -0.2, 0.2)), 0.3, 3.0),
        "forward_states": noise(arg_keys[1], (STEPS, NZ, NX, NY), 1.0, 6.0, ((1, 8), (2, 16)), jnp.float32),
        "sensor_cell": plant(jax.random.randint(arg_keys[2], (SENSORS,), 0, CZ * CX * NY), jax.random.fold_in(arg_keys[2], 1), 0, (CZ * CX * NY) - 1).astype(jnp.int32),
        "sensor_window": plant(jax.random.randint(arg_keys[3], (SENSORS,), 0, STEPS), jax.random.fold_in(arg_keys[3], 1), 0, STEPS - 1).astype(jnp.int32),
        "sensor_misfit": noise(arg_keys[4], (SENSORS,), 1.0, 6.0, ((0, 128),), jnp.float32),
        "prior_conductance": draw_prior_conductance(jax.random.fold_in(arg_keys[6], 71), 0),
    }


time_step = 1.0
matern_shift = 0.5


def neighbours(padded):
    return (padded[2:, 1:-1, 1:-1], padded[:-2, 1:-1, 1:-1], padded[1:-1, 2:, 1:-1], padded[1:-1, :-2, 1:-1], padded[1:-1, 1:-1, 2:], padded[1:-1, 1:-1, :-2])


def relax(iterate, forcing, conductivity):
    cond_around = neighbours(jnp.pad(conductivity, 1))
    value_around = neighbours(jnp.pad(iterate, 1))
    face_total = jnp.zeros_like(iterate)
    spread = jnp.zeros_like(iterate)
    for cond_other, value_other in zip(cond_around, value_around):
        face = 0.5 * (conductivity + cond_other)
        face_total = face_total + face
        spread = spread + face * value_other
    return (forcing + time_step * spread) / (1.0 + time_step * face_total)


def sensitivity(adjoint, forward, conductivity):
    adjoint_around = neighbours(jnp.pad(adjoint, 1))
    forward_around = neighbours(jnp.pad(forward, 1))
    product = jnp.zeros_like(adjoint)
    for adjoint_other, forward_other in zip(adjoint_around, forward_around):
        product = product + (adjoint - adjoint_other) * (forward - forward_other)
    return -0.5 * time_step * conductivity * product


def prior_faces(weights):
    face_list = []
    for axis_index in range(3):
        beside_all = neighbours(jnp.pad(weights[axis_index], 1))
        for side_index in range(2):
            face_list.append(0.5 * (weights[axis_index] + beside_all[2 * axis_index + side_index]))
    return face_list


def prior_apply(vector, face_list):
    beside_all = neighbours(jnp.pad(vector, 1))
    result = matern_shift * vector
    for slot_index in range(6):
        result = result + face_list[slot_index] * (vector - beside_all[slot_index])
    return result


def reference(conductivity, forward_states, sensor_cell, sensor_window, sensor_misfit, prior_conductance):
    owner_index = jnp.arange(SENSORS, dtype=jnp.int32) // SENS_DEV
    layer_block = owner_index // N_STRIP
    column_block = owner_index % N_STRIP
    local_layer = sensor_cell // (CX * NY)
    local_column = (sensor_cell // NY) % CX
    lateral_pos = sensor_cell % NY
    flat_cell = ((layer_block * CZ + local_layer) * NX + column_block * CX + local_column) * NY + lateral_pos
    carried = jnp.zeros((NZ, NX, NY), jnp.float32)
    gradient = jnp.zeros((NZ, NX, NY), jnp.float32)
    for step_index in reversed(range(STEPS)):
        source = jnp.where(sensor_window == step_index, sensor_misfit, jnp.zeros_like(sensor_misfit))
        injected = jnp.zeros((NZ * NX * NY,), jnp.float32).at[flat_cell].add(source).reshape(NZ, NX, NY)
        forcing = carried + injected
        adjoint = forcing
        for sweep_index in range(SWEEPS):
            adjoint = relax(adjoint, forcing, conductivity)
        gradient = gradient + sensitivity(adjoint, forward_states[step_index], conductivity)
        carried = adjoint
    coarse_grad = jnp.transpose(gradient.reshape(NZ, PX, 4, PY, 4).sum(axis=(2, 4)), (1, 2, 0))
    face_list = prior_faces(prior_conductance)
    face_total = jnp.zeros_like(coarse_grad)
    for face in face_list:
        face_total = face_total + face
    upper_bound = jnp.max(matern_shift + 2.0 * face_total)
    lower_bound = matern_shift
    centre_value = 0.5 * (upper_bound + lower_bound)
    half_width = 0.5 * (upper_bound - lower_bound)
    sigma_ratio = centre_value / half_width
    recur_now = 1.0 / sigma_ratio
    solution = jnp.zeros_like(coarse_grad)
    residual = coarse_grad
    direction = residual / centre_value
    for cheb_index in range(CHEB):
        solution = solution + direction
        if cheb_index + 1 < CHEB:
            residual = residual - prior_apply(direction, face_list)
            recur_next = 1.0 / (2.0 * sigma_ratio - recur_now)
            direction = recur_next * recur_now * direction + (2.0 * recur_next / half_width) * residual
            recur_now = recur_next
    return coarse_grad, solution
```

```python
import functools

import jax
import jax.numpy as jnp
from jax import lax
from jax.experimental import pallas as pl
from jax.experimental.pallas import tpu as pltpu
from jax.sharding import PartitionSpec as P

F32 = jnp.float32
STEPS = 5
CHEB = 6
CZ, CX, NY = 16, 8, 1536
TILES = NY // 128
XR = TILES * CZ
WIN = 64
SHIFT = 0.5
EXACT = lax.Precision.HIGHEST

VM = pl.BlockSpec(memory_space=pltpu.VMEM)
SM = pl.BlockSpec(memory_space=pltpu.SMEM)


def shape(*dims):
    return jax.ShapeDtypeStruct(dims, F32)


def call(body, outs, ins, scratch=(), limit=48, flops=10**7, traffic=5 * 10**6):
    return pl.pallas_call(
        body,
        out_shape=outs,
        in_specs=ins,
        out_specs=jax.tree.map(lambda _: VM, outs),
        scratch_shapes=list(scratch),
        compiler_params=pltpu.CompilerParams(vmem_limit_bytes=limit * 2**20),
        cost_estimate=pl.CostEstimate(flops=flops, bytes_accessed=traffic, transcendentals=0),
    )


def pairs_a(n):
    return [(i, i ^ 1) for i in range(n)]


def pairs_b(n):
    return [(i, (((i + 1) ^ 1) - 1) % n) for i in range(n)]


def swap(send, axis):
    n = lax.axis_size(axis)
    return lax.ppermute(send[0], axis, pairs_a(n)), lax.ppermute(send[1], axis, pairs_b(n))


def to_sides(info, k, first, second):
    odd = info[k] == 1
    below = jnp.where(info[2 + 2 * k] == 1, jnp.where(odd, first, second), 0.0)
    above = jnp.where(info[3 + 2 * k] == 1, jnp.where(odd, second, first), 0.0)
    return below, above


def from_sides(info, k, below, above):
    odd = info[k] == 1
    return jnp.where(odd, below, above), jnp.where(odd, above, below)


def iota(axis, width=NY):
    return lax.broadcasted_iota(jnp.int32, (CX, width), axis)


def lane_up(v):
    return pltpu.roll(v, NY - 1, 1)


def lane_down(v):
    return pltpu.roll(v, 1, 1)


def sub_up(v):
    return pltpu.roll(v, CX - 1, 0)


def sub_down(v):
    return pltpu.roll(v, 1, 0)


def slab_row(ref, z):
    return jnp.concatenate([ref[pl.ds(t * CZ + z, 1), :] for t in range(TILES)], axis=1)


def put_rows(info, refs, base, z, plane):
    first, second = from_sides(info, 0, plane[0:1], plane[CX - 1 : CX])
    for t in range(TILES):
        refs[0][pl.ds(base + t * CZ + z, 1), :] = first[:, t * 128 : (t + 1) * 128]
        refs[1][pl.ds(base + t * CZ + z, 1), :] = second[:, t * 128 : (t + 1) * 128]


def put_layers(info, refs, slot, low, high):
    first, second = from_sides(info, 1, low, high)
    refs[0][slot] = first
    refs[1][slot] = second


def load_sides(info, rx, base, lo_ref, hi_ref):
    lo, hi = to_sides(info, 0, rx[0][base : base + XR, :], rx[1][base : base + XR, :])
    lo_ref[...] = lo
    hi_ref[...] = hi


def load_ext(info, ref, rz, slot, ext):
    ext[1 : CZ + 1] = ref[...]
    lo, hi = to_sides(info, 1, rz[0][slot], rz[1][slot])
    ext[0] = lo
    ext[CZ + 1] = hi


EXT = pltpu.VMEM((CZ + 2, CX, NY), F32)
SIDE = pltpu.VMEM((XR, 128), F32)
FULL = (CZ, CX, NY)


def each_layer(body):
    def step(z, carry):
        body(z)
        return carry

    lax.fori_loop(0, CZ, step, 0)


def pack_forward(info, fwd, xa, xb, za, zb):
    for n in range(STEPS):
        put_layers(info, (za, zb), n, fwd[n, 0], fwd[n, CZ - 1])
        each_layer(lambda z: put_rows(info, (xa, xb), n * XR, z, fwd[n, z]))


BUFS = 4


def scatter(info, code, misfit, cond, out, xa, xb, za, zb, *parts):
    for part in parts:
        part[...] = jnp.zeros_like(part)
    place = iota(0, 128) * 128 + iota(1, 128)
    count = code.shape[0] // BUFS

    def step(i, carry):
        for k, part in enumerate(parts):
            c = code[i + k * count]
            layer = lax.shift_right_logical(c, 14)
            tile = pl.multiple_of(lax.shift_right_logical(c, 3) & (15 * 128), 128)
            add = jnp.where(place == (c & 1023), misfit[i + k * count], 0.0)
            part[layer, :, pl.ds(tile, 128)] = part[layer, :, pl.ds(tile, 128)] + add
        return carry

    lax.fori_loop(0, count, step, 0, unroll=4)

    def join(k, carry):
        total = parts[0][k]
        for part in parts[1:]:
            total = total + part[k]
        out[k // CZ, lax.rem(k, CZ)] = total
        return carry

    lax.fori_loop(0, STEPS * CZ, join, 0)
    last = STEPS - 1
    put_layers(info, (za, zb), 0, out[last, 0], out[last, CZ - 1])
    put_layers(info, (za, zb), 1, cond[0], cond[CZ - 1])

    def rows(z):
        put_rows(info, (xa, xb), 0, z, out[last, z])
        put_rows(info, (xa, xb), XR, z, cond[z])

    each_layer(rows)


def faces(info, cond, rxa, rxb, rza, rzb, fz, fy, fx, fxb, inv, ext, lo, hi):
    load_ext(info, cond, (rza, rzb), 1, ext)
    load_sides(info, (rxa, rxb), XR, lo, hi)
    sub, lane = iota(0), iota(1)

    def layer(z):
        c = ext[z + 1]
        z_lo = 0.5 * (c + ext[z])
        z_hi = 0.5 * (c + ext[z + 2])
        y_hi = 0.5 * (c + jnp.where(lane == NY - 1, 0.0, lane_up(c)))
        y_lo = jnp.where(lane == 0, 0.5 * c, lane_down(y_hi))
        x_hi = 0.5 * (c + jnp.where(sub == CX - 1, slab_row(hi, z), sub_up(c)))
        x_lo = jnp.where(sub == 0, 0.5 * (c + slab_row(lo, z)), sub_down(x_hi))
        fz[z] = z_lo
        fz[z + 1] = z_hi
        fy[z] = jnp.where(lane == NY - 1, 0.0, y_hi)
        fx[z] = jnp.where(sub == CX - 1, 0.0, x_hi)
        fxb[z] = jnp.where(sub == CX - 1, x_hi, jnp.where(sub == 0, x_lo, 0.0))
        inv[z] = 1.0 / (1.0 + (((((z_hi + z_lo) + x_hi) + x_lo) + y_hi) + y_lo))

    each_layer(layer)


def sweep(info, right, fz, fy, fx, fxb, inv, ext, lo, hi, sub, z):
    v = ext[z + 1]
    y_face = fy[z]
    x_face = fx[z]
    spread = fz[z + 1] * ext[z + 2] + fz[z] * ext[z]
    spread = spread + x_face * sub_up(v) + sub_down(x_face * v)
    spread = spread + fxb[z] * jnp.where(sub == CX - 1, slab_row(hi, z), slab_row(lo, z))
    spread = spread + y_face * lane_up(v) + lane_down(y_face * v)
    return (right[z] + spread) * inv[z]


def first_sweep(
    base, slot, info, forcing, fz, fy, fx, fxb, inv, rxa, rxb, rza, rzb, out, xa, xb, za, zb, ext, lo, hi
):
    load_ext(info, forcing, (rza, rzb), slot, ext)
    load_sides(info, (rxa, rxb), base, lo, hi)
    sub = iota(0)

    def layer(z):
        new = sweep(info, forcing, fz, fy, fx, fxb, inv, ext, lo, hi, sub, z)
        out[z] = new
        put_rows(info, (xa, xb), 0, z, new)

    each_layer(layer)
    put_layers(info, (za, zb), 0, out[0], out[CZ - 1])


def second_sweep(
    more, info, v, forcing, source, fz, fy, fx, fxb, inv, rxa, rxb, rza, rzb, out, after, xa, xb, za, zb, ext, lo, hi
):
    load_ext(info, v, (rza, rzb), 0, ext)
    load_sides(info, (rxa, rxb), 0, lo, hi)
    sub = iota(0)

    def layer(z):
        new = sweep(info, forcing, fz, fy, fx, fxb, inv, ext, lo, hi, sub, z)
        out[z] = new
        put_rows(info, (xa, xb), 0, z, new)
        if more:
            fresh = new + source[0, z]
            after[z] = fresh
            put_rows(info, (xa, xb), XR, z, fresh)

    each_layer(layer)
    put_layers(info, (za, zb), 0, out[0], out[CZ - 1])
    if more:
        put_layers(info, (za, zb), 1, after[0], after[CZ - 1])


def gradient(
    n, first, info, a_ref, f_ref, acc, rxa, rxb, rza, rzb, fxa, fxb, fza, fzb, out, a_ext, f_ext, a_lo, a_hi, f_lo, f_hi
):
    load_ext(info, a_ref, (rza, rzb), 0, a_ext)
    load_sides(info, (rxa, rxb), 0, a_lo, a_hi)
    f_ext[1 : CZ + 1] = f_ref[0]
    below, above = to_sides(info, 1, fza[n], fzb[n])
    f_ext[0] = below
    f_ext[CZ + 1] = above
    load_sides(info, (fxa, fxb), n * XR, f_lo, f_hi)
    sub, lane = iota(0), iota(1)

    def layer(z):
        a, f = a_ext[z + 1], f_ext[z + 1]
        total = (a - a_ext[z + 2]) * (f - f_ext[z + 2]) + (a - a_ext[z]) * (f - f_ext[z])
        x_hi = (a - jnp.where(sub == CX - 1, slab_row(a_hi, z), sub_up(a))) * (
            f - jnp.where(sub == CX - 1, slab_row(f_hi, z), sub_up(f))
        )
        x_lo = jnp.where(sub == 0, (a - slab_row(a_lo, z)) * (f - slab_row(f_lo, z)), sub_down(x_hi))
        y_hi = (a - jnp.where(lane == NY - 1, 0.0, lane_up(a))) * (f - jnp.where(lane == NY - 1, 0.0, lane_up(f)))
        y_lo = jnp.where(lane == 0, a * f, lane_down(y_hi))
        total = total + (x_hi + x_lo) + (y_hi + y_lo)
        out[z] = total if first else acc[z] + total

    each_layer(layer)


def coarsen(acc, cond, out, rows, tall):
    def layer(z):
        g = -0.5 * cond[z] * acc[z]
        g = g + sub_up(g)
        g = g + pltpu.roll(g, CX - 2, 0)
        rows[pl.ds(z, 1), :] = g[0:1]
        rows[pl.ds(CZ + z, 1), :] = g[4:5]

    each_layer(layer)
    group = lax.broadcasted_iota(jnp.int32, (128, 512), 1) // 4
    pick = jnp.where(group == lax.broadcasted_iota(jnp.int32, (128, 512), 0), 1.0, 0.0)
    tall[...] = jnp.zeros_like(tall)
    for k in range(3):
        tall[8 + 128 * k : 8 + 128 * (k + 1), :] = lax.dot_general(
            pick,
            rows[:, 512 * k : 512 * (k + 1)],
            (((1,), (1,)), ((), ())),
            precision=EXACT,
            preferred_element_type=F32,
        )
    for d in range(out.shape[0]):
        out[d] = tall[48 * d : 48 * d + WIN, :]


def assemble(pieces, window, coarse):
    k = lax.broadcasted_iota(jnp.int32, (2 * CZ, 128), 0)
    z = lax.broadcasted_iota(jnp.int32, (2 * CZ, 128), 1)
    for p in range(2):
        total = jnp.zeros((WIN, 128), F32)
        for d in range(pieces.shape[0]):
            own = (z >= CZ * d) & (z < CZ * (d + 1)) & (k - CZ * p == z - CZ * d)
            total = total + jnp.dot(
                pieces[d], jnp.where(own, 1.0, 0.0), precision=EXACT, preferred_element_type=F32
            )
        window[p] = total
        coarse[p] = total[8:56]


SPAN = 12


def prior_faces(first_column, first_row, w, fx, fy, fz, diag, peak):
    row = lax.broadcasted_iota(jnp.int32, (WIN, 128), 0)
    lane = lax.broadcasted_iota(jnp.int32, (WIN, 128), 1)
    y_in = (row + first_row >= 0) & (row + first_row < 384)
    y_link = y_in & (row + first_row + 1 >= 0) & (row + first_row + 1 < 384) & (row < WIN - 1)

    def x_in(j):
        return (first_column + j >= 0) & (first_column + j < 32)

    def wx(j):
        if j < 0 or j >= SPAN:
            return jnp.zeros((WIN, 128), F32)
        return jnp.where(x_in(j) & y_in, w[0, j], 0.0)

    best = None
    for j in range(SPAN):
        inside = x_in(j) & y_in
        here = wx(j)
        x_hi = 0.5 * (here + wx(j + 1))
        x_lo = 0.5 * (here + wx(j - 1))
        v = jnp.where(inside, w[1, j], 0.0)
        y_hi = 0.5 * (v + jnp.where(row == WIN - 1, 0.0, pltpu.roll(v, WIN - 1, 0)))
        y_lo = jnp.where(row == 0, 0.5 * v, pltpu.roll(y_hi, 1, 0))
        v = jnp.where(inside, w[2, j], 0.0)
        z_hi = 0.5 * (v + jnp.where(lane == 127, 0.0, pltpu.roll(v, 127, 1)))
        z_lo = jnp.where(lane == 0, 0.5 * v, pltpu.roll(z_hi, 1, 1))
        total = ((((x_hi + x_lo) + y_hi) + y_lo) + z_hi) + z_lo
        diag[j] = SHIFT + total
        fx[j] = jnp.where(inside & x_in(j + 1), x_hi, 0.0) if j + 1 < SPAN else jnp.zeros_like(x_hi)
        fy[j] = jnp.where(x_in(j) & y_link, y_hi, 0.0)
        fz[j] = jnp.where(inside & (lane < 127), z_hi, 0.0)
        if j in (5, 6):
            bound = jnp.max((SHIFT + 2.0 * total)[8:56].reshape(6, 8, 128), axis=0)
            best = bound if best is None else jnp.maximum(best, bound)
    peak[...] = best


def prior_setup(place, w, fx, fy, fz, diag, peak):
    prior_faces(place[0], place[1], w, fx, fy, fz, diag, peak)


def chebyshev(place, upper, g, fx, fy, fz, diag, out, r, d):
    row = lax.broadcasted_iota(jnp.int32, (WIN, 128), 0)
    y_in = (row + place[1] >= 0) & (row + place[1] < 384)
    top = upper[0:1, 0:1]
    centre = 0.5 * (top + SHIFT)
    half = 0.5 * (top - SHIFT)
    sigma = centre / half
    rho = 1.0 / sigma
    for j in range(SPAN):
        inside = (place[0] + j >= 0) & (place[0] + j < 32) & y_in
        start = jnp.where(inside, g[j], 0.0)
        r[j] = start
        d[0, j] = start / centre
    for p in range(2):
        out[p] = d[0, 5 + p, 8:56]
    for it in range(CHEB - 1):
        now, later = it % 2, (it + 1) % 2
        rho_new = 1.0 / (2.0 * sigma - rho)
        scale_d = rho_new * rho
        scale_r = 2.0 * rho_new / half
        for j in range(it + 1, SPAN - 1 - it):
            v = d[now, j]
            y_face, z_face = fy[j], fz[j]
            pull = fx[j] * d[now, j + 1] + fx[j - 1] * d[now, j - 1]
            pull = pull + y_face * pltpu.roll(v, WIN - 1, 0) + pltpu.roll(y_face * v, 1, 0)
            pull = pull + z_face * pltpu.roll(v, 127, 1) + pltpu.roll(z_face * v, 1, 1)
            left = r[j] - (diag[j] * v - pull)
            r[j] = left
            d[later, j] = scale_d * v + scale_r * left
        for p in range(2):
            out[p] = out[p] + d[later, 5 + p, 8:56]
        rho = rho_new


def on_device(
    conductivity, forward_states, sensor_cell, sensor_window, sensor_misfit, prior_conductance
):
    z_at, x_at = lax.axis_index("depth"), lax.axis_index("strip")
    z_n, x_n = lax.axis_size("depth"), lax.axis_size("strip")
    info = jnp.stack(
        [
            x_at % 2,
            z_at % 2,
            (x_at > 0).astype(jnp.int32),
            (x_at < x_n - 1).astype(jnp.int32),
            (z_at > 0).astype(jnp.int32),
            (z_at < z_n - 1).astype(jnp.int32),
        ]
    ).astype(jnp.int32)
    place = jnp.stack([2 * x_at - 5, 48 * z_at - 8]).astype(jnp.int32)
    x_odd, z_odd = x_at % 2 == 1, z_at % 2 == 1

    xs, zs = shape(STEPS * XR, 128), shape(STEPS, CX, NY)
    fxa, fxb, fza, fzb = call(pack_forward, (xs, xs, zs, zs), [SM, VM])(info, forward_states)
    prior_flat = prior_conductance.reshape(288, 128)
    fxa, fxb = swap((jnp.concatenate([fxa, prior_flat]), jnp.concatenate([fxb, prior_flat])), "strip")
    forward_x = (fxa, fxb)
    forward_z = swap((fza, fzb), "depth")

    layer = sensor_window * CZ + sensor_cell // (CX * NY)
    lateral = sensor_cell % NY
    code = layer * 16384 + (lateral // 128) * 1024 + (sensor_cell // NY) % CX * 128 + lateral % 128
    xs, zs = shape(2 * XR, 128), shape(2, CX, NY)
    sources, xa, xb, za, zb = call(
        scatter,
        (shape(STEPS, *FULL), xs, xs, zs, zs),
        [SM, SM, SM, VM],
        [pltpu.VMEM((STEPS * CZ, CX, NY), F32)] * BUFS,
        limit=56,
        flops=4 * 10**7,
    )(info, code, sensor_misfit, conductivity)
    rx, rz = swap((xa, xb), "strip"), swap((za, zb), "depth")

    full = shape(*FULL)
    table = call(
        faces, (shape(CZ + 1, CX, NY), full, full, full, full), [SM] + [VM] * 5, [EXT, SIDE, SIDE]
    )(info, conductivity, *rx, *rz)

    above = jnp.where(x_odd, fxb[STEPS * XR :], fxa[STEPS * XR :]).reshape(3, 2, 48, 128)
    below = jnp.where(x_odd, fxa[STEPS * XR :], fxb[STEPS * XR :]).reshape(3, 2, 48, 128)
    ring = [(i, (i + 2) % x_n) for i in range(x_n)]
    back = [(j, i) for i, j in ring]
    below2 = lax.ppermute(
        jnp.concatenate([below[:, 1:], prior_conductance], axis=1).reshape(432, 128), "strip", ring
    ).reshape(3, 3, 48, 128)
    above2 = lax.ppermute(
        jnp.concatenate([prior_conductance, above[:, :1]], axis=1).reshape(432, 128), "strip", back
    ).reshape(3, 3, 48, 128)
    weights = jnp.concatenate([below2, below, prior_conductance, above, above2], axis=1)
    low, high = weights[:, :, :8].reshape(288, 128), weights[:, :, 40:].reshape(288, 128)
    wza, wzb = swap((jnp.where(z_odd, low, high), jnp.where(z_odd, high, low)), "depth")
    under = jnp.where(z_odd, wza, wzb).reshape(3, SPAN, 8, 128)
    over = jnp.where(z_odd, wzb, wza).reshape(3, SPAN, 8, 128)
    weights = jnp.concatenate([under, weights, over], axis=2)
    span = shape(SPAN, WIN, 128)
    *prior, peak = call(prior_setup, (span, span, span, span, shape(8, 128)), [SM, VM])(place, weights)
    spread_peak = jnp.broadcast_to(jnp.max(peak), (z_n * x_n, 1, 128))
    peaks = lax.all_to_all(spread_peak, ("depth", "strip"), 0, 0)
    upper = jnp.broadcast_to(jnp.max(peaks), (8, 128))

    forcing = sources[STEPS - 1]
    base, slot = 0, 0
    acc = None
    for n in reversed(range(STEPS)):
        xs, zs = shape(XR, 128), shape(1, CX, NY)
        v, xa, xb, za, zb = call(
            functools.partial(first_sweep, base, slot),
            (full, xs, xs, zs, zs),
            [SM] + [VM] * 10,
            [EXT, SIDE, SIDE],
        )(info, forcing, *table, *rx, *rz)
        rx, rz = swap((xa, xb), "strip"), swap((za, zb), "depth")
        more = n > 0
        fields = 2 if more else 1
        xs, zs = shape(fields * XR, 128), shape(fields, CX, NY)
        before = max(n - 1, 0)
        adjoint, after, xa, xb, za, zb = call(
            functools.partial(second_sweep, more),
            (full, full if more else shape(8, 128), xs, xs, zs, zs),
            [SM] + [VM] * 12,
            [EXT, SIDE, SIDE],
        )(info, v, forcing, sources[before : before + 1], *table, *rx, *rz)
        rx, rz = swap((xa, xb), "strip"), swap((za, zb), "depth")
        first = acc is None
        acc = call(
            functools.partial(gradient, n, first),
            full,
            [SM] + [VM] * 11,
            [EXT, EXT, SIDE, SIDE, SIDE, SIDE],
        )(info, adjoint, forward_states[n : n + 1], adjoint if first else acc, *rx, *rz, *forward_x, *forward_z)
        forcing = after
        base, slot = XR, 1

    pieces = call(
        coarsen, shape(z_n, WIN, 2 * CZ), [VM, VM], [pltpu.VMEM((2 * CZ, NY), F32), pltpu.VMEM((400, 2 * CZ), F32)]
    )(acc, conductivity)
    pieces = lax.all_to_all(pieces, "depth", 0, 0)
    window, coarse_grad = call(assemble, (shape(2, WIN, 128), shape(2, 48, 128)), [VM])(pieces)
    flat = window.reshape(2 * WIN, 128)
    ga, gb = swap((flat, flat), "strip")
    above = jnp.where(x_odd, gb, ga)
    below = jnp.where(x_odd, ga, gb)
    below2 = lax.ppermute(jnp.concatenate([below[WIN:], flat]), "strip", ring)
    above2 = lax.ppermute(jnp.concatenate([flat, above[:WIN]]), "strip", back)
    g = jnp.concatenate([below2, below, flat, above, above2]).reshape(SPAN, WIN, 128)
    step = call(
        chebyshev,
        shape(2, 48, 128),
        [SM] + [VM] * 6,
        [pltpu.VMEM((SPAN, WIN, 128), F32), pltpu.VMEM((2, SPAN, WIN, 128), F32)],
    )(place, upper, g, *prior)
    return coarse_grad, step


def solution(mesh):
    placed = (
        P("depth", "strip", None),
        P(None, "depth", "strip", None),
        P(("depth", "strip")),
        P(("depth", "strip")),
        P(("depth", "strip")),
        P(None, "strip", "depth", None),
    )
    return jax.shard_map(
        on_device,
        mesh=mesh,
        in_specs=placed,
        out_specs=(P("strip", "depth", None), P("strip", "depth", None)),
        check_vma=False,
    )
```

```python
import functools

import jax
import jax.numpy as jnp
from jax import lax
from jax.experimental import pallas as pl
from jax.experimental.pallas import tpu as pltpu
from jax.sharding import PartitionSpec as P

F32 = jnp.float32
STEPS = 5
CHEB = 6
CZ, CX, NY = 16, 8, 1536
TILES = NY // 128
XR = TILES * CZ
WIN = 64
SHIFT = 0.5
EXACT = lax.Precision.HIGHEST

VM = pl.BlockSpec(memory_space=pltpu.VMEM)
SM = pl.BlockSpec(memory_space=pltpu.SMEM)


def shape(*dims):
    return jax.ShapeDtypeStruct(dims, F32)


def call(body, outs, ins, scratch=(), limit=6, flops=10**7, traffic=5 * 10**6):
    return pl.pallas_call(
        body,
        out_shape=outs,
        in_specs=ins,
        out_specs=jax.tree.map(lambda _: VM, outs),
        scratch_shapes=list(scratch),
        compiler_params=pltpu.CompilerParams(vmem_limit_bytes=limit * 2**20),
        cost_estimate=pl.CostEstimate(flops=flops, bytes_accessed=traffic, transcendentals=0),
    )


def pairs_a(n):
    return [(i, i ^ 1) for i in range(n)]


def pairs_b(n):
    return [(i, (((i + 1) ^ 1) - 1) % n) for i in range(n)]


def swap(send, axis):
    n = lax.axis_size(axis)
    return lax.ppermute(send[0], axis, pairs_a(n)), lax.ppermute(send[1], axis, pairs_b(n))


def to_sides(info, k, first, second):
    odd = info[k] == 1
    below = jnp.where(info[2 + 2 * k] == 1, jnp.where(odd, first, second), 0.0)
    above = jnp.where(info[3 + 2 * k] == 1, jnp.where(odd, second, first), 0.0)
    return below, above


def from_sides(info, k, below, above):
    odd = info[k] == 1
    return jnp.where(odd, below, above), jnp.where(odd, above, below)


def iota(axis, width=NY):
    return lax.broadcasted_iota(jnp.int32, (CX, width), axis)


def lane_up(v):
    return pltpu.roll(v, NY - 1, 1)


def lane_down(v):
    return pltpu.roll(v, 1, 1)


def sub_up(v):
    return pltpu.roll(v, CX - 1, 0)


def sub_down(v):
    return pltpu.roll(v, 1, 0)


def slab_row(ref, z):
    return jnp.concatenate([ref[pl.ds(t * CZ + z, 1), :] for t in range(TILES)], axis=1)


def put_rows(info, refs, base, z, plane):
    first, second = from_sides(info, 0, plane[0:1], plane[CX - 1 : CX])
    for t in range(TILES):
        refs[0][pl.ds(base + t * CZ + z, 1), :] = first[:, t * 128 : (t + 1) * 128]
        refs[1][pl.ds(base + t * CZ + z, 1), :] = second[:, t * 128 : (t + 1) * 128]


def put_layers(info, refs, slot, low, high):
    first, second = from_sides(info, 1, low, high)
    refs[0][slot] = first
    refs[1][slot] = second


def load_sides(info, rx, base, lo_ref, hi_ref):
    lo, hi = to_sides(info, 0, rx[0][base : base + XR, :], rx[1][base : base + XR, :])
    lo_ref[...] = lo
    hi_ref[...] = hi


def pass_peak(mine, rx, at, sends, to, out):
    best = mine[...]
    if at is not None:
        best = jnp.maximum(best, jnp.maximum(rx[0][at : at + 8, :], rx[1][at : at + 8, :]))
    out[...] = best
    if sends is not None:
        for send in sends:
            send[to : to + 8, :] = best


def load_ext(info, ref, rz, slot, ext):
    ext[1 : CZ + 1] = ref[...]
    lo, hi = to_sides(info, 1, rz[0][slot], rz[1][slot])
    ext[0] = lo
    ext[CZ + 1] = hi


EXT = pltpu.VMEM((CZ + 2, CX, NY), F32)
SIDE = pltpu.VMEM((XR, 128), F32)
FULL = (CZ, CX, NY)


def each_layer(body):
    def step(z, carry):
        body(z)
        return carry

    lax.fori_loop(0, CZ, step, 0)


def pack_forward(info, fwd, xa, xb, za, zb):
    for n in range(STEPS):
        put_layers(info, (za, zb), n, fwd[n, 0], fwd[n, CZ - 1])
        each_layer(lambda z: put_rows(info, (xa, xb), n * XR, z, fwd[n, z]))


BUFS = 4


def scatter(info, code, misfit, cond, out, xa, xb, za, zb, *parts):
    for part in parts:
        part[...] = jnp.zeros_like(part)
    place = iota(0, 128) * 128 + iota(1, 128)
    count = code.shape[0] // BUFS

    def step(i, carry):
        for k, part in enumerate(parts):
            c = code[i + k * count]
            layer = lax.shift_right_logical(c, 14)
            tile = pl.multiple_of(lax.shift_right_logical(c, 3) & (15 * 128), 128)
            add = jnp.where(place == (c & 1023), misfit[i + k * count], 0.0)
            part[layer, :, pl.ds(tile, 128)] = part[layer, :, pl.ds(tile, 128)] + add
        return carry

    lax.fori_loop(0, count, step, 0, unroll=4)

    def join(k, carry):
        total = parts[0][k]
        for part in parts[1:]:
            total = total + part[k]
        out[k // CZ, lax.rem(k, CZ)] = total
        return carry

    lax.fori_loop(0, STEPS * CZ, join, 0)
    last = STEPS - 1
    put_layers(info, (za, zb), 0, out[last, 0], out[last, CZ - 1])
    put_layers(info, (za, zb), 1, cond[0], cond[CZ - 1])

    def rows(z):
        put_rows(info, (xa, xb), 0, z, out[last, z])
        put_rows(info, (xa, xb), XR, z, cond[z])

    each_layer(rows)


def faces(info, cond, rxa, rxb, rza, rzb, fz, fy, fx, fxb, inv, ext, lo, hi):
    load_ext(info, cond, (rza, rzb), 1, ext)
    load_sides(info, (rxa, rxb), XR, lo, hi)
    sub, lane = iota(0), iota(1)

    def layer(z):
        c = ext[z + 1]
        z_lo = 0.5 * (c + ext[z])
        z_hi = 0.5 * (c + ext[z + 2])
        y_hi = 0.5 * (c + jnp.where(lane == NY - 1, 0.0, lane_up(c)))
        y_lo = jnp.where(lane == 0, 0.5 * c, lane_down(y_hi))
        x_hi = 0.5 * (c + jnp.where(sub == CX - 1, slab_row(hi, z), sub_up(c)))
        x_lo = jnp.where(sub == 0, 0.5 * (c + slab_row(lo, z)), sub_down(x_hi))
        fz[z] = z_lo
        fz[z + 1] = z_hi
        fy[z] = jnp.where(lane == NY - 1, 0.0, y_hi)
        fx[z] = jnp.where(sub == CX - 1, 0.0, x_hi)
        fxb[z] = jnp.where(sub == CX - 1, x_hi, jnp.where(sub == 0, x_lo, 0.0))
        inv[z] = 1.0 / (1.0 + (((((z_hi + z_lo) + x_hi) + x_lo) + y_hi) + y_lo))

    each_layer(layer)


def sweep(info, right, fz, fy, fx, fxb, inv, ext, lo, hi, sub, z):
    v = ext[z + 1]
    y_face = fy[z]
    x_face = fx[z]
    spread = fz[z + 1] * ext[z + 2] + fz[z] * ext[z]
    spread = spread + x_face * sub_up(v) + sub_down(x_face * v)
    spread = spread + fxb[z] * jnp.where(sub == CX - 1, slab_row(hi, z), slab_row(lo, z))
    spread = spread + y_face * lane_up(v) + lane_down(y_face * v)
    return (right[z] + spread) * inv[z]


def first_sweep(
    base, slot, at, info, peak, forcing, fz, fy, fx, fxb, inv, rxa, rxb, rza, rzb,
    out, known, xa, xb, za, zb, ext, lo, hi,
):
    pass_peak(peak, (rxa, rxb), at, (xa, xb), XR, known)
    load_ext(info, forcing, (rza, rzb), slot, ext)
    load_sides(info, (rxa, rxb), base, lo, hi)
    sub = iota(0)

    def layer(z):
        new = sweep(info, forcing, fz, fy, fx, fxb, inv, ext, lo, hi, sub, z)
        out[z] = new
        put_rows(info, (xa, xb), 0, z, new)

    each_layer(layer)
    put_layers(info, (za, zb), 0, out[0], out[CZ - 1])


def second_sweep(
    more, info, peak, v, forcing, source, fz, fy, fx, fxb, inv, rxa, rxb, rza, rzb,
    out, after, known, xa, xb, za, zb, ext, lo, hi,
):
    pass_peak(peak, (rxa, rxb), XR, (xa, xb), 2 * XR if more else XR, known)
    load_ext(info, v, (rza, rzb), 0, ext)
    load_sides(info, (rxa, rxb), 0, lo, hi)
    sub = iota(0)

    def layer(z):
        new = sweep(info, forcing, fz, fy, fx, fxb, inv, ext, lo, hi, sub, z)
        out[z] = new
        put_rows(info, (xa, xb), 0, z, new)
        if more:
            fresh = new + source[0, z]
            after[z] = fresh
            put_rows(info, (xa, xb), XR, z, fresh)

    each_layer(layer)
    put_layers(info, (za, zb), 0, out[0], out[CZ - 1])
    if more:
        put_layers(info, (za, zb), 1, after[0], after[CZ - 1])


def gradient(
    n, first, info, a_ref, f_ref, acc, rxa, rxb, rza, rzb, fxa, fxb, fza, fzb, out, a_ext, f_ext, a_lo, a_hi, f_lo, f_hi
):
    load_ext(info, a_ref, (rza, rzb), 0, a_ext)
    load_sides(info, (rxa, rxb), 0, a_lo, a_hi)
    f_ext[1 : CZ + 1] = f_ref[0]
    below, above = to_sides(info, 1, fza[n], fzb[n])
    f_ext[0] = below
    f_ext[CZ + 1] = above
    load_sides(info, (fxa, fxb), n * XR, f_lo, f_hi)
    sub, lane = iota(0), iota(1)

    def layer(z):
        a, f = a_ext[z + 1], f_ext[z + 1]
        total = (a - a_ext[z + 2]) * (f - f_ext[z + 2]) + (a - a_ext[z]) * (f - f_ext[z])
        x_hi = (a - jnp.where(sub == CX - 1, slab_row(a_hi, z), sub_up(a))) * (
            f - jnp.where(sub == CX - 1, slab_row(f_hi, z), sub_up(f))
        )
        x_lo = jnp.where(sub == 0, (a - slab_row(a_lo, z)) * (f - slab_row(f_lo, z)), sub_down(x_hi))
        y_hi = (a - jnp.where(lane == NY - 1, 0.0, lane_up(a))) * (f - jnp.where(lane == NY - 1, 0.0, lane_up(f)))
        y_lo = jnp.where(lane == 0, a * f, lane_down(y_hi))
        total = total + (x_hi + x_lo) + (y_hi + y_lo)
        out[z] = total if first else acc[z] + total

    each_layer(layer)


def coarsen(acc, cond, peak, rxa, rxb, out, known, rows, tall):
    pass_peak(peak, (rxa, rxb), XR, None, None, known)
    def layer(z):
        g = -0.5 * cond[z] * acc[z]
        g = g + sub_up(g)
        g = g + pltpu.roll(g, CX - 2, 0)
        rows[pl.ds(z, 1), :] = g[0:1]
        rows[pl.ds(CZ + z, 1), :] = g[4:5]

    each_layer(layer)
    group = lax.broadcasted_iota(jnp.int32, (128, 512), 1) // 4
    pick = jnp.where(group == lax.broadcasted_iota(jnp.int32, (128, 512), 0), 1.0, 0.0)
    tall[...] = jnp.zeros_like(tall)
    for k in range(3):
        tall[8 + 128 * k : 8 + 128 * (k + 1), :] = lax.dot_general(
            pick,
            rows[:, 512 * k : 512 * (k + 1)],
            (((1,), (1,)), ((), ())),
            precision=EXACT,
            preferred_element_type=F32,
        )
    for d in range(out.shape[0]):
        out[d, 0:WIN] = tall[48 * d : 48 * d + WIN, :]
        out[d, WIN : WIN + 8] = known[:, : 2 * CZ]


def assemble(pieces, window, coarse, upper):
    best = pieces[0, WIN : WIN + 8]
    for d in range(1, pieces.shape[0]):
        best = jnp.maximum(best, pieces[d, WIN : WIN + 8])
    upper[...] = best
    k = lax.broadcasted_iota(jnp.int32, (2 * CZ, 128), 0)
    z = lax.broadcasted_iota(jnp.int32, (2 * CZ, 128), 1)
    for p in range(2):
        total = jnp.zeros((WIN, 128), F32)
        for d in range(pieces.shape[0]):
            own = (z >= CZ * d) & (z < CZ * (d + 1)) & (k - CZ * p == z - CZ * d)
            total = total + jnp.dot(
                pieces[d, 0:WIN], jnp.where(own, 1.0, 0.0), precision=EXACT, preferred_element_type=F32
            )
        window[p] = total
        coarse[p] = total[8:56]


SPAN = 12


def prior_faces(first_column, first_row, w, fx, fy, fz, diag, peak):
    row = lax.broadcasted_iota(jnp.int32, (WIN, 128), 0)
    lane = lax.broadcasted_iota(jnp.int32, (WIN, 128), 1)
    y_in = (row + first_row >= 0) & (row + first_row < 384)
    y_link = y_in & (row + first_row + 1 >= 0) & (row + first_row + 1 < 384) & (row < WIN - 1)

    def x_in(j):
        return (first_column + j >= 0) & (first_column + j < 32)

    def wx(j):
        if j < 0 or j >= SPAN:
            return jnp.zeros((WIN, 128), F32)
        return jnp.where(x_in(j) & y_in, w[0, j], 0.0)

    best = None
    for j in range(SPAN):
        inside = x_in(j) & y_in
        here = wx(j)
        x_hi = 0.5 * (here + wx(j + 1))
        x_lo = 0.5 * (here + wx(j - 1))
        v = jnp.where(inside, w[1, j], 0.0)
        y_hi = 0.5 * (v + jnp.where(row == WIN - 1, 0.0, pltpu.roll(v, WIN - 1, 0)))
        y_lo = jnp.where(row == 0, 0.5 * v, pltpu.roll(y_hi, 1, 0))
        v = jnp.where(inside, w[2, j], 0.0)
        z_hi = 0.5 * (v + jnp.where(lane == 127, 0.0, pltpu.roll(v, 127, 1)))
        z_lo = jnp.where(lane == 0, 0.5 * v, pltpu.roll(z_hi, 1, 1))
        total = ((((x_hi + x_lo) + y_hi) + y_lo) + z_hi) + z_lo
        diag[j] = SHIFT + total
        fx[j] = jnp.where(inside & x_in(j + 1), x_hi, 0.0) if j + 1 < SPAN else jnp.zeros_like(x_hi)
        fy[j] = jnp.where(x_in(j) & y_link, y_hi, 0.0)
        fz[j] = jnp.where(inside & (lane < 127), z_hi, 0.0)
        if j in (5, 6):
            bound = jnp.max((SHIFT + 2.0 * total)[8:56].reshape(6, 8, 128), axis=0)
            best = bound if best is None else jnp.maximum(best, bound)
    peak[...] = jnp.full((8, 128), jnp.max(best))


def prior_setup(place, w, fx, fy, fz, diag, peak):
    prior_faces(place[0], place[1], w, fx, fy, fz, diag, peak)


def chebyshev(place, upper, g, fx, fy, fz, diag, out, r, d):
    row = lax.broadcasted_iota(jnp.int32, (WIN, 128), 0)
    y_in = (row + place[1] >= 0) & (row + place[1] < 384)
    top = upper[0:1, 0:1]
    centre = 0.5 * (top + SHIFT)
    half = 0.5 * (top - SHIFT)
    sigma = centre / half
    rho = 1.0 / sigma
    for j in range(SPAN):
        inside = (place[0] + j >= 0) & (place[0] + j < 32) & y_in
        start = jnp.where(inside, g[j], 0.0)
        r[j] = start
        d[0, j] = start / centre
    for p in range(2):
        out[p] = d[0, 5 + p, 8:56]
    for it in range(CHEB - 1):
        now, later = it % 2, (it + 1) % 2
        rho_new = 1.0 / (2.0 * sigma - rho)
        scale_d = rho_new * rho
        scale_r = 2.0 * rho_new / half
        for j in range(it + 1, SPAN - 1 - it):
            v = d[now, j]
            y_face, z_face = fy[j], fz[j]
            pull = fx[j] * d[now, j + 1] + fx[j - 1] * d[now, j - 1]
            pull = pull + y_face * pltpu.roll(v, WIN - 1, 0) + pltpu.roll(y_face * v, 1, 0)
            pull = pull + z_face * pltpu.roll(v, 127, 1) + pltpu.roll(z_face * v, 1, 1)
            left = r[j] - (diag[j] * v - pull)
            r[j] = left
            d[later, j] = scale_d * v + scale_r * left
        for p in range(2):
            out[p] = out[p] + d[later, 5 + p, 8:56]
        rho = rho_new


def on_device(
    conductivity, forward_states, sensor_cell, sensor_window, sensor_misfit, prior_conductance
):
    z_at, x_at = lax.axis_index("depth"), lax.axis_index("strip")
    z_n, x_n = lax.axis_size("depth"), lax.axis_size("strip")
    info = jnp.stack(
        [
            x_at % 2,
            z_at % 2,
            (x_at > 0).astype(jnp.int32),
            (x_at < x_n - 1).astype(jnp.int32),
            (z_at > 0).astype(jnp.int32),
            (z_at < z_n - 1).astype(jnp.int32),
        ]
    ).astype(jnp.int32)
    place = jnp.stack([2 * x_at - 5, 48 * z_at - 8]).astype(jnp.int32)
    x_odd, z_odd = x_at % 2 == 1, z_at % 2 == 1

    xs, zs = shape(STEPS * XR, 128), shape(STEPS, CX, NY)
    fxa, fxb, fza, fzb = call(pack_forward, (xs, xs, zs, zs), [SM, VM])(info, forward_states)
    prior_flat = prior_conductance.reshape(288, 128)
    fxa, fxb = swap((jnp.concatenate([fxa, prior_flat]), jnp.concatenate([fxb, prior_flat])), "strip")
    forward_x = (fxa, fxb)
    forward_z = swap((fza, fzb), "depth")

    layer = sensor_window * CZ + sensor_cell // (CX * NY)
    lateral = sensor_cell % NY
    code = layer * 16384 + (lateral // 128) * 1024 + (sensor_cell // NY) % CX * 128 + lateral % 128
    xs, zs = shape(2 * XR, 128), shape(2, CX, NY)
    sources, xa, xb, za, zb = call(
        scatter,
        (shape(STEPS, *FULL), xs, xs, zs, zs),
        [SM, SM, SM, VM],
        [pltpu.VMEM((STEPS * CZ, CX, NY), F32)] * BUFS,
        limit=18,
        flops=4 * 10**7,
    )(info, code, sensor_misfit, conductivity)
    rx, rz = swap((xa, xb), "strip"), swap((za, zb), "depth")

    full = shape(*FULL)
    table = call(
        faces, (shape(CZ + 1, CX, NY), full, full, full, full), [SM] + [VM] * 5, [EXT, SIDE, SIDE]
    )(info, conductivity, *rx, *rz)

    above = jnp.where(x_odd, fxb[STEPS * XR :], fxa[STEPS * XR :]).reshape(3, 2, 48, 128)
    below = jnp.where(x_odd, fxa[STEPS * XR :], fxb[STEPS * XR :]).reshape(3, 2, 48, 128)
    ring = [(i, (i + 2) % x_n) for i in range(x_n)]
    back = [(j, i) for i, j in ring]
    below2 = lax.ppermute(
        jnp.concatenate([below[:, 1:], prior_conductance], axis=1).reshape(432, 128), "strip", ring
    ).reshape(3, 3, 48, 128)
    above2 = lax.ppermute(
        jnp.concatenate([prior_conductance, above[:, :1]], axis=1).reshape(432, 128), "strip", back
    ).reshape(3, 3, 48, 128)
    weights = jnp.concatenate([below2, below, prior_conductance, above, above2], axis=1)
    low, high = weights[:, :, :8].reshape(288, 128), weights[:, :, 40:].reshape(288, 128)
    wza, wzb = swap((jnp.where(z_odd, low, high), jnp.where(z_odd, high, low)), "depth")
    under = jnp.where(z_odd, wza, wzb).reshape(3, SPAN, 8, 128)
    over = jnp.where(z_odd, wzb, wza).reshape(3, SPAN, 8, 128)
    weights = jnp.concatenate([under, weights, over], axis=2)
    span = shape(SPAN, WIN, 128)
    *prior, peak = call(prior_setup, (span, span, span, span, shape(8, 128)), [SM, VM])(place, weights)
    forcing = sources[STEPS - 1]
    base, slot = 0, 0
    acc = None
    small = shape(8, 128)
    known = jnp.zeros((8, 128), F32)
    for n in reversed(range(STEPS)):
        if n == STEPS - 2:
            known = peak
        xs, zs = shape(XR + 8, 128), shape(1, CX, NY)
        v, known, xa, xb, za, zb = call(
            functools.partial(first_sweep, base, slot, 2 * XR if n < STEPS - 1 else None),
            (full, small, xs, xs, zs, zs),
            [SM] + [VM] * 11,
            [EXT, SIDE, SIDE],
        )(info, known, forcing, *table, *rx, *rz)
        rx, rz = swap((xa, xb), "strip"), swap((za, zb), "depth")
        more = n > 0
        fields = 2 if more else 1
        xs, zs = shape(fields * XR + 8, 128), shape(fields, CX, NY)
        before = max(n - 1, 0)
        adjoint, after, known, xa, xb, za, zb = call(
            functools.partial(second_sweep, more),
            (full, full if more else small, small, xs, xs, zs, zs),
            [SM] + [VM] * 13,
            [EXT, SIDE, SIDE],
        )(info, known, v, forcing, sources[before : before + 1], *table, *rx, *rz)
        rx, rz = swap((xa, xb), "strip"), swap((za, zb), "depth")
        first = acc is None
        acc = call(
            functools.partial(gradient, n, first),
            full,
            [SM] + [VM] * 11,
            [EXT, EXT, SIDE, SIDE, SIDE, SIDE],
        )(info, adjoint, forward_states[n : n + 1], adjoint if first else acc, *rx, *rz, *forward_x, *forward_z)
        forcing = after
        base, slot = XR, 1

    pieces, _ = call(
        coarsen,
        (shape(z_n, WIN + 8, 2 * CZ), small),
        [VM] * 5,
        [pltpu.VMEM((2 * CZ, NY), F32), pltpu.VMEM((400, 2 * CZ), F32)],
    )(acc, conductivity, known, *rx)
    pieces = lax.all_to_all(pieces, "depth", 0, 0)
    window, coarse_grad, upper = call(
        assemble, (shape(2, WIN, 128), shape(2, 48, 128), shape(8, 2 * CZ)), [VM]
    )(pieces)
    flat = window.reshape(2 * WIN, 128)
    ga, gb = swap((flat, flat), "strip")
    above = jnp.where(x_odd, gb, ga)
    below = jnp.where(x_odd, ga, gb)
    below2 = lax.ppermute(jnp.concatenate([below[WIN:], flat]), "strip", ring)
    above2 = lax.ppermute(jnp.concatenate([flat, above[:WIN]]), "strip", back)
    g = jnp.concatenate([below2, below, flat, above, above2]).reshape(SPAN, WIN, 128)
    step = call(
        chebyshev,
        shape(2, 48, 128),
        [SM] + [VM] * 6,
        [pltpu.VMEM((SPAN, WIN, 128), F32), pltpu.VMEM((2, SPAN, WIN, 128), F32)],
    )(place, upper, g, *prior)
    return coarse_grad, step


def solution(mesh):
    placed = (
        P("depth", "strip", None),
        P(None, "depth", "strip", None),
        P(("depth", "strip")),
        P(("depth", "strip")),
        P(("depth", "strip")),
        P(None, "strip", "depth", None),
    )
    return jax.shard_map(
        on_device,
        mesh=mesh,
        in_specs=placed,
        out_specs=(P("strip", "depth", None), P("strip", "depth", None)),
        check_vma=False,
    )
```

```python
import functools

import jax
import jax.numpy as jnp
from jax import lax
from jax.experimental import pallas as pl
from jax.experimental.pallas import tpu as pltpu
from jax.sharding import PartitionSpec as P

F32 = jnp.float32
STEPS = 5
CHEB = 6
CZ, CX, NY = 16, 8, 1536
TILES = NY // 128
ZR = TILES * CX
XR = TILES * CZ
ROWS = CZ * ZR
OWN = 8 + ZR
WIN = 64
SPAN = 6
PRIOR = 288
SHIFT = 0.5
EXACT = lax.Precision.HIGHEST

VM = pl.BlockSpec(memory_space=pltpu.VMEM)
SM = pl.BlockSpec(memory_space=pltpu.SMEM)
ANY = pl.BlockSpec(memory_space=pl.ANY)


def shape(*dims):
    return jax.ShapeDtypeStruct(dims, F32)


def call(body, outs, ins, scratch=(), limit=6, flops=4 * 10**6, traffic=5 * 10**6):
    return pl.pallas_call(
        body,
        out_shape=outs,
        in_specs=ins,
        out_specs=jax.tree.map(lambda _: VM, outs),
        scratch_shapes=list(scratch),
        compiler_params=pltpu.CompilerParams(vmem_limit_bytes=limit * 2**20),
        cost_estimate=pl.CostEstimate(flops=flops, bytes_accessed=traffic, transcendentals=0),
    )


def pairs_a(n):
    return [(i, i ^ 1) for i in range(n)]


def pairs_b(n):
    return [(i, (((i + 1) ^ 1) - 1) % n) for i in range(n)]


def swap(send, axis):
    n = lax.axis_size(axis)
    return lax.ppermute(send[0], axis, pairs_a(n)), lax.ppermute(send[1], axis, pairs_b(n))


def to_sides(info, k, first, second):
    odd = info[k] == 1
    below = jnp.where(info[2 + 2 * k] == 1, jnp.where(odd, first, second), 0.0)
    above = jnp.where(info[3 + 2 * k] == 1, jnp.where(odd, second, first), 0.0)
    return below, above


def from_sides(info, k, below, above):
    odd = info[k] == 1
    return jnp.where(odd, below, above), jnp.where(odd, above, below)


def put_x(info, refs, to, field, base):
    for t in range(TILES):
        low = field[pl.ds(base + t * CX, CZ, stride=ZR), :]
        high = field[pl.ds(base + t * CX + CX - 1, CZ, stride=ZR), :]
        first, second = from_sides(info, 0, low, high)
        refs[0][to + t * CZ : to + (t + 1) * CZ, :] = first
        refs[1][to + t * CZ : to + (t + 1) * CZ, :] = second


def put_z(info, refs, to, field, base):
    first, second = from_sides(info, 1, field[base : base + ZR, :], field[base + ROWS - ZR : base + ROWS, :])
    refs[0][to : to + ZR, :] = first
    refs[1][to : to + ZR, :] = second


def load_sides(info, rx, base, side):
    side[...] = jnp.zeros_like(side)
    for t in range(TILES):
        at = base + t * CZ
        low, high = to_sides(info, 0, rx[0][at : at + CZ, :], rx[1][at : at + CZ, :])
        side[pl.ds(t * CX, CZ, stride=ZR), :] = low
        side[pl.ds(t * CX + CX - 1, CZ, stride=ZR), :] = high


def load_ext(info, field, base, rz, at, ext):
    ext[OWN : OWN + ROWS, :] = field[base : base + ROWS, :]
    low, high = to_sides(info, 1, rz[0][at : at + ZR, :], rz[1][at : at + ZR, :])
    ext[OWN - ZR : OWN, :] = low
    ext[OWN + ROWS : OWN + ROWS + ZR, :] = high


def pass_peak(mine, rx, at, sends, to, out):
    best = mine[...]
    if at is not None:
        best = jnp.maximum(best, jnp.maximum(rx[0][at : at + 8, :], rx[1][at : at + 8, :]))
    out[...] = best
    if sends is not None:
        for send in sends:
            send[to : to + 8, :] = best


EXT = pltpu.VMEM((OWN + ROWS + ZR + 8, 128), F32)
SIDE = pltpu.VMEM((ROWS, 128), F32)


def iota(axis):
    return lax.broadcasted_iota(jnp.int32, (CX, 128), axis)


def lanes_up(tiles, lane):
    moved = [pltpu.roll(v, 127, 1) for v in tiles]
    return [jnp.where(lane == 127, moved[(t + 1) % TILES], moved[t]) for t in range(TILES)]


def lanes_down(tiles, lane):
    moved = [pltpu.roll(v, 1, 1) for v in tiles]
    return [jnp.where(lane == 0, moved[t - 1], moved[t]) for t in range(TILES)]


def rows_of(z, t):
    return pl.multiple_of(z * ZR + t * CX, CX)


def tile(ref, row, offset=0):
    return ref[pl.ds(row + offset, CX), :]


def each_layer(body):
    def step(z, carry):
        body(z)
        return carry

    lax.fori_loop(0, CZ, step, 0)


GROUP = 4


def scatter(info, code, misfit, cond, prior, out, xa, xb, za, zb):
    out[...] = jnp.zeros_like(out)
    place = iota(0) * 128 + iota(1)

    def step(i, carry):
        codes = [code[i * GROUP + k] for k in range(GROUP)]
        at = [lax.shift_right_logical(c, 10) * CX for c in codes]
        adds = [jnp.where(place == (c & 1023), misfit[i * GROUP + k], 0.0) for k, c in enumerate(codes)]
        sums = [tile(out, pl.multiple_of(a, CX)) for a in at]
        for k in range(GROUP):
            total = sums[k] + adds[k]
            for j in range(k):
                total = total + jnp.where(at[j] == at[k], adds[j], 0.0)
            out[pl.ds(pl.multiple_of(at[k], CX), CX), :] = total
        return carry

    lax.fori_loop(0, code.shape[0] // GROUP, step, 0, unroll=8)
    base = (STEPS - 1) * ROWS
    put_x(info, (xa, xb), 0, out, base)
    put_x(info, (xa, xb), XR, cond, 0)
    xa[2 * XR :, :] = prior[...]
    xb[2 * XR :, :] = prior[...]
    put_z(info, (za, zb), 0, out, base)
    put_z(info, (za, zb), ZR, cond, 0)


def faces(info, cond, rxa, rxb, rza, rzb, fz, fy, fxh, fxl, fxb, inv, ext, side):
    load_ext(info, cond, 0, (rza, rzb), ZR, ext)
    load_sides(info, (rxa, rxb), XR, side)
    sub, lane = iota(0), iota(1)

    def layer(z):
        rows = [rows_of(z, t) for t in range(TILES)]
        cs = [tile(ext, r, OWN) for r in rows]
        ups = lanes_up(cs, lane)
        ups[-1] = jnp.where(lane == 127, 0.0, ups[-1])
        y_hi = [0.5 * (c + u) for c, u in zip(cs, ups)]
        y_lo = lanes_down(y_hi, lane)
        y_lo[0] = jnp.where(lane == 0, 0.5 * cs[0], y_lo[0])
        for t, r in enumerate(rows):
            c = cs[t]
            here = pl.ds(r, CX)
            beside = tile(side, r)
            z_lo = 0.5 * (c + tile(ext, r, OWN - ZR))
            z_hi = 0.5 * (c + tile(ext, r, OWN + ZR))
            x_hi = 0.5 * (c + jnp.where(sub == CX - 1, beside, tile(ext, r, OWN + 1)))
            x_lo = 0.5 * (c + jnp.where(sub == 0, beside, tile(ext, r, OWN - 1)))
            fz[here, :] = z_lo
            fz[pl.ds(r + ZR, CX), :] = z_hi
            fy[here, :] = jnp.where(lane == 127, 0.0, y_hi[t]) if t == TILES - 1 else y_hi[t]
            fxh[here, :] = jnp.where(sub == CX - 1, 0.0, x_hi)
            fxl[here, :] = jnp.where(sub == 0, 0.0, x_lo)
            fxb[here, :] = jnp.where(sub == CX - 1, x_hi, jnp.where(sub == 0, x_lo, 0.0))
            inv[here, :] = 1.0 / (1.0 + (((((z_hi + z_lo) + x_hi) + x_lo) + y_hi[t]) + y_lo[t]))

    each_layer(layer)


def sweep(right, base, fz, fy, fxh, fxl, fxb, inv, ext, side, lane, z):
    rows = [rows_of(z, t) for t in range(TILES)]
    vs = [tile(ext, r, OWN) for r in rows]
    ys = [tile(fy, r) for r in rows]
    ups = lanes_up(vs, lane)
    downs = lanes_down([y * v for y, v in zip(ys, vs)], lane)
    new = []
    for t, r in enumerate(rows):
        spread = tile(fz, r, ZR) * tile(ext, r, OWN + ZR) + tile(fz, r) * tile(ext, r, OWN - ZR)
        spread = spread + (tile(fxh, r) * tile(ext, r, OWN + 1) + tile(fxl, r) * tile(ext, r, OWN - 1))
        spread = spread + tile(fxb, r) * tile(side, r)
        spread = spread + (ys[t] * ups[t] + downs[t])
        new.append((tile(right, r, base) + spread) * tile(inv, r))
    return rows, new


def first_sweep(n, info, peak, forcing, fwd, low, high, *refs):
    first = n == STEPS - 1
    fz, fy, fxh, fxl, fxb, inv, rxa, rxb, rza, rzb, out, known, xa, xb, za, zb, ext, side = refs
    base = (STEPS - 1) * ROWS if first else 0
    pass_peak(peak, (rxa, rxb), None if first else 2 * XR, (xa, xb), 2 * XR, known)
    load_ext(info, forcing, base, (rza, rzb), 0 if first else ZR, ext)
    load_sides(info, (rxa, rxb), 0 if first else XR, side)
    lane = iota(1)

    def layer(z):
        rows, new = sweep(forcing, base, fz, fy, fxh, fxl, fxb, inv, ext, side, lane, z)
        for r, v in zip(rows, new):
            out[pl.ds(r, CX), :] = v

    each_layer(layer)
    put_x(info, (xa, xb), 0, out, 0)
    put_z(info, (za, zb), 0, out, 0)
    put_x(info, (xa, xb), XR, fwd, n * ROWS)
    put_z(info, (za, zb), ZR, fwd, n * ROWS)
    if first:
        one, two = from_sides(info, 1, low[...], high[...])
        za[2 * ZR :, :] = one
        zb[2 * ZR :, :] = two


def second_sweep(n, info, peak, v, forcing, source, earlier, *refs):
    fz, fy, fxh, fxl, fxb, inv, rxa, rxb, rza, rzb, out, after, known, xa, xb, za, zb, ext, side = refs
    base = (STEPS - 1) * ROWS if n == STEPS - 1 else 0
    pass_peak(peak, (rxa, rxb), 2 * XR, (xa, xb), 2 * XR if n else XR, known)
    load_ext(info, v, 0, (rza, rzb), 0, ext)
    load_sides(info, (rxa, rxb), 0, side)
    lane = iota(1)

    def layer(z):
        rows, new = sweep(forcing, base, fz, fy, fxh, fxl, fxb, inv, ext, side, lane, z)
        for r, v in zip(rows, new):
            out[pl.ds(r, CX), :] = v
            if n:
                after[pl.ds(r, CX), :] = v + tile(source, r, (n - 1) * ROWS)

    each_layer(layer)
    put_x(info, (xa, xb), 0, out, 0)
    put_z(info, (za, zb), 0, out, 0)
    if n:
        put_x(info, (xa, xb), XR, after, 0)
        put_z(info, (za, zb), ZR, after, 0)


def gradient(n, info, a_ref, f_ref, acc, *refs):
    rxa, rxb, rza, rzb, fxa, fxb, fza, fzb, out, a_ext, f_ext, a_side, f_side = refs
    load_ext(info, a_ref, 0, (rza, rzb), 0, a_ext)
    load_sides(info, (rxa, rxb), 0, a_side)
    load_ext(info, f_ref, n * ROWS, (fza, fzb), ZR, f_ext)
    load_sides(info, (fxa, fxb), XR, f_side)
    sub, lane = iota(0), iota(1)

    def layer(z):
        rows = [rows_of(z, t) for t in range(TILES)]
        a_s = [tile(a_ext, r, OWN) for r in rows]
        f_s = [tile(f_ext, r, OWN) for r in rows]
        a_up, f_up = lanes_up(a_s, lane), lanes_up(f_s, lane)
        a_up[-1] = jnp.where(lane == 127, 0.0, a_up[-1])
        f_up[-1] = jnp.where(lane == 127, 0.0, f_up[-1])
        y_hi = [(a - au) * (f - fu) for a, au, f, fu in zip(a_s, a_up, f_s, f_up)]
        y_lo = lanes_down(y_hi, lane)
        y_lo[0] = jnp.where(lane == 0, a_s[0] * f_s[0], y_lo[0])
        for t, r in enumerate(rows):
            a, f = a_s[t], f_s[t]
            total = y_hi[t] + y_lo[t]
            for step in (ZR, -ZR):
                total = total + (a - tile(a_ext, r, OWN + step)) * (f - tile(f_ext, r, OWN + step))
            for step, edge in ((1, CX - 1), (-1, 0)):
                a_by = jnp.where(sub == edge, tile(a_side, r), tile(a_ext, r, OWN + step))
                f_by = jnp.where(sub == edge, tile(f_side, r), tile(f_ext, r, OWN + step))
                total = total + (a - a_by) * (f - f_by)
            out[pl.ds(r, CX), :] = total if n == STEPS - 1 else tile(acc, r) + total

    each_layer(layer)


def coarsen(acc, cond, peak, rxa, rxb, out, known, fine, rows, tall):
    pass_peak(peak, (rxa, rxb), XR, None, None, known)
    fine[...] = -0.5 * cond[...] * acc[...]
    for t in range(TILES):
        for p in range(2):
            total = None
            for x in range(4):
                part = fine[pl.ds(t * CX + 4 * p + x, CZ, stride=ZR), :]
                total = part if total is None else total + part
            rows[p * CZ : (p + 1) * CZ, t * 128 : (t + 1) * 128] = total
    group = lax.broadcasted_iota(jnp.int32, (128, 512), 1) // 4
    pick = jnp.where(group == lax.broadcasted_iota(jnp.int32, (128, 512), 0), 1.0, 0.0)
    tall[...] = jnp.zeros_like(tall)
    for k in range(3):
        tall[8 + 128 * k : 8 + 128 * (k + 1), :] = lax.dot_general(
            pick,
            rows[:, 512 * k : 512 * (k + 1)],
            (((1,), (1,)), ((), ())),
            precision=EXACT,
            preferred_element_type=F32,
        )
    for d in range(out.shape[0]):
        out[d, 0:WIN] = tall[48 * d : 48 * d + WIN, :]
        out[d, WIN : WIN + 8] = known[:, : 2 * CZ]


def assemble(pieces, window, coarse, upper):
    best = pieces[0, WIN : WIN + 8]
    for d in range(1, pieces.shape[0]):
        best = jnp.maximum(best, pieces[d, WIN : WIN + 8])
    upper[...] = best
    k = lax.broadcasted_iota(jnp.int32, (2 * CZ, 128), 0)
    z = lax.broadcasted_iota(jnp.int32, (2 * CZ, 128), 1)
    for p in range(2):
        total = jnp.zeros((WIN, 128), F32)
        for d in range(pieces.shape[0]):
            own = (z >= CZ * d) & (z < CZ * (d + 1)) & (k - CZ * p == z - CZ * d)
            total = total + jnp.dot(
                pieces[d, 0:WIN], jnp.where(own, 1.0, 0.0), precision=EXACT, preferred_element_type=F32
            )
        window[p * WIN : (p + 1) * WIN, :] = total
        coarse[p] = total[8:56]


def prior_setup(place, w, fx, fy, fz, diag, peak):
    first_column, first_row = place[0], place[1]
    row = lax.broadcasted_iota(jnp.int32, (WIN, 128), 0)
    lane = lax.broadcasted_iota(jnp.int32, (WIN, 128), 1)
    y_in = (row + first_row >= 0) & (row + first_row < 384)
    y_link = y_in & (row + first_row + 1 >= 0) & (row + first_row + 1 < 384) & (row < WIN - 1)

    def x_in(j):
        return (first_column + j >= 0) & (first_column + j < 32)

    def wx(j):
        if j < 0 or j >= SPAN:
            return jnp.zeros((WIN, 128), F32)
        return jnp.where(x_in(j) & y_in, w[0, j], 0.0)

    best = None
    for j in range(SPAN):
        inside = x_in(j) & y_in
        here = wx(j)
        x_hi = 0.5 * (here + wx(j + 1))
        x_lo = 0.5 * (here + wx(j - 1))
        v = jnp.where(inside, w[1, j], 0.0)
        y_hi = 0.5 * (v + jnp.where(row == WIN - 1, 0.0, pltpu.roll(v, WIN - 1, 0)))
        y_lo = jnp.where(row == 0, 0.5 * v, pltpu.roll(y_hi, 1, 0))
        v = jnp.where(inside, w[2, j], 0.0)
        z_hi = 0.5 * (v + jnp.where(lane == 127, 0.0, pltpu.roll(v, 127, 1)))
        z_lo = jnp.where(lane == 0, 0.5 * v, pltpu.roll(z_hi, 1, 1))
        total = ((((x_hi + x_lo) + y_hi) + y_lo) + z_hi) + z_lo
        diag[j] = SHIFT + total
        fx[j] = jnp.where(inside & x_in(j + 1), x_hi, 0.0) if j + 1 < SPAN else jnp.zeros_like(x_hi)
        fy[j] = jnp.where(x_in(j) & y_link, y_hi, 0.0)
        fz[j] = jnp.where(inside & (lane < 127), z_hi, 0.0)
        if j in (2, 3):
            bound = jnp.max((SHIFT + 2.0 * total)[8:56].reshape(6, 8, 128), axis=0)
            best = bound if best is None else jnp.maximum(best, bound)
    peak[...] = jnp.full((8, 128), jnp.max(best))


def coefficients(upper):
    top = upper[0:1, 0:1]
    centre = 0.5 * (top + SHIFT)
    half = 0.5 * (top - SHIFT)
    sigma = centre / half
    rho = 1.0 / sigma
    scales = []
    for _ in range(CHEB - 1):
        rho_new = 1.0 / (2.0 * sigma - rho)
        scales.append((rho_new * rho, 2.0 * rho_new / half))
        rho = rho_new
    return centre, scales


def cheb_column(j, scale, r, d, prior):
    fx, fy, fz, diag = prior
    v = d[j]
    y_face, z_face = fy[j], fz[j]
    pull = fx[j] * d[j + 1] + fx[j - 1] * d[j - 1]
    pull = pull + y_face * pltpu.roll(v, WIN - 1, 0) + pltpu.roll(y_face * v, 1, 0)
    pull = pull + z_face * pltpu.roll(v, 127, 1) + pltpu.roll(z_face * v, 1, 1)
    left = r[j] - (diag[j] * v - pull)
    return left, scale[0] * v + scale[1] * left


def block(ref, k):
    return ref[k * WIN : (k + 1) * WIN, :]


def cheb_send(info, d, r, sa, sb):
    for k, (low, high) in enumerate(((d[2], d[2]), (d[3], d[3]), (r[2], r[3]))):
        one, two = from_sides(info, 0, low, high)
        sa[k * WIN : (k + 1) * WIN, :] = one
        sb[k * WIN : (k + 1) * WIN, :] = two


def cheb_two(first, r, d, scales, prior):
    r, d = dict(r), dict(d)
    sums = []
    for it in range(2):
        fresh = {}
        for j in range(1 + it, SPAN - 1 - it):
            r[j], fresh[j] = cheb_column(j, scales[first + it], r, d, prior)
        d = fresh
        sums.append((d[2], d[3]))
    return r, d, sums


def cheb_one(info, upper, g, ra, rb, fx, fy, fz, diag, out, r_out, d_out, sa, sb):
    centre, scales = coefficients(upper)
    r = {2: block(g, 0), 3: block(g, 1)}
    for k in range(2):
        r[k], r[4 + k] = to_sides(info, 0, block(ra, k), block(rb, k))
    d = {j: v / centre for j, v in r.items()}
    start = (d[2], d[3])
    r, d, sums = cheb_two(0, r, d, scales, (fx, fy, fz, diag))
    for p in range(2):
        out[p] = ((start[p] + sums[0][p]) + sums[1][p])[8:56]
        r_out[p], d_out[p] = r[2 + p], d[2 + p]
    cheb_send(info, d, r, sa, sb)


def cheb_mid(info, upper, x, r_in, d_in, ra, rb, fx, fy, fz, diag, out, r_out, d_out, sa, sb):
    _, scales = coefficients(upper)
    r, d = {2: r_in[0], 3: r_in[1]}, {2: d_in[0], 3: d_in[1]}
    for k in range(2):
        d[k], d[4 + k] = to_sides(info, 0, block(ra, k), block(rb, k))
    r[1], r[4] = to_sides(info, 0, block(ra, 2), block(rb, 2))
    r, d, sums = cheb_two(2, r, d, scales, (fx, fy, fz, diag))
    for p in range(2):
        out[p] = (x[p] + sums[0][p][8:56]) + sums[1][p][8:56]
        r_out[p], d_out[p] = r[2 + p], d[2 + p]
    one, two = from_sides(info, 0, d[2], d[3])
    sa[...] = one
    sb[...] = two


def cheb_last(info, upper, x, r_in, d_in, ra, rb, fx, fy, fz, diag, out):
    _, scales = coefficients(upper)
    r, d = {2: r_in[0], 3: r_in[1]}, {2: d_in[0], 3: d_in[1]}
    d[1], d[4] = to_sides(info, 0, ra[...], rb[...])
    for p in range(2):
        _, new = cheb_column(2 + p, scales[4], r, d, (fx, fy, fz, diag))
        out[p] = x[p] + new[8:56]


def as_rows(field):
    lead = field.shape[:-2]
    return jnp.swapaxes(field.reshape(*lead, CX, TILES, 128), -3, -2).reshape(-1, 128)


def on_device(
    conductivity, forward_states, sensor_cell, sensor_window, sensor_misfit, prior_conductance
):
    z_at, x_at = lax.axis_index("depth"), lax.axis_index("strip")
    z_n, x_n = lax.axis_size("depth"), lax.axis_size("strip")
    info = jnp.stack(
        [
            x_at % 2,
            z_at % 2,
            (x_at > 0).astype(jnp.int32),
            (x_at < x_n - 1).astype(jnp.int32),
            (z_at > 0).astype(jnp.int32),
            (z_at < z_n - 1).astype(jnp.int32),
        ]
    ).astype(jnp.int32)
    place = jnp.stack([2 * x_at - 2, 48 * z_at - 8]).astype(jnp.int32)
    x_odd, z_odd = x_at % 2 == 1, z_at % 2 == 1
    cond = as_rows(conductivity)
    fwd = as_rows(forward_states)
    field, small = shape(ROWS, 128), shape(8, 128)

    layer = sensor_window * CZ + sensor_cell // (CX * NY)
    lateral = sensor_cell % NY
    code = (layer * TILES + lateral // 128) * 1024 + (sensor_cell // NY) % CX * 128 + lateral % 128
    xs, zs = shape(2 * XR + PRIOR, 128), shape(2 * ZR, 128)
    sources, xa, xb, za, zb = call(
        scatter, (shape(STEPS * ROWS, 128), xs, xs, zs, zs), [SM, SM, SM, VM, VM], flops=4 * 10**7
    )(info, code, sensor_misfit, cond, prior_conductance.reshape(PRIOR, 128))
    rx, rz = swap((xa, xb), "strip"), swap((za, zb), "depth")
    table = call(
        faces, (shape(ROWS + ZR, 128),) + (field,) * 5, [SM] + [VM] * 5, [EXT, SIDE]
    )(info, cond, *rx, *rz)
    above = jnp.where(x_odd, rx[1][2 * XR :], rx[0][2 * XR :]).reshape(3, 2, 48, 128)
    below = jnp.where(x_odd, rx[0][2 * XR :], rx[1][2 * XR :]).reshape(3, 2, 48, 128)
    weights = jnp.concatenate([below, prior_conductance, above], axis=1)
    low, high = weights[:, :, :8].reshape(144, 128), weights[:, :, 40:].reshape(144, 128)

    forcing = sources
    known = jnp.zeros((8, 128), F32)
    acc = known
    waiting = None
    for n in reversed(range(STEPS)):
        first = n == STEPS - 1
        xs, zs = shape(2 * XR + 8, 128), shape(2 * ZR + (144 if first else 0), 128)
        v, known, xa, xb, za, zb = call(
            functools.partial(first_sweep, n),
            (field, small, xs, xs, zs, zs),
            [SM] + [VM] * 3 + [VM if first else ANY] * 2 + [VM] * 10,
            [EXT, SIDE],
        )(info, known, forcing, fwd, low, high, *table, *rx, *rz)
        rx, rz = swap((xa, xb), "strip"), swap((za, zb), "depth")
        if first:
            tails = rz[0][2 * ZR :], rz[1][2 * ZR :]
            under = jnp.where(z_odd, tails[0], tails[1]).reshape(3, SPAN, 8, 128)
            over = jnp.where(z_odd, tails[1], tails[0]).reshape(3, SPAN, 8, 128)
            span = shape(SPAN, WIN, 128)
            *prior, peak = call(prior_setup, (span, span, span, span, small), [SM, VM])(
                place, jnp.concatenate([under, weights, over], axis=2)
            )
        if waiting is not None:
            acc = waiting()
        forward_x, forward_z = rx, rz
        fields = 2 if n else 1
        xs, zs = shape(fields * XR + 8, 128), shape(fields * ZR, 128)
        adjoint, after, known, xa, xb, za, zb = call(
            functools.partial(second_sweep, n),
            (field, field if n else small, small, xs, xs, zs, zs),
            [SM] + [VM] * 3 + [VM if n else ANY, ANY] + [VM] * 10,
            [EXT, SIDE],
        )(info, known, v, forcing, sources, acc, *table, *rx, *rz)
        rx, rz = swap((xa, xb), "strip"), swap((za, zb), "depth")

        def waiting(n=n, adjoint=adjoint, acc=acc, halos=(*rx, *rz, *forward_x, *forward_z)):
            return call(
                functools.partial(gradient, n),
                field,
                [SM] + [VM] * 2 + [ANY if n == STEPS - 1 else VM] + [VM] * 8,
                [EXT, EXT, SIDE, SIDE],
            )(info, adjoint, fwd, acc, *halos)

        if first:
            known = peak
        forcing = after
    acc = waiting()

    pieces, _ = call(
        coarsen,
        (shape(z_n, WIN + 8, 2 * CZ), small),
        [VM] * 5,
        [SIDE, pltpu.VMEM((2 * CZ, NY), F32), pltpu.VMEM((400, 2 * CZ), F32)],
    )(acc, cond, known, *rx)
    pieces = lax.all_to_all(pieces, "depth", 0, 0)
    window, coarse_grad, upper = call(
        assemble, (shape(2 * WIN, 128), shape(2, 48, 128), shape(8, 2 * CZ)), [VM]
    )(pieces)

    own, both = shape(2, 48, 128), shape(2, WIN, 128)
    sides = swap((window, window), "strip")
    x, r, d, sa, sb = call(
        cheb_one, (own, both, both, shape(3 * WIN, 128), shape(3 * WIN, 128)), [SM] + [VM] * 8
    )(info, upper, window, *sides, *prior)
    sides = swap((sa, sb), "strip")
    x, r, d, sa, sb = call(
        cheb_mid, (own, both, both, shape(WIN, 128), shape(WIN, 128)), [SM] + [VM] * 10
    )(info, upper, x, r, d, *sides, *prior)
    sides = swap((sa, sb), "strip")
    step = call(cheb_last, own, [SM] + [VM] * 10)(info, upper, x, r, d, *sides, *prior)
    return coarse_grad, step


def solution(mesh):
    placed = (
        P("depth", "strip", None),
        P(None, "depth", "strip", None),
        P(("depth", "strip")),
        P(("depth", "strip")),
        P(("depth", "strip")),
        P(None, "strip", "depth", None),
    )
    return jax.shard_map(
        on_device,
        mesh=mesh,
        in_specs=placed,
        out_specs=(P("strip", "depth", None), P("strip", "depth", None)),
        check_vma=False,
    )
```

```python
import functools

import jax
import jax.numpy as jnp
from jax import lax
from jax.experimental import pallas as pl
from jax.experimental.pallas import tpu as pltpu
from jax.sharding import PartitionSpec as P

F32 = jnp.float32
STEPS = 5
CHEB = 6
CZ, CX, NY = 16, 8, 1536
TILES = NY // 128
ZR = TILES * CX
XR = TILES * CZ
ROWS = CZ * ZR
OWN = 8 + ZR
WIN = 64
SPAN = 6
PRIOR = 288
SHIFT = 0.5
EXACT = lax.Precision.HIGHEST

VM = pl.BlockSpec(memory_space=pltpu.VMEM)
SM = pl.BlockSpec(memory_space=pltpu.SMEM)
ANY = pl.BlockSpec(memory_space=pl.ANY)


def shape(*dims):
    return jax.ShapeDtypeStruct(dims, F32)


def call(body, outs, ins, scratch=(), limit=6, flops=4 * 10**6, traffic=5 * 10**6):
    return pl.pallas_call(
        body,
        out_shape=outs,
        in_specs=ins,
        out_specs=jax.tree.map(lambda _: VM, outs),
        scratch_shapes=list(scratch),
        compiler_params=pltpu.CompilerParams(vmem_limit_bytes=limit * 2**20),
        cost_estimate=pl.CostEstimate(flops=flops, bytes_accessed=traffic, transcendentals=0),
    )


def pairs_a(n):
    return [(i, i ^ 1) for i in range(n)]


def pairs_b(n):
    return [(i, (((i + 1) ^ 1) - 1) % n) for i in range(n)]


def swap(send, axis):
    n = lax.axis_size(axis)
    return lax.ppermute(send[0], axis, pairs_a(n)), lax.ppermute(send[1], axis, pairs_b(n))


def to_sides(info, k, first, second):
    odd = info[k] == 1
    below = jnp.where(info[2 + 2 * k] == 1, jnp.where(odd, first, second), 0.0)
    above = jnp.where(info[3 + 2 * k] == 1, jnp.where(odd, second, first), 0.0)
    return below, above


def from_sides(info, k, below, above):
    odd = info[k] == 1
    return jnp.where(odd, below, above), jnp.where(odd, above, below)


def put_x(info, refs, to, field, base):
    for t in range(TILES):
        low = field[pl.ds(base + t * CX, CZ, stride=ZR), :]
        high = field[pl.ds(base + t * CX + CX - 1, CZ, stride=ZR), :]
        first, second = from_sides(info, 0, low, high)
        refs[0][to + t * CZ : to + (t + 1) * CZ, :] = first
        refs[1][to + t * CZ : to + (t + 1) * CZ, :] = second


def put_z(info, refs, to, field, base):
    first, second = from_sides(info, 1, field[base : base + ZR, :], field[base + ROWS - ZR : base + ROWS, :])
    refs[0][to : to + ZR, :] = first
    refs[1][to : to + ZR, :] = second


def load_sides(info, rx, base, side):
    side[...] = jnp.zeros_like(side)
    for t in range(TILES):
        at = base + t * CZ
        low, high = to_sides(info, 0, rx[0][at : at + CZ, :], rx[1][at : at + CZ, :])
        side[pl.ds(t * CX, CZ, stride=ZR), :] = low
        side[pl.ds(t * CX + CX - 1, CZ, stride=ZR), :] = high


def load_ext(info, field, base, rz, at, ext):
    ext[OWN : OWN + ROWS, :] = field[base : base + ROWS, :]
    low, high = to_sides(info, 1, rz[0][at : at + ZR, :], rz[1][at : at + ZR, :])
    ext[OWN - ZR : OWN, :] = low
    ext[OWN + ROWS : OWN + ROWS + ZR, :] = high


def pass_peak(mine, rx, at, sends, to, out):
    best = jnp.zeros((8, 128), F32) if mine is None else mine[...]
    if at is not None:
        best = jnp.maximum(best, jnp.maximum(rx[0][at : at + 8, :], rx[1][at : at + 8, :]))
    out[...] = best
    if sends is not None:
        for send in sends:
            send[to : to + 8, :] = best


EXT = pltpu.VMEM((OWN + ROWS + ZR + 8, 128), F32)
SIDE = pltpu.VMEM((ROWS, 128), F32)


def iota(axis):
    return lax.broadcasted_iota(jnp.int32, (CX, 128), axis)


def lanes_up(tiles, lane):
    moved = [pltpu.roll(v, 127, 1) for v in tiles]
    return [jnp.where(lane == 127, moved[(t + 1) % TILES], moved[t]) for t in range(TILES)]


def lanes_down(tiles, lane):
    moved = [pltpu.roll(v, 1, 1) for v in tiles]
    return [jnp.where(lane == 0, moved[t - 1], moved[t]) for t in range(TILES)]


def rows_of(z, t):
    return pl.multiple_of(z * ZR + t * CX, CX)


def tile(ref, row, offset=0):
    return ref[pl.ds(row + offset, CX), :]


def each_layer(body):
    def step(z, carry):
        body(z)
        return carry

    lax.fori_loop(0, CZ, step, 0, unroll=CZ)


GROUP = 4


def encode(cell, window, out):
    line = lax.shift_right_logical(lax.shift_right_logical(cell[...], 9) * 171, 9)
    lateral = cell[...] - line * NY
    layer = window[...] * CZ + lax.shift_right_logical(line, 3)
    spot = (layer * TILES + lax.shift_right_logical(lateral, 7)) * 1024
    out[...] = spot + (line & (CX - 1)) * 128 + (lateral & 127)


def scatter(info, code, misfit, cond, prior, out, xa, xb, za, zb):
    out[...] = jnp.zeros_like(out)
    place = iota(0) * 128 + iota(1)

    def step(i, carry):
        codes = [code[i * GROUP + k] for k in range(GROUP)]
        at = [lax.shift_right_logical(c, 10) * CX for c in codes]
        adds = [jnp.where(place == (c & 1023), misfit[i * GROUP + k], 0.0) for k, c in enumerate(codes)]
        sums = [tile(out, pl.multiple_of(a, CX)) for a in at]
        for k in range(GROUP):
            total = sums[k] + adds[k]
            for j in range(k):
                total = total + jnp.where(at[j] == at[k], adds[j], 0.0)
            out[pl.ds(pl.multiple_of(at[k], CX), CX), :] = total
        return carry

    lax.fori_loop(0, code.shape[0] // GROUP, step, 0, unroll=8)
    base = (STEPS - 1) * ROWS
    put_x(info, (xa, xb), 0, out, base)
    put_x(info, (xa, xb), XR, cond, 0)
    xa[2 * XR :, :] = prior[...]
    xb[2 * XR :, :] = prior[...]
    put_z(info, (za, zb), 0, out, base)
    put_z(info, (za, zb), ZR, cond, 0)


def faces(info, cond, rxa, rxb, rza, rzb, fz, fy, fxh, fxl, fxb, inv, ext, side):
    load_ext(info, cond, 0, (rza, rzb), ZR, ext)
    load_sides(info, (rxa, rxb), XR, side)
    sub, lane = iota(0), iota(1)

    def layer(z):
        rows = [rows_of(z, t) for t in range(TILES)]
        cs = [tile(ext, r, OWN) for r in rows]
        ups = lanes_up(cs, lane)
        ups[-1] = jnp.where(lane == 127, 0.0, ups[-1])
        y_hi = [0.5 * (c + u) for c, u in zip(cs, ups)]
        y_lo = lanes_down(y_hi, lane)
        y_lo[0] = jnp.where(lane == 0, 0.5 * cs[0], y_lo[0])
        for t, r in enumerate(rows):
            c = cs[t]
            here = pl.ds(r, CX)
            beside = tile(side, r)
            z_lo = 0.5 * (c + tile(ext, r, OWN - ZR))
            z_hi = 0.5 * (c + tile(ext, r, OWN + ZR))
            x_hi = 0.5 * (c + jnp.where(sub == CX - 1, beside, tile(ext, r, OWN + 1)))
            x_lo = 0.5 * (c + jnp.where(sub == 0, beside, tile(ext, r, OWN - 1)))
            fz[here, :] = z_lo
            fz[pl.ds(r + ZR, CX), :] = z_hi
            fy[here, :] = jnp.where(lane == 127, 0.0, y_hi[t]) if t == TILES - 1 else y_hi[t]
            fxh[here, :] = jnp.where(sub == CX - 1, 0.0, x_hi)
            fxl[here, :] = jnp.where(sub == 0, 0.0, x_lo)
            fxb[here, :] = jnp.where(sub == CX - 1, x_hi, jnp.where(sub == 0, x_lo, 0.0))
            inv[here, :] = 1.0 / (1.0 + (((((z_hi + z_lo) + x_hi) + x_lo) + y_hi[t]) + y_lo[t]))

    each_layer(layer)


def sweep(right, base, fz, fy, fxh, fxl, fxb, inv, ext, side, lane, z):
    rows = [rows_of(z, t) for t in range(TILES)]
    vs = [tile(ext, r, OWN) for r in rows]
    ys = [tile(fy, r) for r in rows]
    ups = lanes_up(vs, lane)
    downs = lanes_down([y * v for y, v in zip(ys, vs)], lane)
    new = []
    for t, r in enumerate(rows):
        spread = tile(fz, r, ZR) * tile(ext, r, OWN + ZR) + tile(fz, r) * tile(ext, r, OWN - ZR)
        spread = spread + (tile(fxh, r) * tile(ext, r, OWN + 1) + tile(fxl, r) * tile(ext, r, OWN - 1))
        spread = spread + tile(fxb, r) * tile(side, r)
        spread = spread + (ys[t] * ups[t] + downs[t])
        new.append((tile(right, r, base) + spread) * tile(inv, r))
    return rows, new


def prior_columns(info, k, prior, rx):
    columns = {}
    for p in range(2):
        at = (2 * k + p) * 48
        columns[2 + p] = prior[at : at + 48, :]
        at = at + 2 * XR
        columns[p], columns[4 + p] = to_sides(info, 0, rx[0][at : at + 48, :], rx[1][at : at + 48, :])
    return [columns[j] for j in range(SPAN)]


def first_sweep(n, info, forcing, fwd, prior, *refs):
    first = n == STEPS - 1
    fz, fy, fxh, fxl, fxb, inv, rxa, rxb, rza, rzb, out, known, xa, xb, za, zb, ext, side = refs
    peak = None if first else prior
    base = (STEPS - 1) * ROWS if first else 0
    pass_peak(peak, (rxa, rxb), None if first else 2 * XR, (xa, xb), 2 * XR, known)
    load_ext(info, forcing, base, (rza, rzb), 0 if first else ZR, ext)
    load_sides(info, (rxa, rxb), 0 if first else XR, side)
    lane = iota(1)

    def layer(z):
        rows, new = sweep(forcing, base, fz, fy, fxh, fxl, fxb, inv, ext, side, lane, z)
        for r, v in zip(rows, new):
            out[pl.ds(r, CX), :] = v

    each_layer(layer)
    put_x(info, (xa, xb), 0, out, 0)
    put_z(info, (za, zb), 0, out, 0)
    put_x(info, (xa, xb), XR, fwd, n * ROWS)
    put_z(info, (za, zb), ZR, fwd, n * ROWS)
    if first:
        for k in range(3):
            columns = prior_columns(info, k, prior, (rxa, rxb))
            for j, column in enumerate(columns):
                at = 2 * ZR + (k * SPAN + j) * 8
                za[at : at + 8, :], zb[at : at + 8, :] = from_sides(info, 1, column[:8], column[40:])


def second_sweep(n, info, v, forcing, source, *refs):
    if n == STEPS - 1:
        peak = None
    else:
        peak, earlier, *refs = refs
    fz, fy, fxh, fxl, fxb, inv, rxa, rxb, rza, rzb, out, after, known, xa, xb, za, zb, ext, side = refs
    base = (STEPS - 1) * ROWS if n == STEPS - 1 else 0
    pass_peak(peak, (rxa, rxb), 2 * XR, (xa, xb), 2 * XR if n else XR, known)
    load_ext(info, v, 0, (rza, rzb), 0, ext)
    load_sides(info, (rxa, rxb), 0, side)
    lane = iota(1)

    def layer(z):
        rows, new = sweep(forcing, base, fz, fy, fxh, fxl, fxb, inv, ext, side, lane, z)
        for r, v in zip(rows, new):
            out[pl.ds(r, CX), :] = v
            if n:
                after[pl.ds(r, CX), :] = v + tile(source, r, (n - 1) * ROWS)

    each_layer(layer)
    put_x(info, (xa, xb), 0, out, 0)
    put_z(info, (za, zb), 0, out, 0)
    if n:
        put_x(info, (xa, xb), XR, after, 0)
        put_z(info, (za, zb), ZR, after, 0)


def gradient(n, info, a_ref, f_ref, *refs):
    acc = None
    if n < STEPS - 1:
        acc, *refs = refs
    rxa, rxb, rza, rzb, fxa, fxb, fza, fzb, out, a_ext, f_ext, a_side, f_side = refs
    load_ext(info, a_ref, 0, (rza, rzb), 0, a_ext)
    load_sides(info, (rxa, rxb), 0, a_side)
    load_ext(info, f_ref, n * ROWS, (fza, fzb), ZR, f_ext)
    load_sides(info, (fxa, fxb), XR, f_side)
    sub, lane = iota(0), iota(1)

    def layer(z):
        rows = [rows_of(z, t) for t in range(TILES)]
        a_s = [tile(a_ext, r, OWN) for r in rows]
        f_s = [tile(f_ext, r, OWN) for r in rows]
        a_up, f_up = lanes_up(a_s, lane), lanes_up(f_s, lane)
        a_up[-1] = jnp.where(lane == 127, 0.0, a_up[-1])
        f_up[-1] = jnp.where(lane == 127, 0.0, f_up[-1])
        y_hi = [(a - au) * (f - fu) for a, au, f, fu in zip(a_s, a_up, f_s, f_up)]
        y_lo = lanes_down(y_hi, lane)
        y_lo[0] = jnp.where(lane == 0, a_s[0] * f_s[0], y_lo[0])
        for t, r in enumerate(rows):
            a, f = a_s[t], f_s[t]
            total = y_hi[t] + y_lo[t]
            for step in (ZR, -ZR):
                total = total + (a - tile(a_ext, r, OWN + step)) * (f - tile(f_ext, r, OWN + step))
            for step, edge in ((1, CX - 1), (-1, 0)):
                a_by = jnp.where(sub == edge, tile(a_side, r), tile(a_ext, r, OWN + step))
                f_by = jnp.where(sub == edge, tile(f_side, r), tile(f_ext, r, OWN + step))
                total = total + (a - a_by) * (f - f_by)
            out[pl.ds(r, CX), :] = total if acc is None else tile(acc, r) + total

    each_layer(layer)


def coarsen(acc, cond, peak, rxa, rxb, out, known, fine, rows, tall):
    pass_peak(peak, (rxa, rxb), XR, None, None, known)
    fine[...] = -0.5 * cond[...] * acc[...]
    for t in range(TILES):
        for p in range(2):
            total = None
            for x in range(4):
                part = fine[pl.ds(t * CX + 4 * p + x, CZ, stride=ZR), :]
                total = part if total is None else total + part
            rows[p * CZ : (p + 1) * CZ, t * 128 : (t + 1) * 128] = total
    group = lax.broadcasted_iota(jnp.int32, (128, 512), 1) // 4
    pick = jnp.where(group == lax.broadcasted_iota(jnp.int32, (128, 512), 0), 1.0, 0.0)
    tall[...] = jnp.zeros_like(tall)
    for k in range(3):
        tall[8 + 128 * k : 8 + 128 * (k + 1), :] = lax.dot_general(
            pick,
            rows[:, 512 * k : 512 * (k + 1)],
            (((1,), (1,)), ((), ())),
            precision=EXACT,
            preferred_element_type=F32,
        )
    for d in range(out.shape[0]):
        out[d, 0:WIN] = tall[48 * d : 48 * d + WIN, :]
        out[d, WIN : WIN + 8] = known[:, : 2 * CZ]


def assemble(pieces, window, coarse, upper):
    best = pieces[0, WIN : WIN + 8]
    for d in range(1, pieces.shape[0]):
        best = jnp.maximum(best, pieces[d, WIN : WIN + 8])
    upper[...] = best
    k = lax.broadcasted_iota(jnp.int32, (2 * CZ, 128), 0)
    z = lax.broadcasted_iota(jnp.int32, (2 * CZ, 128), 1)
    for p in range(2):
        total = jnp.zeros((WIN, 128), F32)
        for d in range(pieces.shape[0]):
            own = (z >= CZ * d) & (z < CZ * (d + 1)) & (k - CZ * p == z - CZ * d)
            total = total + jnp.dot(
                pieces[d, 0:WIN], jnp.where(own, 1.0, 0.0), precision=EXACT, preferred_element_type=F32
            )
        window[p * WIN : (p + 1) * WIN, :] = total
        coarse[p] = total[8:56]


def prior_setup(info, own, rxa, rxb, rza, rzb, fx, fy, fz, diag, peak, w):
    first_column, first_row = info[6], info[7]
    for k in range(3):
        for j, column in enumerate(prior_columns(info, k, own, (rxa, rxb))):
            at = 2 * ZR + (k * SPAN + j) * 8
            low, high = to_sides(info, 1, rza[at : at + 8, :], rzb[at : at + 8, :])
            w[k, j, 0:8] = low
            w[k, j, 8:56] = column
            w[k, j, 56:64] = high
    row = lax.broadcasted_iota(jnp.int32, (WIN, 128), 0)
    lane = lax.broadcasted_iota(jnp.int32, (WIN, 128), 1)
    y_in = (row + first_row >= 0) & (row + first_row < 384)
    y_link = y_in & (row + first_row + 1 >= 0) & (row + first_row + 1 < 384) & (row < WIN - 1)

    def x_in(j):
        return (first_column + j >= 0) & (first_column + j < 32)

    def wx(j):
        if j < 0 or j >= SPAN:
            return jnp.zeros((WIN, 128), F32)
        return jnp.where(x_in(j) & y_in, w[0, j], 0.0)

    best = None
    for j in range(SPAN):
        inside = x_in(j) & y_in
        here = wx(j)
        x_hi = 0.5 * (here + wx(j + 1))
        x_lo = 0.5 * (here + wx(j - 1))
        v = jnp.where(inside, w[1, j], 0.0)
        y_hi = 0.5 * (v + jnp.where(row == WIN - 1, 0.0, pltpu.roll(v, WIN - 1, 0)))
        y_lo = jnp.where(row == 0, 0.5 * v, pltpu.roll(y_hi, 1, 0))
        v = jnp.where(inside, w[2, j], 0.0)
        z_hi = 0.5 * (v + jnp.where(lane == 127, 0.0, pltpu.roll(v, 127, 1)))
        z_lo = jnp.where(lane == 0, 0.5 * v, pltpu.roll(z_hi, 1, 1))
        total = ((((x_hi + x_lo) + y_hi) + y_lo) + z_hi) + z_lo
        diag[j] = SHIFT + total
        fx[j] = jnp.where(inside & x_in(j + 1), x_hi, 0.0) if j + 1 < SPAN else jnp.zeros_like(x_hi)
        fy[j] = jnp.where(x_in(j) & y_link, y_hi, 0.0)
        fz[j] = jnp.where(inside & (lane < 127), z_hi, 0.0)
        if j in (2, 3):
            bound = jnp.max((SHIFT + 2.0 * total)[8:56].reshape(6, 8, 128), axis=0)
            best = bound if best is None else jnp.maximum(best, bound)
    peak[...] = jnp.full((8, 128), jnp.max(best))


def coefficients(upper):
    top = upper[0:1, 0:1]
    centre = 0.5 * (top + SHIFT)
    half = 0.5 * (top - SHIFT)
    sigma = centre / half
    rho = 1.0 / sigma
    scales = []
    for _ in range(CHEB - 1):
        rho_new = 1.0 / (2.0 * sigma - rho)
        scales.append((rho_new * rho, 2.0 * rho_new / half))
        rho = rho_new
    return centre, scales


def cheb_column(j, scale, r, d, prior):
    fx, fy, fz, diag = prior
    v = d[j]
    y_face, z_face = fy[j], fz[j]
    pull = fx[j] * d[j + 1] + fx[j - 1] * d[j - 1]
    pull = pull + y_face * pltpu.roll(v, WIN - 1, 0) + pltpu.roll(y_face * v, 1, 0)
    pull = pull + z_face * pltpu.roll(v, 127, 1) + pltpu.roll(z_face * v, 1, 1)
    left = r[j] - (diag[j] * v - pull)
    return left, scale[0] * v + scale[1] * left


def block(ref, k):
    return ref[k * WIN : (k + 1) * WIN, :]


def cheb_send(info, d, r, sa, sb):
    for k, (low, high) in enumerate(((d[2], d[2]), (d[3], d[3]), (r[2], r[3]))):
        one, two = from_sides(info, 0, low, high)
        sa[k * WIN : (k + 1) * WIN, :] = one
        sb[k * WIN : (k + 1) * WIN, :] = two


def cheb_two(first, r, d, scales, prior):
    r, d = dict(r), dict(d)
    sums = []
    for it in range(2):
        fresh = {}
        for j in range(1 + it, SPAN - 1 - it):
            r[j], fresh[j] = cheb_column(j, scales[first + it], r, d, prior)
        d = fresh
        sums.append((d[2], d[3]))
    return r, d, sums


def cheb_one(info, upper, g, ra, rb, fx, fy, fz, diag, out, r_out, d_out, sa, sb):
    centre, scales = coefficients(upper)
    r = {2: block(g, 0), 3: block(g, 1)}
    for k in range(2):
        r[k], r[4 + k] = to_sides(info, 0, block(ra, k), block(rb, k))
    d = {j: v / centre for j, v in r.items()}
    start = (d[2], d[3])
    r, d, sums = cheb_two(0, r, d, scales, (fx, fy, fz, diag))
    for p in range(2):
        out[p] = ((start[p] + sums[0][p]) + sums[1][p])[8:56]
        r_out[p], d_out[p] = r[2 + p], d[2 + p]
    cheb_send(info, d, r, sa, sb)


def cheb_mid(info, upper, x, r_in, d_in, ra, rb, fx, fy, fz, diag, out, r_out, d_out, sa, sb):
    _, scales = coefficients(upper)
    r, d = {2: r_in[0], 3: r_in[1]}, {2: d_in[0], 3: d_in[1]}
    for k in range(2):
        d[k], d[4 + k] = to_sides(info, 0, block(ra, k), block(rb, k))
    r[1], r[4] = to_sides(info, 0, block(ra, 2), block(rb, 2))
    r, d, sums = cheb_two(2, r, d, scales, (fx, fy, fz, diag))
    for p in range(2):
        out[p] = (x[p] + sums[0][p][8:56]) + sums[1][p][8:56]
        r_out[p], d_out[p] = r[2 + p], d[2 + p]
    one, two = from_sides(info, 0, d[2], d[3])
    sa[...] = one
    sb[...] = two


def cheb_last(info, upper, x, r_in, d_in, ra, rb, fx, fy, fz, diag, out):
    _, scales = coefficients(upper)
    r, d = {2: r_in[0], 3: r_in[1]}, {2: d_in[0], 3: d_in[1]}
    d[1], d[4] = to_sides(info, 0, ra[...], rb[...])
    for p in range(2):
        _, new = cheb_column(2 + p, scales[4], r, d, (fx, fy, fz, diag))
        out[p] = x[p] + new[8:56]


def as_rows(field):
    lead = field.shape[:-2]
    return jnp.swapaxes(field.reshape(*lead, CX, TILES, 128), -3, -2).reshape(-1, 128)


def on_device(
    conductivity, forward_states, sensor_cell, sensor_window, sensor_misfit, prior_conductance
):
    z_at, x_at = lax.axis_index("depth"), lax.axis_index("strip")
    z_n, x_n = lax.axis_size("depth"), lax.axis_size("strip")
    info = jnp.stack(
        [
            x_at % 2,
            z_at % 2,
            (x_at > 0).astype(jnp.int32),
            (x_at < x_n - 1).astype(jnp.int32),
            (z_at > 0).astype(jnp.int32),
            (z_at < z_n - 1).astype(jnp.int32),
            2 * x_at - 2,
            48 * z_at - 8,
        ]
    ).astype(jnp.int32)
    cond = as_rows(conductivity)
    fwd = as_rows(forward_states)
    prior_own = prior_conductance.reshape(PRIOR, 128)
    field, small = shape(ROWS, 128), shape(8, 128)

    code = call(encode, jax.ShapeDtypeStruct((32, 128), jnp.int32), [VM, VM])(
        sensor_cell.reshape(32, 128), sensor_window.reshape(32, 128)
    ).reshape(4096)
    xs, zs = shape(2 * XR + PRIOR, 128), shape(2 * ZR, 128)
    sources, xa, xb, za, zb = call(
        scatter, (shape(STEPS * ROWS, 128), xs, xs, zs, zs), [SM, SM, SM, VM, VM], flops=4 * 10**7
    )(info, code, sensor_misfit, cond, prior_own)
    rx, rz = swap((xa, xb), "strip"), swap((za, zb), "depth")
    table = call(
        faces, (shape(ROWS + ZR, 128),) + (field,) * 5, [SM] + [VM] * 5, [EXT, SIDE]
    )(info, cond, *rx, *rz)
    prior_x = rx

    forcing = sources
    known = acc = waiting = None
    for n in reversed(range(STEPS)):
        first = n == STEPS - 1
        xs, zs = shape(2 * XR + 8, 128), shape(2 * ZR + (144 if first else 0), 128)
        v, known, xa, xb, za, zb = call(
            functools.partial(first_sweep, n),
            (field, small, xs, xs, zs, zs),
            [SM] + [VM] * 13,
            [EXT, SIDE],
        )(info, forcing, fwd, prior_own if first else known, *table, *rx, *rz)
        rx, rz = swap((xa, xb), "strip"), swap((za, zb), "depth")
        if first:
            span = shape(SPAN, WIN, 128)
            *prior, peak = call(
                prior_setup, (span, span, span, span, small), [SM] + [VM] * 5, [pltpu.VMEM((3, SPAN, WIN, 128), F32)]
            )(info, prior_own, *prior_x, *rz)
        if waiting is not None:
            acc = waiting()
        forward_x, forward_z = rx, rz
        fields = 2 if n else 1
        xs, zs = shape(fields * XR + 8, 128), shape(fields * ZR, 128)
        adjoint, after, known, xa, xb, za, zb = call(
            functools.partial(second_sweep, n),
            (field, field if n else small, small, xs, xs, zs, zs),
            [SM] + [VM] * 3 + ([] if first else [VM, ANY]) + [VM] * 10,
            [EXT, SIDE],
        )(info, v, forcing, sources, *([] if first else [known, acc]), *table, *rx, *rz)
        rx, rz = swap((xa, xb), "strip"), swap((za, zb), "depth")

        def waiting(n=n, adjoint=adjoint, acc=acc, halos=(*rx, *rz, *forward_x, *forward_z)):
            return call(
                functools.partial(gradient, n),
                field,
                [SM] + [VM] * (10 if acc is None else 11),
                [EXT, EXT, SIDE, SIDE],
            )(info, adjoint, fwd, *([] if acc is None else [acc]), *halos)

        if first:
            known = peak
        forcing = after
    acc = waiting()

    pieces, _ = call(
        coarsen,
        (shape(z_n, WIN + 8, 2 * CZ), small),
        [VM] * 5,
        [SIDE, pltpu.VMEM((2 * CZ, NY), F32), pltpu.VMEM((400, 2 * CZ), F32)],
    )(acc, cond, known, *rx)
    pieces = lax.all_to_all(pieces, "depth", 0, 0)
    window, coarse_grad, upper = call(
        assemble, (shape(2 * WIN, 128), shape(2, 48, 128), shape(8, 2 * CZ)), [VM]
    )(pieces)

    own, both = shape(2, 48, 128), shape(2, WIN, 128)
    sides = swap((window, window), "strip")
    x, r, d, sa, sb = call(
        cheb_one, (own, both, both, shape(3 * WIN, 128), shape(3 * WIN, 128)), [SM] + [VM] * 8
    )(info, upper, window, *sides, *prior)
    sides = swap((sa, sb), "strip")
    x, r, d, sa, sb = call(
        cheb_mid, (own, both, both, shape(WIN, 128), shape(WIN, 128)), [SM] + [VM] * 10
    )(info, upper, x, r, d, *sides, *prior)
    sides = swap((sa, sb), "strip")
    step = call(cheb_last, own, [SM] + [VM] * 10)(info, upper, x, r, d, *sides, *prior)
    return coarse_grad, step


def solution(mesh):
    placed = (
        P("depth", "strip", None),
        P(None, "depth", "strip", None),
        P(("depth", "strip")),
        P(("depth", "strip")),
        P(("depth", "strip")),
        P(None, "strip", "depth", None),
    )
    return jax.shard_map(
        on_device,
        mesh=mesh,
        in_specs=placed,
        out_specs=(P("strip", "depth", None), P("strip", "depth", None)),
        check_vma=False,
    )
```

```python
import functools

import jax
import jax.numpy as jnp
from jax import lax
from jax.experimental import pallas as pl
from jax.experimental.pallas import tpu as pltpu
from jax.sharding import PartitionSpec as P

F32 = jnp.float32
STEPS = 5
CHEB = 6
CZ, CX, NY = 16, 8, 1536
TILES = NY // 128
ZR = TILES * CX
XR = TILES * CZ
ROWS = CZ * ZR
OWN = 8 + ZR
WIN = 64
SPAN = 6
PRIOR = 288
SHIFT = 0.5
EXACT = lax.Precision.HIGHEST

VM = pl.BlockSpec(memory_space=pltpu.VMEM)
SM = pl.BlockSpec(memory_space=pltpu.SMEM)
ANY = pl.BlockSpec(memory_space=pl.ANY)
HBM = pl.BlockSpec(memory_space=pltpu.HBM)


def shape(*dims):
    return jax.ShapeDtypeStruct(dims, F32)


def call(body, outs, ins, scratch=(), limit=6, flops=4 * 10**6, traffic=5 * 10**6):
    return pl.pallas_call(
        body,
        out_shape=outs,
        in_specs=ins,
        out_specs=jax.tree.map(lambda _: VM, outs),
        scratch_shapes=list(scratch),
        compiler_params=pltpu.CompilerParams(vmem_limit_bytes=limit * 2**20),
        cost_estimate=pl.CostEstimate(flops=flops, bytes_accessed=traffic, transcendentals=0),
    )


def pairs_a(n):
    return [(i, i ^ 1) for i in range(n)]


def pairs_b(n):
    return [(i, (((i + 1) ^ 1) - 1) % n) for i in range(n)]


def swap(send, axis):
    n = lax.axis_size(axis)
    return lax.ppermute(send[0], axis, pairs_a(n)), lax.ppermute(send[1], axis, pairs_b(n))


def to_sides(info, k, first, second):
    odd = info[k] == 1
    below = jnp.where(info[2 + 2 * k] == 1, jnp.where(odd, first, second), 0.0)
    above = jnp.where(info[3 + 2 * k] == 1, jnp.where(odd, second, first), 0.0)
    return below, above


def from_sides(info, k, below, above):
    odd = info[k] == 1
    return jnp.where(odd, below, above), jnp.where(odd, above, below)


def put_x(info, refs, to, field, base):
    for t in range(TILES):
        low = field[pl.ds(base + t * CX, CZ, stride=ZR), :]
        high = field[pl.ds(base + t * CX + CX - 1, CZ, stride=ZR), :]
        first, second = from_sides(info, 0, low, high)
        refs[0][to + t * CZ : to + (t + 1) * CZ, :] = first
        refs[1][to + t * CZ : to + (t + 1) * CZ, :] = second


def put_z(info, refs, to, field, base):
    first, second = from_sides(info, 1, field[base : base + ZR, :], field[base + ROWS - ZR : base + ROWS, :])
    refs[0][to : to + ZR, :] = first
    refs[1][to : to + ZR, :] = second


def load_sides(info, rx, base, side):
    side[...] = jnp.zeros_like(side)
    for t in range(TILES):
        at = base + t * CZ
        low, high = to_sides(info, 0, rx[0][at : at + CZ, :], rx[1][at : at + CZ, :])
        side[pl.ds(t * CX, CZ, stride=ZR), :] = low
        side[pl.ds(t * CX + CX - 1, CZ, stride=ZR), :] = high


def load_ext(info, field, base, rz, at, ext):
    ext[OWN : OWN + ROWS, :] = field[base : base + ROWS, :]
    load_layers(info, rz, at, ext)


def load_layers(info, rz, at, ext):
    low, high = to_sides(info, 1, rz[0][at : at + ZR, :], rz[1][at : at + ZR, :])
    ext[OWN - ZR : OWN, :] = low
    ext[OWN + ROWS : OWN + ROWS + ZR, :] = high


def pass_peak(mine, rx, at, sends, to, out):
    best = jnp.zeros((8, 128), F32) if mine is None else mine[...]
    if at is not None:
        best = jnp.maximum(best, jnp.maximum(rx[0][at : at + 8, :], rx[1][at : at + 8, :]))
    out[...] = best
    if sends is not None:
        for send in sends:
            send[to : to + 8, :] = best


EXT = pltpu.VMEM((OWN + ROWS + ZR + 8, 128), F32)
SIDE = pltpu.VMEM((ROWS, 128), F32)


def iota(axis):
    return lax.broadcasted_iota(jnp.int32, (CX, 128), axis)


def lanes_up(tiles, lane):
    moved = [pltpu.roll(v, 127, 1) for v in tiles]
    return [jnp.where(lane == 127, moved[(t + 1) % TILES], moved[t]) for t in range(TILES)]


def lanes_down(tiles, lane):
    moved = [pltpu.roll(v, 1, 1) for v in tiles]
    return [jnp.where(lane == 0, moved[t - 1], moved[t]) for t in range(TILES)]


def rows_of(z, t):
    return pl.multiple_of(z * ZR + t * CX, CX)


def tile(ref, row, offset=0):
    return ref[pl.ds(row + offset, CX), :]


def each_layer(body):
    def step(z, carry):
        body(z)
        return carry

    lax.fori_loop(0, CZ, step, 0, unroll=CZ)


GROUP = 4


def encode(cell, window, lines):
    line = lax.shift_right_logical(lax.shift_right_logical(cell, 9) * 171, 9)
    lateral = cell - line * NY
    layer = window * CZ + lax.shift_right_logical(line, 3)
    lines[0:32, :] = (layer * TILES + lax.shift_right_logical(lateral, 7)) * CX
    lines[32:64, :] = (line & (CX - 1)) * 128 + (lateral & 127)


def scatter(info, cell, window, misfit, cond, prior, out, field, xa, xb, za, zb, raw, lines, codes, values, sems):
    tail = pl.ds(2 * XR, PRIOR)
    moves = [
        pltpu.make_async_copy(cell, raw.at[0], sems.at[0]),
        pltpu.make_async_copy(window, raw.at[1], sems.at[1]),
        pltpu.make_async_copy(misfit, values, sems.at[2]),
        pltpu.make_async_copy(cond, field, sems.at[3]),
        pltpu.make_async_copy(prior, xa.at[tail, :], sems.at[4]),
        pltpu.make_async_copy(prior, xb.at[tail, :], sems.at[5]),
    ]
    for move in moves:
        move.start()
    out[...] = jnp.zeros_like(out)
    moves[0].wait()
    moves[1].wait()
    encode(raw[0], raw[1], lines)
    to_scalars = pltpu.make_async_copy(lines, codes, sems.at[6])
    to_scalars.start()
    to_scalars.wait()
    moves[2].wait()
    place = iota(0) * 128 + iota(1)

    def step(i, carry):
        row = lax.shift_right_logical(i, 5)
        spots = [(i & 31) * GROUP + k for k in range(GROUP)]
        at = [pl.multiple_of(codes[row, j], CX) for j in spots]
        adds = [jnp.where(place == codes[32 + row, j], values[row, j], 0.0) for j in spots]
        sums = [tile(out, a) for a in at]
        for k in range(GROUP):
            total = sums[k] + adds[k]
            for j in range(k):
                total = total + jnp.where(at[j] == at[k], adds[j], 0.0)
            out[pl.ds(at[k], CX), :] = total
        return carry

    lax.fori_loop(0, 4096 // GROUP, step, 0, unroll=8)
    for move in moves[3:]:
        move.wait()
    base = (STEPS - 1) * ROWS
    put_x(info, (xa, xb), 0, out, base)
    put_x(info, (xa, xb), XR, field, 0)
    put_z(info, (za, zb), 0, out, base)
    put_z(info, (za, zb), ZR, field, 0)


def faces(info, cond, rxa, rxb, rza, rzb, fz, fy, fx, fxb, inv, ext, side):
    load_ext(info, cond, 0, (rza, rzb), ZR, ext)
    load_sides(info, (rxa, rxb), XR, side)
    sub, lane = iota(0), iota(1)

    def layer(z):
        rows = [rows_of(z, t) for t in range(TILES)]
        cs = [tile(ext, r, OWN) for r in rows]
        ups = lanes_up(cs, lane)
        ups[-1] = jnp.where(lane == 127, 0.0, ups[-1])
        y_hi = [0.5 * (c + u) for c, u in zip(cs, ups)]
        y_lo = lanes_down(y_hi, lane)
        y_lo[0] = jnp.where(lane == 0, 0.5 * cs[0], y_lo[0])
        for t, r in enumerate(rows):
            c = cs[t]
            here = pl.ds(r, CX)
            beside = tile(side, r)
            z_lo = 0.5 * (c + tile(ext, r, OWN - ZR))
            z_hi = 0.5 * (c + tile(ext, r, OWN + ZR))
            x_hi = 0.5 * (c + jnp.where(sub == CX - 1, beside, tile(ext, r, OWN + 1)))
            x_lo = 0.5 * (c + jnp.where(sub == 0, beside, tile(ext, r, OWN - 1)))
            fz[here, :] = z_lo
            fz[pl.ds(r + ZR, CX), :] = z_hi
            fy[here, :] = jnp.where(lane == 127, 0.0, y_hi[t]) if t == TILES - 1 else y_hi[t]
            fx[here, :] = jnp.where(sub == CX - 1, 0.0, x_hi)
            fxb[here, :] = jnp.where(sub == CX - 1, x_hi, jnp.where(sub == 0, x_lo, 0.0))
            inv[here, :] = 1.0 / (1.0 + (((((z_hi + z_lo) + x_hi) + x_lo) + y_hi[t]) + y_lo[t]))

    each_layer(layer)


def sweep(right, base, fz, fy, fx, fxb, inv, ext, side, lane, z):
    rows = [rows_of(z, t) for t in range(TILES)]
    vs = [tile(ext, r, OWN) for r in rows]
    ys = [tile(fy, r) for r in rows]
    ups = lanes_up(vs, lane)
    downs = lanes_down([y * v for y, v in zip(ys, vs)], lane)
    new = []
    for t, r in enumerate(rows):
        spread = tile(fz, r, ZR) * tile(ext, r, OWN + ZR) + tile(fz, r) * tile(ext, r, OWN - ZR)
        x_face = tile(fx, r)
        spread = spread + (x_face * pltpu.roll(vs[t], CX - 1, 0) + pltpu.roll(x_face * vs[t], 1, 0))
        spread = spread + tile(fxb, r) * tile(side, r)
        spread = spread + (ys[t] * ups[t] + downs[t])
        new.append((tile(right, r, base) + spread) * tile(inv, r))
    return rows, new


def prior_columns(info, k, prior, rx):
    columns = {}
    for p in range(2):
        at = (2 * k + p) * 48
        columns[2 + p] = prior[at : at + 48, :]
        at = at + 2 * XR
        columns[p], columns[4 + p] = to_sides(info, 0, rx[0][at : at + 48, :], rx[1][at : at + 48, :])
    return [columns[j] for j in range(SPAN)]


def first_sweep(n, info, forcing, fwd, prior, *refs):
    first = n == STEPS - 1
    fz, fy, fx, fxb, inv, rxa, rxb, rza, rzb, out, known, xa, xb, za, zb, ext, side, states, sem = refs
    move = pltpu.make_async_copy(fwd.at[pl.ds(n * ROWS, ROWS), :], states, sem)
    move.start()
    peak = None if first else prior
    base = (STEPS - 1) * ROWS if first else 0
    pass_peak(peak, (rxa, rxb), None if first else 2 * XR, (xa, xb), 2 * XR, known)
    load_ext(info, forcing, base, (rza, rzb), 0 if first else ZR, ext)
    load_sides(info, (rxa, rxb), 0 if first else XR, side)
    lane = iota(1)

    def layer(z):
        rows, new = sweep(forcing, base, fz, fy, fx, fxb, inv, ext, side, lane, z)
        for r, v in zip(rows, new):
            out[pl.ds(r, CX), :] = v

    each_layer(layer)
    put_x(info, (xa, xb), 0, out, 0)
    put_z(info, (za, zb), 0, out, 0)
    move.wait()
    put_x(info, (xa, xb), XR, states, 0)
    put_z(info, (za, zb), ZR, states, 0)
    if first:
        for k in range(3):
            columns = prior_columns(info, k, prior, (rxa, rxb))
            for j, column in enumerate(columns):
                at = 2 * ZR + (k * SPAN + j) * 8
                za[at : at + 8, :], zb[at : at + 8, :] = from_sides(info, 1, column[:8], column[40:])


def second_sweep(n, info, v, forcing, source, *refs):
    if n == STEPS - 1:
        peak = None
    else:
        peak, earlier, *refs = refs
    fz, fy, fx, fxb, inv, rxa, rxb, rza, rzb, out, after, known, xa, xb, za, zb, ext, side = refs
    base = (STEPS - 1) * ROWS if n == STEPS - 1 else 0
    pass_peak(peak, (rxa, rxb), 2 * XR, (xa, xb), 2 * XR if n else XR, known)
    load_ext(info, v, 0, (rza, rzb), 0, ext)
    load_sides(info, (rxa, rxb), 0, side)
    lane = iota(1)

    def layer(z):
        rows, new = sweep(forcing, base, fz, fy, fx, fxb, inv, ext, side, lane, z)
        for r, v in zip(rows, new):
            out[pl.ds(r, CX), :] = v
            if n:
                after[pl.ds(r, CX), :] = v + tile(source, r, (n - 1) * ROWS)

    each_layer(layer)
    put_x(info, (xa, xb), 0, out, 0)
    put_z(info, (za, zb), 0, out, 0)
    if n:
        put_x(info, (xa, xb), XR, after, 0)
        put_z(info, (za, zb), ZR, after, 0)


def gradient(n, info, a_ref, f_ref, *refs):
    acc = None
    if n < STEPS - 1:
        acc, *refs = refs
    rxa, rxb, rza, rzb, fxa, fxb, fza, fzb, out, a_ext, f_ext, a_side, f_side, sem = refs
    move = pltpu.make_async_copy(f_ref.at[pl.ds(n * ROWS, ROWS), :], f_ext.at[pl.ds(OWN, ROWS), :], sem)
    move.start()
    load_ext(info, a_ref, 0, (rza, rzb), 0, a_ext)
    load_sides(info, (rxa, rxb), 0, a_side)
    load_layers(info, (fza, fzb), ZR, f_ext)
    load_sides(info, (fxa, fxb), XR, f_side)
    move.wait()
    sub, lane = iota(0), iota(1)

    def layer(z):
        rows = [rows_of(z, t) for t in range(TILES)]
        a_s = [tile(a_ext, r, OWN) for r in rows]
        f_s = [tile(f_ext, r, OWN) for r in rows]
        a_up, f_up = lanes_up(a_s, lane), lanes_up(f_s, lane)
        a_up[-1] = jnp.where(lane == 127, 0.0, a_up[-1])
        f_up[-1] = jnp.where(lane == 127, 0.0, f_up[-1])
        y_hi = [(a - au) * (f - fu) for a, au, f, fu in zip(a_s, a_up, f_s, f_up)]
        y_lo = lanes_down(y_hi, lane)
        y_lo[0] = jnp.where(lane == 0, a_s[0] * f_s[0], y_lo[0])
        for t, r in enumerate(rows):
            a, f = a_s[t], f_s[t]
            total = y_hi[t] + y_lo[t]
            for step in (ZR, -ZR):
                total = total + (a - tile(a_ext, r, OWN + step)) * (f - tile(f_ext, r, OWN + step))
            for step, edge in ((1, CX - 1), (-1, 0)):
                a_by = jnp.where(sub == edge, tile(a_side, r), tile(a_ext, r, OWN + step))
                f_by = jnp.where(sub == edge, tile(f_side, r), tile(f_ext, r, OWN + step))
                total = total + (a - a_by) * (f - f_by)
            out[pl.ds(r, CX), :] = total if acc is None else tile(acc, r) + total

    each_layer(layer)


def coarsen(acc, cond, peak, rxa, rxb, out, known, fine, rows, tall):
    pass_peak(peak, (rxa, rxb), XR, None, None, known)
    fine[...] = -0.5 * cond[...] * acc[...]
    for t in range(TILES):
        for p in range(2):
            total = None
            for x in range(4):
                part = fine[pl.ds(t * CX + 4 * p + x, CZ, stride=ZR), :]
                total = part if total is None else total + part
            rows[p * CZ : (p + 1) * CZ, t * 128 : (t + 1) * 128] = total
    group = lax.broadcasted_iota(jnp.int32, (128, 512), 1) // 4
    pick = jnp.where(group == lax.broadcasted_iota(jnp.int32, (128, 512), 0), 1.0, 0.0)
    tall[...] = jnp.zeros_like(tall)
    for k in range(3):
        tall[8 + 128 * k : 8 + 128 * (k + 1), :] = lax.dot_general(
            pick,
            rows[:, 512 * k : 512 * (k + 1)],
            (((1,), (1,)), ((), ())),
            precision=EXACT,
            preferred_element_type=F32,
        )
    for d in range(out.shape[0]):
        out[d, 0:WIN] = tall[48 * d : 48 * d + WIN, :]
        out[d, WIN : WIN + 8] = known[:, : 2 * CZ]


def assemble(pieces, window, coarse, upper):
    best = pieces[0, WIN : WIN + 8]
    for d in range(1, pieces.shape[0]):
        best = jnp.maximum(best, pieces[d, WIN : WIN + 8])
    upper[...] = best
    k = lax.broadcasted_iota(jnp.int32, (2 * CZ, 128), 0)
    z = lax.broadcasted_iota(jnp.int32, (2 * CZ, 128), 1)
    for p in range(2):
        total = jnp.zeros((WIN, 128), F32)
        for d in range(pieces.shape[0]):
            own = (z >= CZ * d) & (z < CZ * (d + 1)) & (k - CZ * p == z - CZ * d)
            total = total + jnp.dot(
                pieces[d, 0:WIN], jnp.where(own, 1.0, 0.0), precision=EXACT, preferred_element_type=F32
            )
        window[p * WIN : (p + 1) * WIN, :] = total
        coarse[p] = total[8:56]


def prior_setup(info, own, rxa, rxb, rza, rzb, fx, fy, fz, diag, peak, w):
    first_column, first_row = info[6], info[7]
    for k in range(3):
        for j, column in enumerate(prior_columns(info, k, own, (rxa, rxb))):
            at = 2 * ZR + (k * SPAN + j) * 8
            low, high = to_sides(info, 1, rza[at : at + 8, :], rzb[at : at + 8, :])
            w[k, j, 0:8] = low
            w[k, j, 8:56] = column
            w[k, j, 56:64] = high
    row = lax.broadcasted_iota(jnp.int32, (WIN, 128), 0)
    lane = lax.broadcasted_iota(jnp.int32, (WIN, 128), 1)
    y_in = (row + first_row >= 0) & (row + first_row < 384)
    y_link = y_in & (row + first_row + 1 >= 0) & (row + first_row + 1 < 384) & (row < WIN - 1)

    def x_in(j):
        return (first_column + j >= 0) & (first_column + j < 32)

    def wx(j):
        if j < 0 or j >= SPAN:
            return jnp.zeros((WIN, 128), F32)
        return jnp.where(x_in(j) & y_in, w[0, j], 0.0)

    best = None
    for j in range(SPAN):
        inside = x_in(j) & y_in
        here = wx(j)
        x_hi = 0.5 * (here + wx(j + 1))
        x_lo = 0.5 * (here + wx(j - 1))
        v = jnp.where(inside, w[1, j], 0.0)
        y_hi = 0.5 * (v + jnp.where(row == WIN - 1, 0.0, pltpu.roll(v, WIN - 1, 0)))
        y_lo = jnp.where(row == 0, 0.5 * v, pltpu.roll(y_hi, 1, 0))
        v = jnp.where(inside, w[2, j], 0.0)
        z_hi = 0.5 * (v + jnp.where(lane == 127, 0.0, pltpu.roll(v, 127, 1)))
        z_lo = jnp.where(lane == 0, 0.5 * v, pltpu.roll(z_hi, 1, 1))
        total = ((((x_hi + x_lo) + y_hi) + y_lo) + z_hi) + z_lo
        diag[j] = SHIFT + total
        fx[j] = jnp.where(inside & x_in(j + 1), x_hi, 0.0) if j + 1 < SPAN else jnp.zeros_like(x_hi)
        fy[j] = jnp.where(x_in(j) & y_link, y_hi, 0.0)
        fz[j] = jnp.where(inside & (lane < 127), z_hi, 0.0)
        if j in (2, 3):
            bound = jnp.max((SHIFT + 2.0 * total)[8:56].reshape(6, 8, 128), axis=0)
            best = bound if best is None else jnp.maximum(best, bound)
    peak[...] = jnp.full((8, 128), jnp.max(best))


def coefficients(upper):
    top = upper[0:1, 0:1]
    centre = 0.5 * (top + SHIFT)
    half = 0.5 * (top - SHIFT)
    sigma = centre / half
    rho = 1.0 / sigma
    scales = []
    for _ in range(CHEB - 1):
        rho_new = 1.0 / (2.0 * sigma - rho)
        scales.append((rho_new * rho, 2.0 * rho_new / half))
        rho = rho_new
    return centre, scales


def cheb_column(j, scale, r, d, prior):
    fx, fy, fz, diag = prior
    v = d[j]
    y_face, z_face = fy[j], fz[j]
    pull = fx[j] * d[j + 1] + fx[j - 1] * d[j - 1]
    pull = pull + y_face * pltpu.roll(v, WIN - 1, 0) + pltpu.roll(y_face * v, 1, 0)
    pull = pull + z_face * pltpu.roll(v, 127, 1) + pltpu.roll(z_face * v, 1, 1)
    left = r[j] - (diag[j] * v - pull)
    return left, scale[0] * v + scale[1] * left


def block(ref, k):
    return ref[k * WIN : (k + 1) * WIN, :]


def cheb_send(info, d, r, sa, sb):
    for k, (low, high) in enumerate(((d[2], d[2]), (d[3], d[3]), (r[2], r[3]))):
        one, two = from_sides(info, 0, low, high)
        sa[k * WIN : (k + 1) * WIN, :] = one
        sb[k * WIN : (k + 1) * WIN, :] = two


def cheb_two(first, r, d, scales, prior):
    r, d = dict(r), dict(d)
    sums = []
    for it in range(2):
        fresh = {}
        for j in range(1 + it, SPAN - 1 - it):
            r[j], fresh[j] = cheb_column(j, scales[first + it], r, d, prior)
        d = fresh
        sums.append((d[2], d[3]))
    return r, d, sums


def cheb_one(info, upper, g, ra, rb, fx, fy, fz, diag, out, r_out, d_out, sa, sb):
    centre, scales = coefficients(upper)
    r = {2: block(g, 0), 3: block(g, 1)}
    for k in range(2):
        r[k], r[4 + k] = to_sides(info, 0, block(ra, k), block(rb, k))
    d = {j: v / centre for j, v in r.items()}
    start = (d[2], d[3])
    r, d, sums = cheb_two(0, r, d, scales, (fx, fy, fz, diag))
    for p in range(2):
        out[p] = ((start[p] + sums[0][p]) + sums[1][p])[8:56]
        r_out[p], d_out[p] = r[2 + p], d[2 + p]
    cheb_send(info, d, r, sa, sb)


def cheb_mid(info, upper, x, r_in, d_in, ra, rb, fx, fy, fz, diag, out, r_out, d_out, sa, sb):
    _, scales = coefficients(upper)
    r, d = {2: r_in[0], 3: r_in[1]}, {2: d_in[0], 3: d_in[1]}
    for k in range(2):
        d[k], d[4 + k] = to_sides(info, 0, block(ra, k), block(rb, k))
    r[1], r[4] = to_sides(info, 0, block(ra, 2), block(rb, 2))
    r, d, sums = cheb_two(2, r, d, scales, (fx, fy, fz, diag))
    for p in range(2):
        out[p] = (x[p] + sums[0][p][8:56]) + sums[1][p][8:56]
        r_out[p], d_out[p] = r[2 + p], d[2 + p]
    one, two = from_sides(info, 0, d[2], d[3])
    sa[...] = one
    sb[...] = two


def cheb_last(info, upper, x, r_in, d_in, ra, rb, fx, fy, fz, diag, out):
    _, scales = coefficients(upper)
    r, d = {2: r_in[0], 3: r_in[1]}, {2: d_in[0], 3: d_in[1]}
    d[1], d[4] = to_sides(info, 0, ra[...], rb[...])
    for p in range(2):
        _, new = cheb_column(2 + p, scales[4], r, d, (fx, fy, fz, diag))
        out[p] = x[p] + new[8:56]


def as_rows(field):
    lead = field.shape[:-2]
    return jnp.swapaxes(field.reshape(*lead, CX, TILES, 128), -3, -2).reshape(-1, 128)


def on_device(
    conductivity, forward_states, sensor_cell, sensor_window, sensor_misfit, prior_conductance
):
    z_at, x_at = lax.axis_index("depth"), lax.axis_index("strip")
    z_n, x_n = lax.axis_size("depth"), lax.axis_size("strip")
    info = jnp.stack(
        [
            x_at % 2,
            z_at % 2,
            (x_at > 0).astype(jnp.int32),
            (x_at < x_n - 1).astype(jnp.int32),
            (z_at > 0).astype(jnp.int32),
            (z_at < z_n - 1).astype(jnp.int32),
            2 * x_at - 2,
            48 * z_at - 8,
        ]
    ).astype(jnp.int32)
    fwd = as_rows(forward_states)
    prior_own = prior_conductance.reshape(PRIOR, 128)
    field, small = shape(ROWS, 128), shape(8, 128)

    xs, zs = shape(2 * XR + PRIOR, 128), shape(2 * ZR, 128)
    sources, cond, xa, xb, za, zb = call(
        scatter,
        (shape(STEPS * ROWS, 128), field, xs, xs, zs, zs),
        [SM] + [HBM] * 5,
        [
            pltpu.VMEM((2, 32, 128), jnp.int32),
            pltpu.VMEM((64, 128), jnp.int32),
            pltpu.SMEM((64, 128), jnp.int32),
            pltpu.SMEM((32, 128), F32),
            pltpu.SemaphoreType.DMA((7,)),
        ],
        flops=4 * 10**7,
    )(
        info,
        sensor_cell.reshape(32, 128),
        sensor_window.reshape(32, 128),
        sensor_misfit.reshape(32, 128),
        as_rows(conductivity),
        prior_own,
    )
    rx, rz = swap((xa, xb), "strip"), swap((za, zb), "depth")
    table = call(
        faces, (shape(ROWS + ZR, 128),) + (field,) * 4, [SM] + [VM] * 5, [EXT, SIDE]
    )(info, cond, *rx, *rz)
    prior_x = rx

    forcing = sources
    known = acc = waiting = None
    for n in reversed(range(STEPS)):
        first = n == STEPS - 1
        xs, zs = shape(2 * XR + 8, 128), shape(2 * ZR + (144 if first else 0), 128)
        v, known, xa, xb, za, zb = call(
            functools.partial(first_sweep, n),
            (field, small, xs, xs, zs, zs),
            [SM, VM, HBM] + [VM] * 10,
            [EXT, SIDE, SIDE, pltpu.SemaphoreType.DMA],
        )(info, forcing, fwd, prior_own if first else known, *table, *rx, *rz)
        rx, rz = swap((xa, xb), "strip"), swap((za, zb), "depth")
        if first:
            span = shape(SPAN, WIN, 128)
            *prior, peak = call(
                prior_setup, (span, span, span, span, small), [SM] + [VM] * 5, [pltpu.VMEM((3, SPAN, WIN, 128), F32)]
            )(info, prior_own, *prior_x, *rz)
        if waiting is not None:
            acc = waiting()
        forward_x, forward_z = rx, rz
        fields = 2 if n else 1
        xs, zs = shape(fields * XR + 8, 128), shape(fields * ZR, 128)
        adjoint, after, known, xa, xb, za, zb = call(
            functools.partial(second_sweep, n),
            (field, field if n else small, small, xs, xs, zs, zs),
            [SM] + [VM] * 3 + ([] if first else [VM, ANY]) + [VM] * 9,
            [EXT, SIDE],
        )(info, v, forcing, sources, *([] if first else [known, acc]), *table, *rx, *rz)
        rx, rz = swap((xa, xb), "strip"), swap((za, zb), "depth")

        def waiting(n=n, adjoint=adjoint, acc=acc, halos=(*rx, *rz, *forward_x, *forward_z)):
            return call(
                functools.partial(gradient, n),
                field,
                [SM, VM, HBM] + [VM] * (8 if acc is None else 9),
                [EXT, EXT, SIDE, SIDE, pltpu.SemaphoreType.DMA],
            )(info, adjoint, fwd, *([] if acc is None else [acc]), *halos)

        if first:
            known = peak
        forcing = after
    acc = waiting()

    pieces, _ = call(
        coarsen,
        (shape(z_n, WIN + 8, 2 * CZ), small),
        [VM] * 5,
        [SIDE, pltpu.VMEM((2 * CZ, NY), F32), pltpu.VMEM((400, 2 * CZ), F32)],
    )(acc, cond, known, *rx)
    pieces = lax.all_to_all(pieces, "depth", 0, 0)
    window, coarse_grad, upper = call(
        assemble, (shape(2 * WIN, 128), shape(2, 48, 128), shape(8, 2 * CZ)), [VM]
    )(pieces)

    own, both = shape(2, 48, 128), shape(2, WIN, 128)
    sides = swap((window, window), "strip")
    x, r, d, sa, sb = call(
        cheb_one, (own, both, both, shape(3 * WIN, 128), shape(3 * WIN, 128)), [SM] + [VM] * 8
    )(info, upper, window, *sides, *prior)
    sides = swap((sa, sb), "strip")
    x, r, d, sa, sb = call(
        cheb_mid, (own, both, both, shape(WIN, 128), shape(WIN, 128)), [SM] + [VM] * 10
    )(info, upper, x, r, d, *sides, *prior)
    sides = swap((sa, sb), "strip")
    step = call(cheb_last, own, [SM] + [VM] * 10)(info, upper, x, r, d, *sides, *prior)
    return coarse_grad, step


def solution(mesh):
    placed = (
        P("depth", "strip", None),
        P(None, "depth", "strip", None),
        P(("depth", "strip")),
        P(("depth", "strip")),
        P(("depth", "strip")),
        P(None, "strip", "depth", None),
    )
    return jax.shard_map(
        on_device,
        mesh=mesh,
        in_specs=placed,
        out_specs=(P("strip", "depth", None), P("strip", "depth", None)),
        check_vma=False,
    )
```

```python
import functools

import jax
import jax.numpy as jnp
from jax import lax
from jax.experimental import pallas as pl
from jax.experimental.pallas import tpu as pltpu
from jax.sharding import PartitionSpec as P

F32 = jnp.float32
STEPS = 5
CHEB = 6
CZ, CX, NY = 16, 8, 1536
TILES = NY // 128
ZR = TILES * CX
XR = TILES * CZ
ROWS = CZ * ZR
OWN = 8 + ZR
WIN = 64
SPAN = 6
PRIOR = 288
SHIFT = 0.5
EXACT = lax.Precision.HIGHEST

VM = pl.BlockSpec(memory_space=pltpu.VMEM)
SM = pl.BlockSpec(memory_space=pltpu.SMEM)
ANY = pl.BlockSpec(memory_space=pl.ANY)


def shape(*dims):
    return jax.ShapeDtypeStruct(dims, F32)


def call(body, outs, ins, scratch=(), limit=6, flops=4 * 10**6, traffic=5 * 10**6):
    return pl.pallas_call(
        body,
        out_shape=outs,
        in_specs=ins,
        out_specs=jax.tree.map(lambda _: VM, outs),
        scratch_shapes=list(scratch),
        compiler_params=pltpu.CompilerParams(vmem_limit_bytes=limit * 2**20),
        cost_estimate=pl.CostEstimate(flops=flops, bytes_accessed=traffic, transcendentals=0),
    )


def pairs_a(n):
    return [(i, i ^ 1) for i in range(n)]


def pairs_b(n):
    return [(i, (((i + 1) ^ 1) - 1) % n) for i in range(n)]


def swap(send, axis):
    n = lax.axis_size(axis)
    return lax.ppermute(send[0], axis, pairs_a(n)), lax.ppermute(send[1], axis, pairs_b(n))


def to_sides(info, k, first, second):
    odd = info[k] == 1
    below = jnp.where(info[2 + 2 * k] == 1, jnp.where(odd, first, second), 0.0)
    above = jnp.where(info[3 + 2 * k] == 1, jnp.where(odd, second, first), 0.0)
    return below, above


def from_sides(info, k, below, above):
    odd = info[k] == 1
    return jnp.where(odd, below, above), jnp.where(odd, above, below)


def put_x(info, refs, to, field, base):
    for t in range(TILES):
        low = field[pl.ds(base + t * CX, CZ, stride=ZR), :]
        high = field[pl.ds(base + t * CX + CX - 1, CZ, stride=ZR), :]
        first, second = from_sides(info, 0, low, high)
        refs[0][to + t * CZ : to + (t + 1) * CZ, :] = first
        refs[1][to + t * CZ : to + (t + 1) * CZ, :] = second


def put_z(info, refs, to, field, base):
    first, second = from_sides(info, 1, field[base : base + ZR, :], field[base + ROWS - ZR : base + ROWS, :])
    refs[0][to : to + ZR, :] = first
    refs[1][to : to + ZR, :] = second


def load_sides(info, rx, base, side):
    side[...] = jnp.zeros_like(side)
    for t in range(TILES):
        at = base + t * CZ
        low, high = to_sides(info, 0, rx[0][at : at + CZ, :], rx[1][at : at + CZ, :])
        side[pl.ds(t * CX, CZ, stride=ZR), :] = low
        side[pl.ds(t * CX + CX - 1, CZ, stride=ZR), :] = high


def load_ext(info, field, base, rz, at, ext):
    ext[OWN : OWN + ROWS, :] = field[base : base + ROWS, :]
    low, high = to_sides(info, 1, rz[0][at : at + ZR, :], rz[1][at : at + ZR, :])
    ext[OWN - ZR : OWN, :] = low
    ext[OWN + ROWS : OWN + ROWS + ZR, :] = high


def pass_peak(mine, rx, at, sends, to, out):
    best = jnp.zeros((8, 128), F32) if mine is None else mine[...]
    if at is not None:
        best = jnp.maximum(best, jnp.maximum(rx[0][at : at + 8, :], rx[1][at : at + 8, :]))
    out[...] = best
    if sends is not None:
        for send in sends:
            send[to : to + 8, :] = best


EXT = pltpu.VMEM((OWN + ROWS + ZR + 8, 128), F32)
SIDE = pltpu.VMEM((ROWS, 128), F32)


def iota(axis):
    return lax.broadcasted_iota(jnp.int32, (CX, 128), axis)


def lanes_up(tiles, lane):
    moved = [pltpu.roll(v, 127, 1) for v in tiles]
    return [jnp.where(lane == 127, moved[(t + 1) % TILES], moved[t]) for t in range(TILES)]


def lanes_down(tiles, lane):
    moved = [pltpu.roll(v, 1, 1) for v in tiles]
    return [jnp.where(lane == 0, moved[t - 1], moved[t]) for t in range(TILES)]


def rows_of(z, t):
    return pl.multiple_of(z * ZR + t * CX, CX)


def tile(ref, row, offset=0):
    return ref[pl.ds(row + offset, CX), :]


def each_layer(body):
    def step(z, carry):
        body(z)
        return carry

    lax.fori_loop(0, CZ, step, 0, unroll=CZ)


GROUP = 4


def encode(cell_ref, window, out):
    cell = cell_ref[...]
    line = lax.shift_right_logical(lax.shift_right_logical(cell, 9) * 171, 9)
    lateral = cell - line * NY
    layer = window[...] * CZ + lax.shift_right_logical(line, 3)
    out[0:32, :] = (layer * TILES + lax.shift_right_logical(lateral, 7)) * CX
    out[32:64, :] = (line & (CX - 1)) * 128 + (lateral & 127)


def scatter(info, code, misfit, cond, prior, out, field, xa, xb, za, zb):
    out[...] = jnp.zeros_like(out)
    count = misfit.shape[0]
    place = iota(0) * 128 + iota(1)

    def step(i, carry):
        spots = [i * GROUP + k for k in range(GROUP)]
        at = [pl.multiple_of(code[j], CX) for j in spots]
        adds = [jnp.where(place == code[count + j], misfit[j], 0.0) for j in spots]
        sums = [tile(out, a) for a in at]
        for k in range(GROUP):
            total = sums[k] + adds[k]
            for j in range(k):
                total = total + jnp.where(at[j] == at[k], adds[j], 0.0)
            out[pl.ds(at[k], CX), :] = total
        return carry

    lax.fori_loop(0, count // GROUP, step, 0, unroll=8)
    field[...] = cond[...]
    xa[2 * XR :, :] = prior[...]
    xb[2 * XR :, :] = prior[...]
    base = (STEPS - 1) * ROWS
    put_x(info, (xa, xb), 0, out, base)
    put_x(info, (xa, xb), XR, field, 0)
    put_z(info, (za, zb), 0, out, base)
    put_z(info, (za, zb), ZR, field, 0)


def faces(info, cond, rxa, rxb, rza, rzb, fz, fy, fx, fxb, inv, ext, side):
    load_ext(info, cond, 0, (rza, rzb), ZR, ext)
    load_sides(info, (rxa, rxb), XR, side)
    sub, lane = iota(0), iota(1)

    def layer(z):
        rows = [rows_of(z, t) for t in range(TILES)]
        cs = [tile(ext, r, OWN) for r in rows]
        ups = lanes_up(cs, lane)
        ups[-1] = jnp.where(lane == 127, 0.0, ups[-1])
        y_hi = [0.5 * (c + u) for c, u in zip(cs, ups)]
        y_lo = lanes_down(y_hi, lane)
        y_lo[0] = jnp.where(lane == 0, 0.5 * cs[0], y_lo[0])
        for t, r in enumerate(rows):
            c = cs[t]
            here = pl.ds(r, CX)
            beside = tile(side, r)
            z_lo = 0.5 * (c + tile(ext, r, OWN - ZR))
            z_hi = 0.5 * (c + tile(ext, r, OWN + ZR))
            x_hi = 0.5 * (c + jnp.where(sub == CX - 1, beside, tile(ext, r, OWN + 1)))
            x_lo = 0.5 * (c + jnp.where(sub == 0, beside, tile(ext, r, OWN - 1)))
            fz[here, :] = z_lo
            fz[pl.ds(r + ZR, CX), :] = z_hi
            fy[here, :] = jnp.where(lane == 127, 0.0, y_hi[t]) if t == TILES - 1 else y_hi[t]
            fx[here, :] = jnp.where(sub == CX - 1, 0.0, x_hi)
            fxb[here, :] = jnp.where(sub == CX - 1, x_hi, jnp.where(sub == 0, x_lo, 0.0))
            inv[here, :] = 1.0 / (1.0 + (((((z_hi + z_lo) + x_hi) + x_lo) + y_hi[t]) + y_lo[t]))

    each_layer(layer)


def sweep(right, base, fz, fy, fx, fxb, inv, ext, side, lane, z):
    rows = [rows_of(z, t) for t in range(TILES)]
    vs = [tile(ext, r, OWN) for r in rows]
    ys = [tile(fy, r) for r in rows]
    ups = lanes_up(vs, lane)
    downs = lanes_down([y * v for y, v in zip(ys, vs)], lane)
    new = []
    for t, r in enumerate(rows):
        spread = tile(fz, r, ZR) * tile(ext, r, OWN + ZR) + tile(fz, r) * tile(ext, r, OWN - ZR)
        x_face = tile(fx, r)
        spread = spread + (x_face * pltpu.roll(vs[t], CX - 1, 0) + pltpu.roll(x_face * vs[t], 1, 0))
        spread = spread + tile(fxb, r) * tile(side, r)
        spread = spread + (ys[t] * ups[t] + downs[t])
        new.append((tile(right, r, base) + spread) * tile(inv, r))
    return rows, new


def prior_columns(info, k, prior, rx):
    columns = {}
    for p in range(2):
        at = (2 * k + p) * 48
        columns[2 + p] = prior[at : at + 48, :]
        at = at + 2 * XR
        columns[p], columns[4 + p] = to_sides(info, 0, rx[0][at : at + 48, :], rx[1][at : at + 48, :])
    return [columns[j] for j in range(SPAN)]


def first_sweep(n, info, forcing, fwd, prior, *refs):
    first = n == STEPS - 1
    fz, fy, fx, fxb, inv, rxa, rxb, rza, rzb, out, known, xa, xb, za, zb, ext, side = refs
    peak = None if first else prior
    base = (STEPS - 1) * ROWS if first else 0
    pass_peak(peak, (rxa, rxb), None if first else 2 * XR, (xa, xb), 2 * XR, known)
    load_ext(info, forcing, base, (rza, rzb), 0 if first else ZR, ext)
    load_sides(info, (rxa, rxb), 0 if first else XR, side)
    lane = iota(1)

    def layer(z):
        rows, new = sweep(forcing, base, fz, fy, fx, fxb, inv, ext, side, lane, z)
        for r, v in zip(rows, new):
            out[pl.ds(r, CX), :] = v

    each_layer(layer)
    put_x(info, (xa, xb), 0, out, 0)
    put_z(info, (za, zb), 0, out, 0)
    put_x(info, (xa, xb), XR, fwd, n * ROWS)
    put_z(info, (za, zb), ZR, fwd, n * ROWS)
    if first:
        for k in range(3):
            columns = prior_columns(info, k, prior, (rxa, rxb))
            for j, column in enumerate(columns):
                at = 2 * ZR + (k * SPAN + j) * 8
                za[at : at + 8, :], zb[at : at + 8, :] = from_sides(info, 1, column[:8], column[40:])


def second_sweep(n, info, v, forcing, source, *refs):
    if n == STEPS - 1:
        peak = None
    else:
        peak, earlier, *refs = refs
    fz, fy, fx, fxb, inv, rxa, rxb, rza, rzb, out, after, known, xa, xb, za, zb, ext, side = refs
    base = (STEPS - 1) * ROWS if n == STEPS - 1 else 0
    pass_peak(peak, (rxa, rxb), 2 * XR, (xa, xb), 2 * XR if n else XR, known)
    load_ext(info, v, 0, (rza, rzb), 0, ext)
    load_sides(info, (rxa, rxb), 0, side)
    lane = iota(1)

    def layer(z):
        rows, new = sweep(forcing, base, fz, fy, fx, fxb, inv, ext, side, lane, z)
        for r, v in zip(rows, new):
            out[pl.ds(r, CX), :] = v
            if n:
                after[pl.ds(r, CX), :] = v + tile(source, r, (n - 1) * ROWS)

    each_layer(layer)
    put_x(info, (xa, xb), 0, out, 0)
    put_z(info, (za, zb), 0, out, 0)
    if n:
        put_x(info, (xa, xb), XR, after, 0)
        put_z(info, (za, zb), ZR, after, 0)


def gradient(n, info, a_ref, f_ref, *refs):
    acc = None
    if n < STEPS - 1:
        acc, *refs = refs
    rxa, rxb, rza, rzb, fxa, fxb, fza, fzb, out, a_ext, f_ext, a_side, f_side = refs
    load_ext(info, a_ref, 0, (rza, rzb), 0, a_ext)
    load_sides(info, (rxa, rxb), 0, a_side)
    load_ext(info, f_ref, n * ROWS, (fza, fzb), ZR, f_ext)
    load_sides(info, (fxa, fxb), XR, f_side)
    sub, lane = iota(0), iota(1)

    def layer(z):
        rows = [rows_of(z, t) for t in range(TILES)]
        a_s = [tile(a_ext, r, OWN) for r in rows]
        f_s = [tile(f_ext, r, OWN) for r in rows]
        a_up, f_up = lanes_up(a_s, lane), lanes_up(f_s, lane)
        a_up[-1] = jnp.where(lane == 127, 0.0, a_up[-1])
        f_up[-1] = jnp.where(lane == 127, 0.0, f_up[-1])
        y_hi = [(a - au) * (f - fu) for a, au, f, fu in zip(a_s, a_up, f_s, f_up)]
        y_lo = lanes_down(y_hi, lane)
        y_lo[0] = jnp.where(lane == 0, a_s[0] * f_s[0], y_lo[0])
        for t, r in enumerate(rows):
            a, f = a_s[t], f_s[t]
            total = y_hi[t] + y_lo[t]
            for step in (ZR, -ZR):
                total = total + (a - tile(a_ext, r, OWN + step)) * (f - tile(f_ext, r, OWN + step))
            for step, edge in ((1, CX - 1), (-1, 0)):
                a_by = jnp.where(sub == edge, tile(a_side, r), tile(a_ext, r, OWN + step))
                f_by = jnp.where(sub == edge, tile(f_side, r), tile(f_ext, r, OWN + step))
                total = total + (a - a_by) * (f - f_by)
            out[pl.ds(r, CX), :] = total if acc is None else tile(acc, r) + total

    each_layer(layer)


def coarsen(acc, cond, peak, rxa, rxb, out, known, fine, rows, tall):
    pass_peak(peak, (rxa, rxb), XR, None, None, known)
    fine[...] = -0.5 * cond[...] * acc[...]
    for t in range(TILES):
        for p in range(2):
            total = None
            for x in range(4):
                part = fine[pl.ds(t * CX + 4 * p + x, CZ, stride=ZR), :]
                total = part if total is None else total + part
            rows[p * CZ : (p + 1) * CZ, t * 128 : (t + 1) * 128] = total
    group = lax.broadcasted_iota(jnp.int32, (128, 512), 1) // 4
    pick = jnp.where(group == lax.broadcasted_iota(jnp.int32, (128, 512), 0), 1.0, 0.0)
    tall[...] = jnp.zeros_like(tall)
    for k in range(3):
        tall[8 + 128 * k : 8 + 128 * (k + 1), :] = lax.dot_general(
            pick,
            rows[:, 512 * k : 512 * (k + 1)],
            (((1,), (1,)), ((), ())),
            precision=EXACT,
            preferred_element_type=F32,
        )
    for d in range(out.shape[0]):
        out[d, 0:WIN] = tall[48 * d : 48 * d + WIN, :]
        out[d, WIN : WIN + 8] = known[:, : 2 * CZ]


def assemble(pieces, window, coarse, upper):
    best = pieces[0, WIN : WIN + 8]
    for d in range(1, pieces.shape[0]):
        best = jnp.maximum(best, pieces[d, WIN : WIN + 8])
    upper[...] = best
    k = lax.broadcasted_iota(jnp.int32, (2 * CZ, 128), 0)
    z = lax.broadcasted_iota(jnp.int32, (2 * CZ, 128), 1)
    for p in range(2):
        total = jnp.zeros((WIN, 128), F32)
        for d in range(pieces.shape[0]):
            own = (z >= CZ * d) & (z < CZ * (d + 1)) & (k - CZ * p == z - CZ * d)
            total = total + jnp.dot(
                pieces[d, 0:WIN], jnp.where(own, 1.0, 0.0), precision=EXACT, preferred_element_type=F32
            )
        window[p * WIN : (p + 1) * WIN, :] = total
        coarse[p] = total[8:56]


def prior_setup(info, own, rxa, rxb, rza, rzb, fx, fy, fz, diag, peak, w):
    first_column, first_row = info[6], info[7]
    for k in range(3):
        for j, column in enumerate(prior_columns(info, k, own, (rxa, rxb))):
            at = 2 * ZR + (k * SPAN + j) * 8
            low, high = to_sides(info, 1, rza[at : at + 8, :], rzb[at : at + 8, :])
            w[k, j, 0:8] = low
            w[k, j, 8:56] = column
            w[k, j, 56:64] = high
    row = lax.broadcasted_iota(jnp.int32, (WIN, 128), 0)
    lane = lax.broadcasted_iota(jnp.int32, (WIN, 128), 1)
    y_in = (row + first_row >= 0) & (row + first_row < 384)
    y_link = y_in & (row + first_row + 1 >= 0) & (row + first_row + 1 < 384) & (row < WIN - 1)

    def x_in(j):
        return (first_column + j >= 0) & (first_column + j < 32)

    def wx(j):
        if j < 0 or j >= SPAN:
            return jnp.zeros((WIN, 128), F32)
        return jnp.where(x_in(j) & y_in, w[0, j], 0.0)

    best = None
    for j in range(SPAN):
        inside = x_in(j) & y_in
        here = wx(j)
        x_hi = 0.5 * (here + wx(j + 1))
        x_lo = 0.5 * (here + wx(j - 1))
        v = jnp.where(inside, w[1, j], 0.0)
        y_hi = 0.5 * (v + jnp.where(row == WIN - 1, 0.0, pltpu.roll(v, WIN - 1, 0)))
        y_lo = jnp.where(row == 0, 0.5 * v, pltpu.roll(y_hi, 1, 0))
        v = jnp.where(inside, w[2, j], 0.0)
        z_hi = 0.5 * (v + jnp.where(lane == 127, 0.0, pltpu.roll(v, 127, 1)))
        z_lo = jnp.where(lane == 0, 0.5 * v, pltpu.roll(z_hi, 1, 1))
        total = ((((x_hi + x_lo) + y_hi) + y_lo) + z_hi) + z_lo
        diag[j] = SHIFT + total
        fx[j] = jnp.where(inside & x_in(j + 1), x_hi, 0.0) if j + 1 < SPAN else jnp.zeros_like(x_hi)
        fy[j] = jnp.where(x_in(j) & y_link, y_hi, 0.0)
        fz[j] = jnp.where(inside & (lane < 127), z_hi, 0.0)
        if j in (2, 3):
            bound = jnp.max((SHIFT + 2.0 * total)[8:56].reshape(6, 8, 128), axis=0)
            best = bound if best is None else jnp.maximum(best, bound)
    peak[...] = jnp.full((8, 128), jnp.max(best))


def coefficients(upper):
    top = upper[0:1, 0:1]
    centre = 0.5 * (top + SHIFT)
    half = 0.5 * (top - SHIFT)
    sigma = centre / half
    rho = 1.0 / sigma
    scales = []
    for _ in range(CHEB - 1):
        rho_new = 1.0 / (2.0 * sigma - rho)
        scales.append((rho_new * rho, 2.0 * rho_new / half))
        rho = rho_new
    return centre, scales


def cheb_column(j, scale, r, d, prior):
    fx, fy, fz, diag = prior
    v = d[j]
    y_face, z_face = fy[j], fz[j]
    pull = fx[j] * d[j + 1] + fx[j - 1] * d[j - 1]
    pull = pull + y_face * pltpu.roll(v, WIN - 1, 0) + pltpu.roll(y_face * v, 1, 0)
    pull = pull + z_face * pltpu.roll(v, 127, 1) + pltpu.roll(z_face * v, 1, 1)
    left = r[j] - (diag[j] * v - pull)
    return left, scale[0] * v + scale[1] * left


def block(ref, k):
    return ref[k * WIN : (k + 1) * WIN, :]


def cheb_send(info, d, r, sa, sb):
    for k, (low, high) in enumerate(((d[2], d[2]), (d[3], d[3]), (r[2], r[3]))):
        one, two = from_sides(info, 0, low, high)
        sa[k * WIN : (k + 1) * WIN, :] = one
        sb[k * WIN : (k + 1) * WIN, :] = two


def cheb_two(first, r, d, scales, prior):
    r, d = dict(r), dict(d)
    sums = []
    for it in range(2):
        fresh = {}
        for j in range(1 + it, SPAN - 1 - it):
            r[j], fresh[j] = cheb_column(j, scales[first + it], r, d, prior)
        d = fresh
        sums.append((d[2], d[3]))
    return r, d, sums


def cheb_one(info, upper, g, ra, rb, fx, fy, fz, diag, out, r_out, d_out, sa, sb):
    centre, scales = coefficients(upper)
    r = {2: block(g, 0), 3: block(g, 1)}
    for k in range(2):
        r[k], r[4 + k] = to_sides(info, 0, block(ra, k), block(rb, k))
    d = {j: v / centre for j, v in r.items()}
    start = (d[2], d[3])
    r, d, sums = cheb_two(0, r, d, scales, (fx, fy, fz, diag))
    for p in range(2):
        out[p] = ((start[p] + sums[0][p]) + sums[1][p])[8:56]
        r_out[p], d_out[p] = r[2 + p], d[2 + p]
    cheb_send(info, d, r, sa, sb)


def cheb_mid(info, upper, x, r_in, d_in, ra, rb, fx, fy, fz, diag, out, r_out, d_out, sa, sb):
    _, scales = coefficients(upper)
    r, d = {2: r_in[0], 3: r_in[1]}, {2: d_in[0], 3: d_in[1]}
    for k in range(2):
        d[k], d[4 + k] = to_sides(info, 0, block(ra, k), block(rb, k))
    r[1], r[4] = to_sides(info, 0, block(ra, 2), block(rb, 2))
    r, d, sums = cheb_two(2, r, d, scales, (fx, fy, fz, diag))
    for p in range(2):
        out[p] = (x[p] + sums[0][p][8:56]) + sums[1][p][8:56]
        r_out[p], d_out[p] = r[2 + p], d[2 + p]
    one, two = from_sides(info, 0, d[2], d[3])
    sa[...] = one
    sb[...] = two


def cheb_last(info, upper, x, r_in, d_in, ra, rb, fx, fy, fz, diag, out):
    _, scales = coefficients(upper)
    r, d = {2: r_in[0], 3: r_in[1]}, {2: d_in[0], 3: d_in[1]}
    d[1], d[4] = to_sides(info, 0, ra[...], rb[...])
    for p in range(2):
        _, new = cheb_column(2 + p, scales[4], r, d, (fx, fy, fz, diag))
        out[p] = x[p] + new[8:56]


def as_rows(field):
    lead = field.shape[:-2]
    return jnp.swapaxes(field.reshape(*lead, CX, TILES, 128), -3, -2).reshape(-1, 128)


def on_device(
    conductivity, forward_states, sensor_cell, sensor_window, sensor_misfit, prior_conductance
):
    z_at, x_at = lax.axis_index("depth"), lax.axis_index("strip")
    z_n, x_n = lax.axis_size("depth"), lax.axis_size("strip")
    info = jnp.stack(
        [
            x_at % 2,
            z_at % 2,
            (x_at > 0).astype(jnp.int32),
            (x_at < x_n - 1).astype(jnp.int32),
            (z_at > 0).astype(jnp.int32),
            (z_at < z_n - 1).astype(jnp.int32),
            2 * x_at - 2,
            48 * z_at - 8,
        ]
    ).astype(jnp.int32)
    fwd = as_rows(forward_states)
    prior_own = prior_conductance.reshape(PRIOR, 128)
    field, small = shape(ROWS, 128), shape(8, 128)

    xs, zs = shape(2 * XR + PRIOR, 128), shape(2 * ZR, 128)
    code = call(encode, jax.ShapeDtypeStruct((64, 128), jnp.int32), [VM, VM], limit=60)(
        sensor_cell.reshape(32, 128), sensor_window.reshape(32, 128)
    ).reshape(8192)
    sources, cond, xa, xb, za, zb = call(
        scatter,
        (shape(STEPS * ROWS, 128), field, xs, xs, zs, zs),
        [SM, SM, SM, VM, VM],
        limit=6,
        flops=4 * 10**7,
    )(info, code, sensor_misfit, as_rows(conductivity), prior_own)
    rx, rz = swap((xa, xb), "strip"), swap((za, zb), "depth")
    table = call(
        faces, (shape(ROWS + ZR, 128),) + (field,) * 4, [SM] + [VM] * 5, [EXT, SIDE]
    )(info, cond, *rx, *rz)
    prior_x = rx

    forcing = sources
    known = acc = waiting = None
    for n in reversed(range(STEPS)):
        first = n == STEPS - 1
        xs, zs = shape(2 * XR + 8, 128), shape(2 * ZR + (144 if first else 0), 128)
        v, known, xa, xb, za, zb = call(
            functools.partial(first_sweep, n),
            (field, small, xs, xs, zs, zs),
            [SM] + [VM] * 12,
            [EXT, SIDE],
        )(info, forcing, fwd, prior_own if first else known, *table, *rx, *rz)
        rx, rz = swap((xa, xb), "strip"), swap((za, zb), "depth")
        if first:
            span = shape(SPAN, WIN, 128)
            *prior, peak = call(
                prior_setup, (span, span, span, span, small), [SM] + [VM] * 5, [pltpu.VMEM((3, SPAN, WIN, 128), F32)]
            )(info, prior_own, *prior_x, *rz)
        if waiting is not None:
            acc = waiting()
        forward_x, forward_z = rx, rz
        fields = 2 if n else 1
        xs, zs = shape(fields * XR + 8, 128), shape(fields * ZR, 128)
        adjoint, after, known, xa, xb, za, zb = call(
            functools.partial(second_sweep, n),
            (field, field if n else small, small, xs, xs, zs, zs),
            [SM] + [VM] * 3 + ([] if first else [VM, ANY]) + [VM] * 9,
            [EXT, SIDE],
        )(info, v, forcing, sources, *([] if first else [known, acc]), *table, *rx, *rz)
        rx, rz = swap((xa, xb), "strip"), swap((za, zb), "depth")

        def waiting(n=n, adjoint=adjoint, acc=acc, halos=(*rx, *rz, *forward_x, *forward_z)):
            return call(
                functools.partial(gradient, n),
                field,
                [SM] + [VM] * (10 if acc is None else 11),
                [EXT, EXT, SIDE, SIDE],
            )(info, adjoint, fwd, *([] if acc is None else [acc]), *halos)

        if first:
            known = peak
        forcing = after
    acc = waiting()

    pieces, _ = call(
        coarsen,
        (shape(z_n, WIN + 8, 2 * CZ), small),
        [VM] * 5,
        [SIDE, pltpu.VMEM((2 * CZ, NY), F32), pltpu.VMEM((400, 2 * CZ), F32)],
    )(acc, cond, known, *rx)
    pieces = lax.all_to_all(pieces, "depth", 0, 0)
    window, coarse_grad, upper = call(
        assemble, (shape(2 * WIN, 128), shape(2, 48, 128), shape(8, 2 * CZ)), [VM]
    )(pieces)

    own, both = shape(2, 48, 128), shape(2, WIN, 128)
    sides = swap((window, window), "strip")
    x, r, d, sa, sb = call(
        cheb_one, (own, both, both, shape(3 * WIN, 128), shape(3 * WIN, 128)), [SM] + [VM] * 8
    )(info, upper, window, *sides, *prior)
    sides = swap((sa, sb), "strip")
    x, r, d, sa, sb = call(
        cheb_mid, (own, both, both, shape(WIN, 128), shape(WIN, 128)), [SM] + [VM] * 10
    )(info, upper, x, r, d, *sides, *prior)
    sides = swap((sa, sb), "strip")
    step = call(cheb_last, own, [SM] + [VM] * 10)(info, upper, x, r, d, *sides, *prior)
    return coarse_grad, step


def solution(mesh):
    placed = (
        P("depth", "strip", None),
        P(None, "depth", "strip", None),
        P(("depth", "strip")),
        P(("depth", "strip")),
        P(("depth", "strip")),
        P(None, "strip", "depth", None),
    )
    return jax.shard_map(
        on_device,
        mesh=mesh,
        in_specs=placed,
        out_specs=(P("strip", "depth", None), P("strip", "depth", None)),
        check_vma=False,
    )
```

```python
import functools

import jax
import jax.numpy as jnp
from jax import lax
from jax.experimental import pallas as pl
from jax.experimental.pallas import tpu as pltpu
from jax.sharding import PartitionSpec as P

F32 = jnp.float32
STEPS = 5
CHEB = 6
CZ, CX, NY = 16, 8, 1536
TILES = NY // 128
ZR = TILES * CX
XR = TILES * CZ
ROWS = CZ * ZR
OWN = 8 + ZR
WIN = 64
SPAN = 6
PRIOR = 288
SHIFT = 0.5
EXACT = lax.Precision.HIGHEST

VM = pl.BlockSpec(memory_space=pltpu.VMEM)
SM = pl.BlockSpec(memory_space=pltpu.SMEM)
ANY = pl.BlockSpec(memory_space=pl.ANY)
HBM = pl.BlockSpec(memory_space=pltpu.HBM)


def shape(*dims):
    return jax.ShapeDtypeStruct(dims, F32)


def call(body, outs, ins, scratch=(), limit=6, flops=4 * 10**6, traffic=5 * 10**6):
    return pl.pallas_call(
        body,
        out_shape=outs,
        in_specs=ins,
        out_specs=jax.tree.map(lambda _: VM, outs),
        scratch_shapes=list(scratch),
        compiler_params=pltpu.CompilerParams(vmem_limit_bytes=limit * 2**20),
        cost_estimate=pl.CostEstimate(flops=flops, bytes_accessed=traffic, transcendentals=0),
    )


def pairs_a(n):
    return [(i, i ^ 1) for i in range(n)]


def pairs_b(n):
    return [(i, (((i + 1) ^ 1) - 1) % n) for i in range(n)]


def swap(send, axis):
    n = lax.axis_size(axis)
    return lax.ppermute(send[0], axis, pairs_a(n)), lax.ppermute(send[1], axis, pairs_b(n))


def to_sides(info, k, first, second):
    odd = info[k] == 1
    below = jnp.where(info[2 + 2 * k] == 1, jnp.where(odd, first, second), 0.0)
    above = jnp.where(info[3 + 2 * k] == 1, jnp.where(odd, second, first), 0.0)
    return below, above


def from_sides(info, k, below, above):
    odd = info[k] == 1
    return jnp.where(odd, below, above), jnp.where(odd, above, below)


def put_x(info, refs, to, field, base):
    for t in range(TILES):
        low = field[pl.ds(base + t * CX, CZ, stride=ZR), :]
        high = field[pl.ds(base + t * CX + CX - 1, CZ, stride=ZR), :]
        first, second = from_sides(info, 0, low, high)
        refs[0][to + t * CZ : to + (t + 1) * CZ, :] = first
        refs[1][to + t * CZ : to + (t + 1) * CZ, :] = second


def put_z(info, refs, to, field, base):
    first, second = from_sides(info, 1, field[base : base + ZR, :], field[base + ROWS - ZR : base + ROWS, :])
    refs[0][to : to + ZR, :] = first
    refs[1][to : to + ZR, :] = second


def load_sides(info, rx, base, side):
    side[...] = jnp.zeros_like(side)
    for t in range(TILES):
        at = base + t * CZ
        low, high = to_sides(info, 0, rx[0][at : at + CZ, :], rx[1][at : at + CZ, :])
        side[pl.ds(t * CX, CZ, stride=ZR), :] = low
        side[pl.ds(t * CX + CX - 1, CZ, stride=ZR), :] = high


def load_ext(info, field, base, rz, at, ext):
    ext[OWN : OWN + ROWS, :] = field[base : base + ROWS, :]
    load_layers(info, rz, at, ext)


def load_layers(info, rz, at, ext):
    low, high = to_sides(info, 1, rz[0][at : at + ZR, :], rz[1][at : at + ZR, :])
    ext[OWN - ZR : OWN, :] = low
    ext[OWN + ROWS : OWN + ROWS + ZR, :] = high


def pass_peak(mine, rx, at, sends, to, out):
    best = jnp.zeros((8, 128), F32) if mine is None else mine[...]
    if at is not None:
        best = jnp.maximum(best, jnp.maximum(rx[0][at : at + 8, :], rx[1][at : at + 8, :]))
    out[...] = best
    if sends is not None:
        for send in sends:
            send[to : to + 8, :] = best


EXT = pltpu.VMEM((OWN + ROWS + ZR + 8, 128), F32)
SIDE = pltpu.VMEM((ROWS, 128), F32)


def iota(axis):
    return lax.broadcasted_iota(jnp.int32, (CX, 128), axis)


def lanes_up(tiles, lane):
    moved = [pltpu.roll(v, 127, 1) for v in tiles]
    return [jnp.where(lane == 127, moved[(t + 1) % TILES], moved[t]) for t in range(TILES)]


def lanes_down(tiles, lane):
    moved = [pltpu.roll(v, 1, 1) for v in tiles]
    return [jnp.where(lane == 0, moved[t - 1], moved[t]) for t in range(TILES)]


def rows_of(z, t):
    return pl.multiple_of(z * ZR + t * CX, CX)


def tile(ref, row, offset=0):
    return ref[pl.ds(row + offset, CX), :]


def each_layer(body):
    def step(z, carry):
        body(z)
        return carry

    lax.fori_loop(0, CZ, step, 0, unroll=CZ)


GROUP = 4


def encode(cell_ref, window, out):
    cell = cell_ref[...]
    line = lax.shift_right_logical(lax.shift_right_logical(cell, 9) * 171, 9)
    lateral = cell - line * NY
    layer = window[...] * CZ + lax.shift_right_logical(line, 3)
    out[0:32, :] = (layer * TILES + lax.shift_right_logical(lateral, 7)) * CX
    out[32:64, :] = (line & (CX - 1)) * 128 + (lateral & 127)


def scatter(info, code, misfit, cond, out, field, xa, xb, za, zb, sem):
    move = pltpu.make_async_copy(cond, field, sem)
    move.start()
    out[...] = jnp.zeros_like(out)
    count = misfit.shape[0]
    place = iota(0) * 128 + iota(1)

    def step(i, carry):
        spots = [i * GROUP + k for k in range(GROUP)]
        at = [pl.multiple_of(code[j], CX) for j in spots]
        adds = [jnp.where(place == code[count + j], misfit[j], 0.0) for j in spots]
        sums = [tile(out, a) for a in at]
        for k in range(GROUP):
            total = sums[k] + adds[k]
            for j in range(k):
                total = total + jnp.where(at[j] == at[k], adds[j], 0.0)
            out[pl.ds(at[k], CX), :] = total
        return carry

    lax.fori_loop(0, count // GROUP, step, 0, unroll=8)
    move.wait()
    base = (STEPS - 1) * ROWS
    put_x(info, (xa, xb), 0, out, base)
    put_x(info, (xa, xb), XR, field, 0)
    put_z(info, (za, zb), 0, out, base)
    put_z(info, (za, zb), ZR, field, 0)


def faces(info, cond, rxa, rxb, rza, rzb, fz, fy, fx, fxb, inv, ext, side):
    load_ext(info, cond, 0, (rza, rzb), ZR, ext)
    load_sides(info, (rxa, rxb), XR, side)
    sub, lane = iota(0), iota(1)

    def layer(z):
        rows = [rows_of(z, t) for t in range(TILES)]
        cs = [tile(ext, r, OWN) for r in rows]
        ups = lanes_up(cs, lane)
        ups[-1] = jnp.where(lane == 127, 0.0, ups[-1])
        y_hi = [0.5 * (c + u) for c, u in zip(cs, ups)]
        y_lo = lanes_down(y_hi, lane)
        y_lo[0] = jnp.where(lane == 0, 0.5 * cs[0], y_lo[0])
        for t, r in enumerate(rows):
            c = cs[t]
            here = pl.ds(r, CX)
            beside = tile(side, r)
            z_lo = 0.5 * (c + tile(ext, r, OWN - ZR))
            z_hi = 0.5 * (c + tile(ext, r, OWN + ZR))
            x_hi = 0.5 * (c + jnp.where(sub == CX - 1, beside, tile(ext, r, OWN + 1)))
            x_lo = 0.5 * (c + jnp.where(sub == 0, beside, tile(ext, r, OWN - 1)))
            fz[here, :] = z_lo
            fz[pl.ds(r + ZR, CX), :] = z_hi
            fy[here, :] = jnp.where(lane == 127, 0.0, y_hi[t]) if t == TILES - 1 else y_hi[t]
            fx[here, :] = jnp.where(sub == CX - 1, 0.0, x_hi)
            fxb[here, :] = jnp.where(sub == CX - 1, x_hi, jnp.where(sub == 0, x_lo, 0.0))
            inv[here, :] = 1.0 / (1.0 + (((((z_hi + z_lo) + x_hi) + x_lo) + y_hi[t]) + y_lo[t]))

    each_layer(layer)


def sweep(right, base, fz, fy, fx, fxb, inv, ext, side, lane, z):
    rows = [rows_of(z, t) for t in range(TILES)]
    vs = [tile(ext, r, OWN) for r in rows]
    ys = [tile(fy, r) for r in rows]
    ups = lanes_up(vs, lane)
    downs = lanes_down([y * v for y, v in zip(ys, vs)], lane)
    new = []
    for t, r in enumerate(rows):
        spread = tile(fz, r, ZR) * tile(ext, r, OWN + ZR) + tile(fz, r) * tile(ext, r, OWN - ZR)
        x_face = tile(fx, r)
        spread = spread + (x_face * pltpu.roll(vs[t], CX - 1, 0) + pltpu.roll(x_face * vs[t], 1, 0))
        spread = spread + tile(fxb, r) * tile(side, r)
        spread = spread + (ys[t] * ups[t] + downs[t])
        new.append((tile(right, r, base) + spread) * tile(inv, r))
    return rows, new


def prior_columns(info, k, prior, rx):
    columns = {}
    for p in range(2):
        at = (2 * k + p) * 48
        columns[2 + p] = prior[at : at + 48, :]
        at = at + 2 * XR + 8
        columns[p], columns[4 + p] = to_sides(info, 0, rx[0][at : at + 48, :], rx[1][at : at + 48, :])
    return [columns[j] for j in range(SPAN)]


def first_sweep(n, info, forcing, fwd, prior, *refs):
    first = n == STEPS - 1
    fz, fy, fx, fxb, inv, rxa, rxb, rza, rzb, out, known, xa, xb, za, zb, ext, side, states, sem = refs
    move = pltpu.make_async_copy(fwd.at[pl.ds(n * ROWS, ROWS), :], states, sem)
    move.start()
    peak = None if first else prior
    base = (STEPS - 1) * ROWS if first else 0
    pass_peak(peak, (rxa, rxb), None if first else 2 * XR, (xa, xb), 2 * XR, known)
    load_ext(info, forcing, base, (rza, rzb), 0 if first else ZR, ext)
    load_sides(info, (rxa, rxb), 0 if first else XR, side)
    lane = iota(1)

    def layer(z):
        rows, new = sweep(forcing, base, fz, fy, fx, fxb, inv, ext, side, lane, z)
        for r, v in zip(rows, new):
            out[pl.ds(r, CX), :] = v

    each_layer(layer)
    put_x(info, (xa, xb), 0, out, 0)
    put_z(info, (za, zb), 0, out, 0)
    move.wait()
    put_x(info, (xa, xb), XR, states, 0)
    put_z(info, (za, zb), ZR, states, 0)
    if first:
        xa[2 * XR + 8 :, :] = prior[...]
        xb[2 * XR + 8 :, :] = prior[...]


def second_sweep(n, info, v, forcing, source, *refs):
    first = n == STEPS - 1
    peak = None
    if first:
        prior, *refs = refs
    else:
        peak, earlier, *refs = refs
    fz, fy, fx, fxb, inv, rxa, rxb, rza, rzb, out, after, known, xa, xb, za, zb, ext, side = refs
    base = (STEPS - 1) * ROWS if n == STEPS - 1 else 0
    pass_peak(peak, (rxa, rxb), 2 * XR, (xa, xb), 2 * XR if n else XR, known)
    load_ext(info, v, 0, (rza, rzb), 0, ext)
    load_sides(info, (rxa, rxb), 0, side)
    lane = iota(1)

    def layer(z):
        rows, new = sweep(forcing, base, fz, fy, fx, fxb, inv, ext, side, lane, z)
        for r, v in zip(rows, new):
            out[pl.ds(r, CX), :] = v
            if n:
                after[pl.ds(r, CX), :] = v + tile(source, r, (n - 1) * ROWS)

    each_layer(layer)
    put_x(info, (xa, xb), 0, out, 0)
    put_z(info, (za, zb), 0, out, 0)
    if n:
        put_x(info, (xa, xb), XR, after, 0)
        put_z(info, (za, zb), ZR, after, 0)
    if first:
        for k in range(3):
            for j, column in enumerate(prior_columns(info, k, prior, (rxa, rxb))):
                at = 2 * ZR + (k * SPAN + j) * 8
                za[at : at + 8, :], zb[at : at + 8, :] = from_sides(info, 1, column[:8], column[40:])


def gradient(n, info, a_ref, f_ref, *refs):
    acc = None
    if n < STEPS - 1:
        acc, *refs = refs
    rxa, rxb, rza, rzb, fxa, fxb, fza, fzb, out, a_ext, f_ext, a_side, f_side, sem = refs
    move = pltpu.make_async_copy(f_ref.at[pl.ds(n * ROWS, ROWS), :], f_ext.at[pl.ds(OWN, ROWS), :], sem)
    move.start()
    load_ext(info, a_ref, 0, (rza, rzb), 0, a_ext)
    load_sides(info, (rxa, rxb), 0, a_side)
    load_layers(info, (fza, fzb), ZR, f_ext)
    load_sides(info, (fxa, fxb), XR, f_side)
    move.wait()
    sub, lane = iota(0), iota(1)

    def layer(z):
        rows = [rows_of(z, t) for t in range(TILES)]
        a_s = [tile(a_ext, r, OWN) for r in rows]
        f_s = [tile(f_ext, r, OWN) for r in rows]
        a_up, f_up = lanes_up(a_s, lane), lanes_up(f_s, lane)
        a_up[-1] = jnp.where(lane == 127, 0.0, a_up[-1])
        f_up[-1] = jnp.where(lane == 127, 0.0, f_up[-1])
        y_hi = [(a - au) * (f - fu) for a, au, f, fu in zip(a_s, a_up, f_s, f_up)]
        y_lo = lanes_down(y_hi, lane)
        y_lo[0] = jnp.where(lane == 0, a_s[0] * f_s[0], y_lo[0])
        for t, r in enumerate(rows):
            a, f = a_s[t], f_s[t]
            total = y_hi[t] + y_lo[t]
            for step in (ZR, -ZR):
                total = total + (a - tile(a_ext, r, OWN + step)) * (f - tile(f_ext, r, OWN + step))
            for step, edge in ((1, CX - 1), (-1, 0)):
                a_by = jnp.where(sub == edge, tile(a_side, r), tile(a_ext, r, OWN + step))
                f_by = jnp.where(sub == edge, tile(f_side, r), tile(f_ext, r, OWN + step))
                total = total + (a - a_by) * (f - f_by)
            out[pl.ds(r, CX), :] = total if acc is None else tile(acc, r) + total

    each_layer(layer)


def coarsen(acc, cond, peak, rxa, rxb, out, known, fine, rows, tall):
    pass_peak(peak, (rxa, rxb), XR, None, None, known)
    fine[...] = -0.5 * cond[...] * acc[...]
    for t in range(TILES):
        for p in range(2):
            total = None
            for x in range(4):
                part = fine[pl.ds(t * CX + 4 * p + x, CZ, stride=ZR), :]
                total = part if total is None else total + part
            rows[p * CZ : (p + 1) * CZ, t * 128 : (t + 1) * 128] = total
    group = lax.broadcasted_iota(jnp.int32, (128, 512), 1) // 4
    pick = jnp.where(group == lax.broadcasted_iota(jnp.int32, (128, 512), 0), 1.0, 0.0)
    tall[...] = jnp.zeros_like(tall)
    for k in range(3):
        tall[8 + 128 * k : 8 + 128 * (k + 1), :] = lax.dot_general(
            pick,
            rows[:, 512 * k : 512 * (k + 1)],
            (((1,), (1,)), ((), ())),
            precision=EXACT,
            preferred_element_type=F32,
        )
    for d in range(out.shape[0]):
        out[d, 0:WIN] = tall[48 * d : 48 * d + WIN, :]
        out[d, WIN : WIN + 8] = known[:, : 2 * CZ]


def assemble(pieces, window, coarse, upper):
    best = pieces[0, WIN : WIN + 8]
    for d in range(1, pieces.shape[0]):
        best = jnp.maximum(best, pieces[d, WIN : WIN + 8])
    upper[...] = best
    k = lax.broadcasted_iota(jnp.int32, (2 * CZ, 128), 0)
    z = lax.broadcasted_iota(jnp.int32, (2 * CZ, 128), 1)
    for p in range(2):
        total = jnp.zeros((WIN, 128), F32)
        for d in range(pieces.shape[0]):
            own = (z >= CZ * d) & (z < CZ * (d + 1)) & (k - CZ * p == z - CZ * d)
            total = total + jnp.dot(
                pieces[d, 0:WIN], jnp.where(own, 1.0, 0.0), precision=EXACT, preferred_element_type=F32
            )
        window[p * WIN : (p + 1) * WIN, :] = total
        coarse[p] = total[8:56]


def prior_setup(info, own, rxa, rxb, rza, rzb, fx, fy, fz, diag, peak, w):
    first_column, first_row = info[6], info[7]
    for k in range(3):
        for j, column in enumerate(prior_columns(info, k, own, (rxa, rxb))):
            at = 2 * ZR + (k * SPAN + j) * 8
            low, high = to_sides(info, 1, rza[at : at + 8, :], rzb[at : at + 8, :])
            w[k, j, 0:8] = low
            w[k, j, 8:56] = column
            w[k, j, 56:64] = high
    row = lax.broadcasted_iota(jnp.int32, (WIN, 128), 0)
    lane = lax.broadcasted_iota(jnp.int32, (WIN, 128), 1)
    y_in = (row + first_row >= 0) & (row + first_row < 384)
    y_link = y_in & (row + first_row + 1 >= 0) & (row + first_row + 1 < 384) & (row < WIN - 1)

    def x_in(j):
        return (first_column + j >= 0) & (first_column + j < 32)

    def wx(j):
        if j < 0 or j >= SPAN:
            return jnp.zeros((WIN, 128), F32)
        return jnp.where(x_in(j) & y_in, w[0, j], 0.0)

    best = None
    for j in range(SPAN):
        inside = x_in(j) & y_in
        here = wx(j)
        x_hi = 0.5 * (here + wx(j + 1))
        x_lo = 0.5 * (here + wx(j - 1))
        v = jnp.where(inside, w[1, j], 0.0)
        y_hi = 0.5 * (v + jnp.where(row == WIN - 1, 0.0, pltpu.roll(v, WIN - 1, 0)))
        y_lo = jnp.where(row == 0, 0.5 * v, pltpu.roll(y_hi, 1, 0))
        v = jnp.where(inside, w[2, j], 0.0)
        z_hi = 0.5 * (v + jnp.where(lane == 127, 0.0, pltpu.roll(v, 127, 1)))
        z_lo = jnp.where(lane == 0, 0.5 * v, pltpu.roll(z_hi, 1, 1))
        total = ((((x_hi + x_lo) + y_hi) + y_lo) + z_hi) + z_lo
        diag[j] = SHIFT + total
        fx[j] = jnp.where(inside & x_in(j + 1), x_hi, 0.0) if j + 1 < SPAN else jnp.zeros_like(x_hi)
        fy[j] = jnp.where(x_in(j) & y_link, y_hi, 0.0)
        fz[j] = jnp.where(inside & (lane < 127), z_hi, 0.0)
        if j in (2, 3):
            bound = jnp.max((SHIFT + 2.0 * total)[8:56].reshape(6, 8, 128), axis=0)
            best = bound if best is None else jnp.maximum(best, bound)
    peak[...] = jnp.full((8, 128), jnp.max(best))


def coefficients(upper):
    top = upper[0:1, 0:1]
    centre = 0.5 * (top + SHIFT)
    half = 0.5 * (top - SHIFT)
    sigma = centre / half
    rho = 1.0 / sigma
    scales = []
    for _ in range(CHEB - 1):
        rho_new = 1.0 / (2.0 * sigma - rho)
        scales.append((rho_new * rho, 2.0 * rho_new / half))
        rho = rho_new
    return centre, scales


def cheb_column(j, scale, r, d, prior):
    fx, fy, fz, diag = prior
    v = d[j]
    y_face, z_face = fy[j], fz[j]
    pull = fx[j] * d[j + 1] + fx[j - 1] * d[j - 1]
    pull = pull + y_face * pltpu.roll(v, WIN - 1, 0) + pltpu.roll(y_face * v, 1, 0)
    pull = pull + z_face * pltpu.roll(v, 127, 1) + pltpu.roll(z_face * v, 1, 1)
    left = r[j] - (diag[j] * v - pull)
    return left, scale[0] * v + scale[1] * left


def block(ref, k):
    return ref[k * WIN : (k + 1) * WIN, :]


def cheb_send(info, d, r, sa, sb):
    for k, (low, high) in enumerate(((d[2], d[2]), (d[3], d[3]), (r[2], r[3]))):
        one, two = from_sides(info, 0, low, high)
        sa[k * WIN : (k + 1) * WIN, :] = one
        sb[k * WIN : (k + 1) * WIN, :] = two


def cheb_two(first, r, d, scales, prior):
    r, d = dict(r), dict(d)
    sums = []
    for it in range(2):
        fresh = {}
        for j in range(1 + it, SPAN - 1 - it):
            r[j], fresh[j] = cheb_column(j, scales[first + it], r, d, prior)
        d = fresh
        sums.append((d[2], d[3]))
    return r, d, sums


def cheb_one(info, upper, g, ra, rb, fx, fy, fz, diag, out, r_out, d_out, sa, sb):
    centre, scales = coefficients(upper)
    r = {2: block(g, 0), 3: block(g, 1)}
    for k in range(2):
        r[k], r[4 + k] = to_sides(info, 0, block(ra, k), block(rb, k))
    d = {j: v / centre for j, v in r.items()}
    start = (d[2], d[3])
    r, d, sums = cheb_two(0, r, d, scales, (fx, fy, fz, diag))
    for p in range(2):
        out[p] = ((start[p] + sums[0][p]) + sums[1][p])[8:56]
        r_out[p], d_out[p] = r[2 + p], d[2 + p]
    cheb_send(info, d, r, sa, sb)


def cheb_mid(info, upper, x, r_in, d_in, ra, rb, fx, fy, fz, diag, out, r_out, d_out, sa, sb):
    _, scales = coefficients(upper)
    r, d = {2: r_in[0], 3: r_in[1]}, {2: d_in[0], 3: d_in[1]}
    for k in range(2):
        d[k], d[4 + k] = to_sides(info, 0, block(ra, k), block(rb, k))
    r[1], r[4] = to_sides(info, 0, block(ra, 2), block(rb, 2))
    r, d, sums = cheb_two(2, r, d, scales, (fx, fy, fz, diag))
    for p in range(2):
        out[p] = (x[p] + sums[0][p][8:56]) + sums[1][p][8:56]
        r_out[p], d_out[p] = r[2 + p], d[2 + p]
    one, two = from_sides(info, 0, d[2], d[3])
    sa[...] = one
    sb[...] = two


def cheb_last(info, upper, x, r_in, d_in, ra, rb, fx, fy, fz, diag, out):
    _, scales = coefficients(upper)
    r, d = {2: r_in[0], 3: r_in[1]}, {2: d_in[0], 3: d_in[1]}
    d[1], d[4] = to_sides(info, 0, ra[...], rb[...])
    for p in range(2):
        _, new = cheb_column(2 + p, scales[4], r, d, (fx, fy, fz, diag))
        out[p] = x[p] + new[8:56]


def as_rows(field):
    lead = field.shape[:-2]
    return jnp.swapaxes(field.reshape(*lead, CX, TILES, 128), -3, -2).reshape(-1, 128)


def on_device(
    conductivity, forward_states, sensor_cell, sensor_window, sensor_misfit, prior_conductance
):
    z_at, x_at = lax.axis_index("depth"), lax.axis_index("strip")
    z_n, x_n = lax.axis_size("depth"), lax.axis_size("strip")
    info = jnp.stack(
        [
            x_at % 2,
            z_at % 2,
            (x_at > 0).astype(jnp.int32),
            (x_at < x_n - 1).astype(jnp.int32),
            (z_at > 0).astype(jnp.int32),
            (z_at < z_n - 1).astype(jnp.int32),
            2 * x_at - 2,
            48 * z_at - 8,
        ]
    ).astype(jnp.int32)
    fwd = pltpu.with_memory_space_constraint(as_rows(forward_states), pltpu.HBM)
    rock = pltpu.with_memory_space_constraint(as_rows(conductivity), pltpu.HBM)
    prior_own = prior_conductance.reshape(PRIOR, 128)
    field, small = shape(ROWS, 128), shape(8, 128)

    xs, zs = shape(2 * XR, 128), shape(2 * ZR, 128)
    code = call(encode, jax.ShapeDtypeStruct((64, 128), jnp.int32), [VM, VM], limit=60)(
        sensor_cell.reshape(32, 128), sensor_window.reshape(32, 128)
    ).reshape(8192)
    sources, cond, xa, xb, za, zb = call(
        scatter,
        (shape(STEPS * ROWS, 128), field, xs, xs, zs, zs),
        [SM, SM, SM, HBM],
        [pltpu.SemaphoreType.DMA],
        limit=6,
        flops=4 * 10**7,
    )(info, code, sensor_misfit, rock)
    rx, rz = swap((xa, xb), "strip"), swap((za, zb), "depth")
    table = call(
        faces, (shape(ROWS + ZR, 128),) + (field,) * 4, [SM] + [VM] * 5, [EXT, SIDE]
    )(info, cond, *rx, *rz)

    forcing = sources
    known = acc = waiting = None
    for n in reversed(range(STEPS)):
        first = n == STEPS - 1
        xs, zs = shape(2 * XR + 8 + (PRIOR if first else 0), 128), shape(2 * ZR, 128)
        v, known, xa, xb, za, zb = call(
            functools.partial(first_sweep, n),
            (field, small, xs, xs, zs, zs),
            [SM, VM, HBM] + [VM] * 10,
            [EXT, SIDE, SIDE, pltpu.SemaphoreType.DMA],
        )(info, forcing, fwd, prior_own if first else known, *table, *rx, *rz)
        rx, rz = swap((xa, xb), "strip"), swap((za, zb), "depth")
        if waiting is not None:
            acc = waiting()
        forward_x, forward_z = rx, rz
        fields = 2 if n else 1
        xs, zs = shape(fields * XR + 8, 128), shape(fields * ZR + (144 if first else 0), 128)
        adjoint, after, known, xa, xb, za, zb = call(
            functools.partial(second_sweep, n),
            (field, field if n else small, small, xs, xs, zs, zs),
            [SM] + [VM] * 3 + ([VM] if first else [VM, ANY]) + [VM] * 9,
            [EXT, SIDE],
        )(info, v, forcing, sources, *([prior_own] if first else [known, acc]), *table, *rx, *rz)
        rx, rz = swap((xa, xb), "strip"), swap((za, zb), "depth")

        def waiting(n=n, adjoint=adjoint, acc=acc, halos=(*rx, *rz, *forward_x, *forward_z)):
            return call(
                functools.partial(gradient, n),
                field,
                [SM, VM, HBM] + [VM] * (8 if acc is None else 9),
                [EXT, EXT, SIDE, SIDE, pltpu.SemaphoreType.DMA],
            )(info, adjoint, fwd, *([] if acc is None else [acc]), *halos)

        if first:
            span = shape(SPAN, WIN, 128)
            *prior, peak = call(
                prior_setup, (span, span, span, span, small), [SM] + [VM] * 5, [pltpu.VMEM((3, SPAN, WIN, 128), F32)]
            )(info, prior_own, *forward_x, *rz)
            known = peak
        forcing = after
    acc = waiting()

    pieces, _ = call(
        coarsen,
        (shape(z_n, WIN + 8, 2 * CZ), small),
        [VM] * 5,
        [SIDE, pltpu.VMEM((2 * CZ, NY), F32), pltpu.VMEM((400, 2 * CZ), F32)],
    )(acc, cond, known, *rx)
    pieces = lax.all_to_all(pieces, "depth", 0, 0)
    window, coarse_grad, upper = call(
        assemble, (shape(2 * WIN, 128), shape(2, 48, 128), shape(8, 2 * CZ)), [VM]
    )(pieces)

    own, both = shape(2, 48, 128), shape(2, WIN, 128)
    sides = swap((window, window), "strip")
    x, r, d, sa, sb = call(
        cheb_one, (own, both, both, shape(3 * WIN, 128), shape(3 * WIN, 128)), [SM] + [VM] * 8
    )(info, upper, window, *sides, *prior)
    sides = swap((sa, sb), "strip")
    x, r, d, sa, sb = call(
        cheb_mid, (own, both, both, shape(WIN, 128), shape(WIN, 128)), [SM] + [VM] * 10
    )(info, upper, x, r, d, *sides, *prior)
    sides = swap((sa, sb), "strip")
    step = call(cheb_last, own, [SM] + [VM] * 10)(info, upper, x, r, d, *sides, *prior)
    return coarse_grad, step


def solution(mesh):
    placed = (
        P("depth", "strip", None),
        P(None, "depth", "strip", None),
        P(("depth", "strip")),
        P(("depth", "strip")),
        P(("depth", "strip")),
        P(None, "strip", "depth", None),
    )
    return jax.shard_map(
        on_device,
        mesh=mesh,
        in_specs=placed,
        out_specs=(P("strip", "depth", None), P("strip", "depth", None)),
        check_vma=False,
    )
```

```python
import functools

import jax
import jax.numpy as jnp
from jax import lax
from jax.experimental import pallas as pl
from jax.experimental.pallas import tpu as pltpu
from jax.sharding import PartitionSpec as P

F32 = jnp.float32
STEPS = 5
CHEB = 6
CZ, CX, NY = 16, 8, 1536
TILES = NY // 128
ZR = TILES * CX
XR = TILES * CZ
ROWS = CZ * ZR
OWN = 8 + ZR
WIN = 64
SPAN = 6
PRIOR = 288
SHIFT = 0.5
EXACT = lax.Precision.HIGHEST

VM = pl.BlockSpec(memory_space=pltpu.VMEM)
SM = pl.BlockSpec(memory_space=pltpu.SMEM)
ANY = pl.BlockSpec(memory_space=pl.ANY)
HBM = pl.BlockSpec(memory_space=pltpu.HBM)


def shape(*dims):
    return jax.ShapeDtypeStruct(dims, F32)


def call(body, outs, ins, scratch=(), limit=6, flops=4 * 10**6, traffic=5 * 10**6):
    return pl.pallas_call(
        body,
        out_shape=outs,
        in_specs=ins,
        out_specs=jax.tree.map(lambda _: VM, outs),
        scratch_shapes=list(scratch),
        compiler_params=pltpu.CompilerParams(vmem_limit_bytes=limit * 2**20),
        cost_estimate=pl.CostEstimate(flops=flops, bytes_accessed=traffic, transcendentals=0),
    )


def pairs_a(n):
    return [(i, i ^ 1) for i in range(n)]


def pairs_b(n):
    return [(i, (((i + 1) ^ 1) - 1) % n) for i in range(n)]


def swap(send, axis):
    n = lax.axis_size(axis)
    return lax.ppermute(send[0], axis, pairs_a(n)), lax.ppermute(send[1], axis, pairs_b(n))


def to_sides(info, k, first, second):
    odd = info[k] == 1
    below = jnp.where(info[2 + 2 * k] == 1, jnp.where(odd, first, second), 0.0)
    above = jnp.where(info[3 + 2 * k] == 1, jnp.where(odd, second, first), 0.0)
    return below, above


def from_sides(info, k, below, above):
    odd = info[k] == 1
    return jnp.where(odd, below, above), jnp.where(odd, above, below)


def put_x(info, refs, to, field, base):
    for t in range(TILES):
        low = field[pl.ds(base + t * CX, CZ, stride=ZR), :]
        high = field[pl.ds(base + t * CX + CX - 1, CZ, stride=ZR), :]
        first, second = from_sides(info, 0, low, high)
        refs[0][to + t * CZ : to + (t + 1) * CZ, :] = first
        refs[1][to + t * CZ : to + (t + 1) * CZ, :] = second


def put_z(info, refs, to, field, base):
    first, second = from_sides(info, 1, field[base : base + ZR, :], field[base + ROWS - ZR : base + ROWS, :])
    refs[0][to : to + ZR, :] = first
    refs[1][to : to + ZR, :] = second


def load_sides(info, rx, base, side):
    side[...] = jnp.zeros_like(side)
    for t in range(TILES):
        at = base + t * CZ
        low, high = to_sides(info, 0, rx[0][at : at + CZ, :], rx[1][at : at + CZ, :])
        side[pl.ds(t * CX, CZ, stride=ZR), :] = low
        side[pl.ds(t * CX + CX - 1, CZ, stride=ZR), :] = high


def load_ext(info, field, base, rz, at, ext):
    ext[OWN : OWN + ROWS, :] = field[base : base + ROWS, :]
    low, high = to_sides(info, 1, rz[0][at : at + ZR, :], rz[1][at : at + ZR, :])
    ext[OWN - ZR : OWN, :] = low
    ext[OWN + ROWS : OWN + ROWS + ZR, :] = high


def pass_peak(mine, rx, at, sends, to, out):
    best = jnp.zeros((8, 128), F32) if mine is None else mine[...]
    if at is not None:
        best = jnp.maximum(best, jnp.maximum(rx[0][at : at + 8, :], rx[1][at : at + 8, :]))
    out[...] = best
    if sends is not None:
        for send in sends:
            send[to : to + 8, :] = best


EXT = pltpu.VMEM((OWN + ROWS + ZR + 8, 128), F32)
SIDE = pltpu.VMEM((ROWS, 128), F32)


def iota(axis):
    return lax.broadcasted_iota(jnp.int32, (CX, 128), axis)


def lanes_up(tiles, lane):
    moved = [pltpu.roll(v, 127, 1) for v in tiles]
    return [jnp.where(lane == 127, moved[(t + 1) % TILES], moved[t]) for t in range(TILES)]


def lanes_down(tiles, lane):
    moved = [pltpu.roll(v, 1, 1) for v in tiles]
    return [jnp.where(lane == 0, moved[t - 1], moved[t]) for t in range(TILES)]


def rows_of(z, t):
    return pl.multiple_of(z * ZR + t * CX, CX)


def tile(ref, row, offset=0):
    return ref[pl.ds(row + offset, CX), :]


def each_layer(body):
    def step(z, carry):
        body(z)
        return carry

    lax.fori_loop(0, CZ, step, 0, unroll=CZ)


GROUP = 4


def encode(cell_ref, window, out):
    cell = cell_ref[...]
    line = lax.shift_right_logical(lax.shift_right_logical(cell, 9) * 171, 9)
    lateral = cell - line * NY
    layer = window[...] * CZ + lax.shift_right_logical(line, 3)
    out[0:32, :] = (layer * TILES + lax.shift_right_logical(lateral, 7)) * CX
    out[32:64, :] = (line & (CX - 1)) * 128 + (lateral & 127)


def scatter(info, code, misfit, cond, prior, out, field, xa, xb, za, zb, sems):
    moves = [
        pltpu.make_async_copy(cond, field, sems.at[0]),
        pltpu.make_async_copy(prior, xa.at[pl.ds(2 * XR, PRIOR), :], sems.at[1]),
        pltpu.make_async_copy(prior, xb.at[pl.ds(2 * XR, PRIOR), :], sems.at[2]),
    ]
    for move in moves:
        move.start()
    out[...] = jnp.zeros_like(out)
    count = misfit.shape[0]
    place = iota(0) * 128 + iota(1)

    def step(i, carry):
        spots = [i * GROUP + k for k in range(GROUP)]
        at = [pl.multiple_of(code[j], CX) for j in spots]
        adds = [jnp.where(place == code[count + j], misfit[j], 0.0) for j in spots]
        sums = [tile(out, a) for a in at]
        for k in range(GROUP):
            total = sums[k] + adds[k]
            for j in range(k):
                total = total + jnp.where(at[j] == at[k], adds[j], 0.0)
            out[pl.ds(at[k], CX), :] = total
        return carry

    lax.fori_loop(0, count // GROUP, step, 0, unroll=8)
    for move in moves:
        move.wait()
    base = (STEPS - 1) * ROWS
    put_x(info, (xa, xb), 0, out, base)
    put_x(info, (xa, xb), XR, field, 0)
    put_z(info, (za, zb), 0, out, base)
    put_z(info, (za, zb), ZR, field, 0)


def faces(info, cond, rxa, rxb, rza, rzb, fz, fy, fx, fxb, inv, ext, side):
    load_ext(info, cond, 0, (rza, rzb), ZR, ext)
    load_sides(info, (rxa, rxb), XR, side)
    sub, lane = iota(0), iota(1)

    def layer(z):
        rows = [rows_of(z, t) for t in range(TILES)]
        cs = [tile(ext, r, OWN) for r in rows]
        ups = lanes_up(cs, lane)
        ups[-1] = jnp.where(lane == 127, 0.0, ups[-1])
        y_hi = [0.5 * (c + u) for c, u in zip(cs, ups)]
        y_lo = lanes_down(y_hi, lane)
        y_lo[0] = jnp.where(lane == 0, 0.5 * cs[0], y_lo[0])
        for t, r in enumerate(rows):
            c = cs[t]
            here = pl.ds(r, CX)
            beside = tile(side, r)
            z_lo = 0.5 * (c + tile(ext, r, OWN - ZR))
            z_hi = 0.5 * (c + tile(ext, r, OWN + ZR))
            x_hi = 0.5 * (c + jnp.where(sub == CX - 1, beside, tile(ext, r, OWN + 1)))
            x_lo = 0.5 * (c + jnp.where(sub == 0, beside, tile(ext, r, OWN - 1)))
            fz[here, :] = z_lo
            fz[pl.ds(r + ZR, CX), :] = z_hi
            fy[here, :] = jnp.where(lane == 127, 0.0, y_hi[t]) if t == TILES - 1 else y_hi[t]
            fx[here, :] = jnp.where(sub == CX - 1, 0.0, x_hi)
            fxb[here, :] = jnp.where(sub == CX - 1, x_hi, jnp.where(sub == 0, x_lo, 0.0))
            inv[here, :] = 1.0 / (1.0 + (((((z_hi + z_lo) + x_hi) + x_lo) + y_hi[t]) + y_lo[t]))

    each_layer(layer)


def sweep(right, base, fz, fy, fx, fxb, inv, ext, side, lane, z):
    rows = [rows_of(z, t) for t in range(TILES)]
    vs = [tile(ext, r, OWN) for r in rows]
    ys = [tile(fy, r) for r in rows]
    ups = lanes_up(vs, lane)
    downs = lanes_down([y * v for y, v in zip(ys, vs)], lane)
    new = []
    for t, r in enumerate(rows):
        spread = tile(fz, r, ZR) * tile(ext, r, OWN + ZR) + tile(fz, r) * tile(ext, r, OWN - ZR)
        x_face = tile(fx, r)
        spread = spread + (x_face * pltpu.roll(vs[t], CX - 1, 0) + pltpu.roll(x_face * vs[t], 1, 0))
        spread = spread + tile(fxb, r) * tile(side, r)
        spread = spread + (ys[t] * ups[t] + downs[t])
        new.append((tile(right, r, base) + spread) * tile(inv, r))
    return rows, new


def prior_columns(info, k, prior, rx):
    columns = {}
    for p in range(2):
        at = (2 * k + p) * 48
        columns[2 + p] = prior[at : at + 48, :]
        at = at + 2 * XR
        columns[p], columns[4 + p] = to_sides(info, 0, rx[0][at : at + 48, :], rx[1][at : at + 48, :])
    return [columns[j] for j in range(SPAN)]


def first_sweep(n, info, forcing, fwd, prior, *refs):
    first = n == STEPS - 1
    fz, fy, fx, fxb, inv, rxa, rxb, rza, rzb, out, known, xa, xb, za, zb, ext, side = refs
    peak = None if first else prior
    base = (STEPS - 1) * ROWS if first else 0
    pass_peak(peak, (rxa, rxb), None if first else 2 * XR, (xa, xb), 2 * XR, known)
    load_ext(info, forcing, base, (rza, rzb), 0 if first else ZR, ext)
    load_sides(info, (rxa, rxb), 0 if first else XR, side)
    lane = iota(1)

    def layer(z):
        rows, new = sweep(forcing, base, fz, fy, fx, fxb, inv, ext, side, lane, z)
        for r, v in zip(rows, new):
            out[pl.ds(r, CX), :] = v

    each_layer(layer)
    put_x(info, (xa, xb), 0, out, 0)
    put_z(info, (za, zb), 0, out, 0)
    put_x(info, (xa, xb), XR, fwd, n * ROWS)
    put_z(info, (za, zb), ZR, fwd, n * ROWS)
    if first:
        for k in range(3):
            columns = prior_columns(info, k, prior, (rxa, rxb))
            for j, column in enumerate(columns):
                at = 2 * ZR + (k * SPAN + j) * 8
                za[at : at + 8, :], zb[at : at + 8, :] = from_sides(info, 1, column[:8], column[40:])


def second_sweep(n, info, v, forcing, source, *refs):
    if n == STEPS - 1:
        peak = None
    else:
        peak, earlier, *refs = refs
    fz, fy, fx, fxb, inv, rxa, rxb, rza, rzb, out, after, known, xa, xb, za, zb, ext, side = refs
    base = (STEPS - 1) * ROWS if n == STEPS - 1 else 0
    pass_peak(peak, (rxa, rxb), 2 * XR, (xa, xb), 2 * XR if n else XR, known)
    load_ext(info, v, 0, (rza, rzb), 0, ext)
    load_sides(info, (rxa, rxb), 0, side)
    lane = iota(1)

    def layer(z):
        rows, new = sweep(forcing, base, fz, fy, fx, fxb, inv, ext, side, lane, z)
        for r, v in zip(rows, new):
            out[pl.ds(r, CX), :] = v
            if n:
                after[pl.ds(r, CX), :] = v + tile(source, r, (n - 1) * ROWS)

    each_layer(layer)
    put_x(info, (xa, xb), 0, out, 0)
    put_z(info, (za, zb), 0, out, 0)
    if n:
        put_x(info, (xa, xb), XR, after, 0)
        put_z(info, (za, zb), ZR, after, 0)


def gradient(n, info, a_ref, f_ref, *refs):
    acc = None
    if n < STEPS - 1:
        acc, *refs = refs
    rxa, rxb, rza, rzb, fxa, fxb, fza, fzb, out, a_ext, f_ext, a_side, f_side = refs
    load_ext(info, a_ref, 0, (rza, rzb), 0, a_ext)
    load_sides(info, (rxa, rxb), 0, a_side)
    load_ext(info, f_ref, n * ROWS, (fza, fzb), ZR, f_ext)
    load_sides(info, (fxa, fxb), XR, f_side)
    sub, lane = iota(0), iota(1)

    def layer(z):
        rows = [rows_of(z, t) for t in range(TILES)]
        a_s = [tile(a_ext, r, OWN) for r in rows]
        f_s = [tile(f_ext, r, OWN) for r in rows]
        a_up, f_up = lanes_up(a_s, lane), lanes_up(f_s, lane)
        a_up[-1] = jnp.where(lane == 127, 0.0, a_up[-1])
        f_up[-1] = jnp.where(lane == 127, 0.0, f_up[-1])
        y_hi = [(a - au) * (f - fu) for a, au, f, fu in zip(a_s, a_up, f_s, f_up)]
        y_lo = lanes_down(y_hi, lane)
        y_lo[0] = jnp.where(lane == 0, a_s[0] * f_s[0], y_lo[0])
        for t, r in enumerate(rows):
            a, f = a_s[t], f_s[t]
            total = y_hi[t] + y_lo[t]
            for step in (ZR, -ZR):
                total = total + (a - tile(a_ext, r, OWN + step)) * (f - tile(f_ext, r, OWN + step))
            for step, edge in ((1, CX - 1), (-1, 0)):
                a_by = jnp.where(sub == edge, tile(a_side, r), tile(a_ext, r, OWN + step))
                f_by = jnp.where(sub == edge, tile(f_side, r), tile(f_ext, r, OWN + step))
                total = total + (a - a_by) * (f - f_by)
            out[pl.ds(r, CX), :] = total if acc is None else tile(acc, r) + total

    each_layer(layer)


def coarsen(acc, cond, peak, rxa, rxb, out, known, fine, rows, tall):
    pass_peak(peak, (rxa, rxb), XR, None, None, known)
    fine[...] = -0.5 * cond[...] * acc[...]
    for t in range(TILES):
        for p in range(2):
            total = None
            for x in range(4):
                part = fine[pl.ds(t * CX + 4 * p + x, CZ, stride=ZR), :]
                total = part if total is None else total + part
            rows[p * CZ : (p + 1) * CZ, t * 128 : (t + 1) * 128] = total
    group = lax.broadcasted_iota(jnp.int32, (128, 512), 1) // 4
    pick = jnp.where(group == lax.broadcasted_iota(jnp.int32, (128, 512), 0), 1.0, 0.0)
    tall[...] = jnp.zeros_like(tall)
    for k in range(3):
        tall[8 + 128 * k : 8 + 128 * (k + 1), :] = lax.dot_general(
            pick,
            rows[:, 512 * k : 512 * (k + 1)],
            (((1,), (1,)), ((), ())),
            precision=EXACT,
            preferred_element_type=F32,
        )
    for d in range(out.shape[0]):
        out[d, 0:WIN] = tall[48 * d : 48 * d + WIN, :]
        out[d, WIN : WIN + 8] = known[:, : 2 * CZ]


def assemble(pieces, window, coarse, upper):
    best = pieces[0, WIN : WIN + 8]
    for d in range(1, pieces.shape[0]):
        best = jnp.maximum(best, pieces[d, WIN : WIN + 8])
    upper[...] = best
    k = lax.broadcasted_iota(jnp.int32, (2 * CZ, 128), 0)
    z = lax.broadcasted_iota(jnp.int32, (2 * CZ, 128), 1)
    for p in range(2):
        total = jnp.zeros((WIN, 128), F32)
        for d in range(pieces.shape[0]):
            own = (z >= CZ * d) & (z < CZ * (d + 1)) & (k - CZ * p == z - CZ * d)
            total = total + jnp.dot(
                pieces[d, 0:WIN], jnp.where(own, 1.0, 0.0), precision=EXACT, preferred_element_type=F32
            )
        window[p * WIN : (p + 1) * WIN, :] = total
        coarse[p] = total[8:56]


def prior_setup(info, own, rxa, rxb, rza, rzb, fx, fy, fz, diag, peak, w):
    first_column, first_row = info[6], info[7]
    for k in range(3):
        for j, column in enumerate(prior_columns(info, k, own, (rxa, rxb))):
            at = 2 * ZR + (k * SPAN + j) * 8
            low, high = to_sides(info, 1, rza[at : at + 8, :], rzb[at : at + 8, :])
            w[k, j, 0:8] = low
            w[k, j, 8:56] = column
            w[k, j, 56:64] = high
    row = lax.broadcasted_iota(jnp.int32, (WIN, 128), 0)
    lane = lax.broadcasted_iota(jnp.int32, (WIN, 128), 1)
    y_in = (row + first_row >= 0) & (row + first_row < 384)
    y_link = y_in & (row + first_row + 1 >= 0) & (row + first_row + 1 < 384) & (row < WIN - 1)

    def x_in(j):
        return (first_column + j >= 0) & (first_column + j < 32)

    def wx(j):
        if j < 0 or j >= SPAN:
            return jnp.zeros((WIN, 128), F32)
        return jnp.where(x_in(j) & y_in, w[0, j], 0.0)

    best = None
    for j in range(SPAN):
        inside = x_in(j) & y_in
        here = wx(j)
        x_hi = 0.5 * (here + wx(j + 1))
        x_lo = 0.5 * (here + wx(j - 1))
        v = jnp.where(inside, w[1, j], 0.0)
        y_hi = 0.5 * (v + jnp.where(row == WIN - 1, 0.0, pltpu.roll(v, WIN - 1, 0)))
        y_lo = jnp.where(row == 0, 0.5 * v, pltpu.roll(y_hi, 1, 0))
        v = jnp.where(inside, w[2, j], 0.0)
        z_hi = 0.5 * (v + jnp.where(lane == 127, 0.0, pltpu.roll(v, 127, 1)))
        z_lo = jnp.where(lane == 0, 0.5 * v, pltpu.roll(z_hi, 1, 1))
        total = ((((x_hi + x_lo) + y_hi) + y_lo) + z_hi) + z_lo
        diag[j] = SHIFT + total
        fx[j] = jnp.where(inside & x_in(j + 1), x_hi, 0.0) if j + 1 < SPAN else jnp.zeros_like(x_hi)
        fy[j] = jnp.where(x_in(j) & y_link, y_hi, 0.0)
        fz[j] = jnp.where(inside & (lane < 127), z_hi, 0.0)
        if j in (2, 3):
            bound = jnp.max((SHIFT + 2.0 * total)[8:56].reshape(6, 8, 128), axis=0)
            best = bound if best is None else jnp.maximum(best, bound)
    peak[...] = jnp.full((8, 128), jnp.max(best))


def coefficients(upper):
    top = upper[0:1, 0:1]
    centre = 0.5 * (top + SHIFT)
    half = 0.5 * (top - SHIFT)
    sigma = centre / half
    rho = 1.0 / sigma
    scales = []
    for _ in range(CHEB - 1):
        rho_new = 1.0 / (2.0 * sigma - rho)
        scales.append((rho_new * rho, 2.0 * rho_new / half))
        rho = rho_new
    return centre, scales


def cheb_column(j, scale, r, d, prior):
    fx, fy, fz, diag = prior
    v = d[j]
    y_face, z_face = fy[j], fz[j]
    pull = fx[j] * d[j + 1] + fx[j - 1] * d[j - 1]
    pull = pull + y_face * pltpu.roll(v, WIN - 1, 0) + pltpu.roll(y_face * v, 1, 0)
    pull = pull + z_face * pltpu.roll(v, 127, 1) + pltpu.roll(z_face * v, 1, 1)
    left = r[j] - (diag[j] * v - pull)
    return left, scale[0] * v + scale[1] * left


def block(ref, k):
    return ref[k * WIN : (k + 1) * WIN, :]


def cheb_send(info, d, r, sa, sb):
    for k, (low, high) in enumerate(((d[2], d[2]), (d[3], d[3]), (r[2], r[3]))):
        one, two = from_sides(info, 0, low, high)
        sa[k * WIN : (k + 1) * WIN, :] = one
        sb[k * WIN : (k + 1) * WIN, :] = two


def cheb_two(first, r, d, scales, prior):
    r, d = dict(r), dict(d)
    sums = []
    for it in range(2):
        fresh = {}
        for j in range(1 + it, SPAN - 1 - it):
            r[j], fresh[j] = cheb_column(j, scales[first + it], r, d, prior)
        d = fresh
        sums.append((d[2], d[3]))
    return r, d, sums


def cheb_one(info, upper, g, ra, rb, fx, fy, fz, diag, out, r_out, d_out, sa, sb):
    centre, scales = coefficients(upper)
    r = {2: block(g, 0), 3: block(g, 1)}
    for k in range(2):
        r[k], r[4 + k] = to_sides(info, 0, block(ra, k), block(rb, k))
    d = {j: v / centre for j, v in r.items()}
    start = (d[2], d[3])
    r, d, sums = cheb_two(0, r, d, scales, (fx, fy, fz, diag))
    for p in range(2):
        out[p] = ((start[p] + sums[0][p]) + sums[1][p])[8:56]
        r_out[p], d_out[p] = r[2 + p], d[2 + p]
    cheb_send(info, d, r, sa, sb)


def cheb_mid(info, upper, x, r_in, d_in, ra, rb, fx, fy, fz, diag, out, r_out, d_out, sa, sb):
    _, scales = coefficients(upper)
    r, d = {2: r_in[0], 3: r_in[1]}, {2: d_in[0], 3: d_in[1]}
    for k in range(2):
        d[k], d[4 + k] = to_sides(info, 0, block(ra, k), block(rb, k))
    r[1], r[4] = to_sides(info, 0, block(ra, 2), block(rb, 2))
    r, d, sums = cheb_two(2, r, d, scales, (fx, fy, fz, diag))
    for p in range(2):
        out[p] = (x[p] + sums[0][p][8:56]) + sums[1][p][8:56]
        r_out[p], d_out[p] = r[2 + p], d[2 + p]
    one, two = from_sides(info, 0, d[2], d[3])
    sa[...] = one
    sb[...] = two


def cheb_last(info, upper, x, r_in, d_in, ra, rb, fx, fy, fz, diag, out):
    _, scales = coefficients(upper)
    r, d = {2: r_in[0], 3: r_in[1]}, {2: d_in[0], 3: d_in[1]}
    d[1], d[4] = to_sides(info, 0, ra[...], rb[...])
    for p in range(2):
        _, new = cheb_column(2 + p, scales[4], r, d, (fx, fy, fz, diag))
        out[p] = x[p] + new[8:56]


def as_rows(field):
    lead = field.shape[:-2]
    return jnp.swapaxes(field.reshape(*lead, CX, TILES, 128), -3, -2).reshape(-1, 128)


def on_device(
    conductivity, forward_states, sensor_cell, sensor_window, sensor_misfit, prior_conductance
):
    z_at, x_at = lax.axis_index("depth"), lax.axis_index("strip")
    z_n, x_n = lax.axis_size("depth"), lax.axis_size("strip")
    info = jnp.stack(
        [
            x_at % 2,
            z_at % 2,
            (x_at > 0).astype(jnp.int32),
            (x_at < x_n - 1).astype(jnp.int32),
            (z_at > 0).astype(jnp.int32),
            (z_at < z_n - 1).astype(jnp.int32),
            2 * x_at - 2,
            48 * z_at - 8,
        ]
    ).astype(jnp.int32)
    fwd = as_rows(forward_states)
    prior_own = prior_conductance.reshape(PRIOR, 128)
    field, small = shape(ROWS, 128), shape(8, 128)

    xs, zs = shape(2 * XR + PRIOR, 128), shape(2 * ZR, 128)
    code = call(encode, jax.ShapeDtypeStruct((64, 128), jnp.int32), [VM, VM], limit=60)(
        sensor_cell.reshape(32, 128), sensor_window.reshape(32, 128)
    ).reshape(8192)
    sources, cond, xa, xb, za, zb = call(
        scatter,
        (shape(STEPS * ROWS, 128), field, xs, xs, zs, zs),
        [SM, SM, SM, HBM, HBM],
        [pltpu.SemaphoreType.DMA((3,))],
        limit=6,
        flops=4 * 10**7,
    )(info, code, sensor_misfit, *(pltpu.with_memory_space_constraint(a, pltpu.HBM) for a in (as_rows(conductivity), prior_own)))
    rx, rz = swap((xa, xb), "strip"), swap((za, zb), "depth")
    table = call(
        faces, (shape(ROWS + ZR, 128),) + (field,) * 4, [SM] + [VM] * 5, [EXT, SIDE]
    )(info, cond, *rx, *rz)
    prior_x = rx

    forcing = sources
    known = acc = waiting = None
    for n in reversed(range(STEPS)):
        first = n == STEPS - 1
        xs, zs = shape(2 * XR + 8, 128), shape(2 * ZR + (144 if first else 0), 128)
        v, known, xa, xb, za, zb = call(
            functools.partial(first_sweep, n),
            (field, small, xs, xs, zs, zs),
            [SM] + [VM] * 12,
            [EXT, SIDE],
        )(info, forcing, fwd, prior_own if first else known, *table, *rx, *rz)
        rx, rz = swap((xa, xb), "strip"), swap((za, zb), "depth")
        if first:
            span = shape(SPAN, WIN, 128)
            *prior, peak = call(
                prior_setup, (span, span, span, span, small), [SM] + [VM] * 5, [pltpu.VMEM((3, SPAN, WIN, 128), F32)]
            )(info, prior_own, *prior_x, *rz)
        if waiting is not None:
            acc = waiting()
        forward_x, forward_z = rx, rz
        fields = 2 if n else 1
        xs, zs = shape(fields * XR + 8, 128), shape(fields * ZR, 128)
        adjoint, after, known, xa, xb, za, zb = call(
            functools.partial(second_sweep, n),
            (field, field if n else small, small, xs, xs, zs, zs),
            [SM] + [VM] * 3 + ([] if first else [VM, ANY]) + [VM] * 9,
            [EXT, SIDE],
        )(info, v, forcing, sources, *([] if first else [known, acc]), *table, *rx, *rz)
        rx, rz = swap((xa, xb), "strip"), swap((za, zb), "depth")

        def waiting(n=n, adjoint=adjoint, acc=acc, halos=(*rx, *rz, *forward_x, *forward_z)):
            return call(
                functools.partial(gradient, n),
                field,
                [SM] + [VM] * (10 if acc is None else 11),
                [EXT, EXT, SIDE, SIDE],
            )(info, adjoint, fwd, *([] if acc is None else [acc]), *halos)

        if first:
            known = peak
        forcing = after
    acc = waiting()

    pieces, _ = call(
        coarsen,
        (shape(z_n, WIN + 8, 2 * CZ), small),
        [VM] * 5,
        [SIDE, pltpu.VMEM((2 * CZ, NY), F32), pltpu.VMEM((400, 2 * CZ), F32)],
    )(acc, cond, known, *rx)
    pieces = lax.all_to_all(pieces, "depth", 0, 0)
    window, coarse_grad, upper = call(
        assemble, (shape(2 * WIN, 128), shape(2, 48, 128), shape(8, 2 * CZ)), [VM]
    )(pieces)

    own, both = shape(2, 48, 128), shape(2, WIN, 128)
    sides = swap((window, window), "strip")
    x, r, d, sa, sb = call(
        cheb_one, (own, both, both, shape(3 * WIN, 128), shape(3 * WIN, 128)), [SM] + [VM] * 8
    )(info, upper, window, *sides, *prior)
    sides = swap((sa, sb), "strip")
    x, r, d, sa, sb = call(
        cheb_mid, (own, both, both, shape(WIN, 128), shape(WIN, 128)), [SM] + [VM] * 10
    )(info, upper, x, r, d, *sides, *prior)
    sides = swap((sa, sb), "strip")
    step = call(cheb_last, own, [SM] + [VM] * 10)(info, upper, x, r, d, *sides, *prior)
    return coarse_grad, step


def solution(mesh):
    placed = (
        P("depth", "strip", None),
        P(None, "depth", "strip", None),
        P(("depth", "strip")),
        P(("depth", "strip")),
        P(("depth", "strip")),
        P(None, "strip", "depth", None),
    )
    return jax.shard_map(
        on_device,
        mesh=mesh,
        in_specs=placed,
        out_specs=(P("strip", "depth", None), P("strip", "depth", None)),
        check_vma=False,
    )
```
